128 devices in a mesh: seq: 16 (over x_hi, y, core), blk: 8 (over x_lo, z).
Axes of the slice: x: 4 (x_hi: 2, x_lo: 2; x = x_hi * 2 + x_lo), y: 4, z: 4, core: 2. Of those that a mesh axis runs over, the one named last changes fastest.
Arguments:
- tokens: bfloat16 [16384, 1536], P(('seq', 'blk')), may hold values from -6 to 6
- boundary: int32 [16384], P(('seq', 'blk')), may hold values from 0 to 1, as said below
- heads_in: bfloat16 [1536, 3, 1536], P(None, None, 'blk')
- heads_out: bfloat16 [1536, 1536], P('blk'), may hold values from -0.15625 to 0.15625
- gate_up: bfloat16 [1536, 2, 4096], P(None, None, 'blk'), may hold values from -0.15625 to 0.15625
- down_weight: bfloat16 [4096, 1536], P('blk'), may hold values from -0.09375 to 0.09375
- widen: bfloat16 [1536, 4096], P(None, 'blk'), may hold values from -0.15625 to 0.15625
- heads_in_two: bfloat16 [4096, 3, 4096], P(None, None, 'blk')
- heads_out_two: bfloat16 [4096, 4096], P('blk'), may hold values from -0.09375 to 0.09375
Outputs:
- level_one: bfloat16 [16384, 1536], P(('seq', 'blk'))
- level_two: bfloat16 [8192, 4096], P('seq', 'blk')
The draws below stay inside these ranges and needn't reach their ends.
Inputs may be any that keep to these rules, and one draw needn't show every extreme that they name: `boundary`: each aligned block of 1024 consecutive rows holds between 256 and 512 ones, and some block holds exactly 512.
All inputs are finite; a program needn't handle non-finite values.
Results may differ from the reference program's by a relative error of at most 0.04.
Values may be sent and summed in bfloat16 or wider, within the bound.
No kernel may reach another device: no remote copies, remote signals or barrier semaphores. Data moves between devices by JAX's collectives and lax.ppermute only.
A program may use at most 128 MiB of HBM per device.

```python
import jax
import jax.numpy as jnp
from jax import lax

D1 = 1536
H1 = 24
F1 = 4096
D2 = 4096
H2 = 32
WIN = 512
T1 = 128
GROUP = 1024
CAPG = 512
L1 = 16384
N_SEQ = 16
N_BLK = 8


def draw_boundary(key, part):
    key = jax.random.fold_in(key, 5)
    first, second, third, fourth = jax.random.split(key, 4)
    device_count = N_SEQ * N_BLK
    leaning = jax.random.randint(first, (device_count,), 1, 5)
    base_score = jax.random.randint(second, (N_SEQ, GROUP), 0, 256)
    score = base_score * jnp.repeat(leaning, T1).reshape(N_SEQ, GROUP)
    order = jnp.argsort(-score, axis=1, stable=True)
    ranking = jnp.argsort(order, axis=1, stable=True)
    counts = jax.random.randint(third, (N_SEQ,), CAPG // 2, CAPG + 1)
    fullest = jax.random.randint(fourth, (), 0, N_SEQ)
    counts = jnp.where(jnp.arange(N_SEQ) == fullest, CAPG, counts)
    return (ranking < counts[:, None]).astype(jnp.int32).reshape(-1)


def projection_draw(key, width, query_gain):
    first = jax.random.fold_in(key, 0)
    base = jax.random.normal(first, (width, 3, width), jnp.float32)
    scaling = jnp.array([query_gain, 1.0, 1.0], jnp.float32) * width ** (-0.5)
    result = base * scaling[None, :, None]
    return result.astype(jnp.bfloat16)


def draw_heads_in(key, part):
    key = jax.random.fold_in(key, 7)
    return projection_draw(key, D1, 2.0)


def draw_heads_in_two(key, part):
    key = jax.random.fold_in(key, 9)
    return projection_draw(key, D2, 3.0)


def steps_of(own_key, extent, cuts, low, top_value):
    loudness, own = 1.0, jax.random.fold_in(own_key, 6)
    for dim, blocks in cuts:
        draws = jnp.exp(jax.random.uniform(jax.random.fold_in(own, dim), (blocks,), jnp.float32, low / len(cuts), top_value / len(cuts)))
        loudness = loudness * jnp.repeat(draws, extent[dim] // blocks).reshape([-1 if axis == dim else 1 for axis in range(len(extent))])
    return loudness


def bell_draw(stream_key, shape, deviation, limit, pieces=(), kind=jnp.bfloat16):
    loudness = steps_of(stream_key, shape, pieces, -0.22, 0.18) if pieces else 1.0
    values = jax.random.normal(stream_key, shape, jnp.float32) * deviation * loudness
    return jnp.minimum(jnp.maximum(values, -limit), limit).astype(kind)


def setup_inputs(seed: int = 0) -> dict:
    keys = jax.random.split(jax.random.key(seed), 10)
    return {
        "tokens": bell_draw(keys[0], (L1, D1), 1.0, 6.0, ((0, 128),)),
        "boundary": draw_boundary(jax.random.fold_in(keys[9], 71), 0),
        "heads_in": draw_heads_in(jax.random.fold_in(keys[9], 71), 0),
        "heads_out": bell_draw(keys[3], (D1, D1), D1 ** -0.5, 0.15625, ((0, 8),)),
        "gate_up": bell_draw(keys[4], (D1, 2, F1), D1 ** -0.5, 0.15625, ((2, 8),)),
        "down_weight": bell_draw(keys[5], (F1, D1), F1 ** -0.5, 0.09375, ((0, 8),)),
        "widen": bell_draw(keys[6], (D1, D2), D1 ** -0.5, 0.15625, ((1, 8),)),
        "heads_in_two": draw_heads_in_two(jax.random.fold_in(keys[9], 71), 0),
        "heads_out_two": bell_draw(keys[8], (D2, D2), D2 ** -0.5, 0.09375, ((0, 8),)),
    }


def normalize(values):
    floats = values.astype(jnp.float32)
    return floats * lax.rsqrt(lax.optimization_barrier(jnp.mean(floats * floats, axis=-1, keepdims=True)) + 1e-06)

def grouped(left, right, groups):
    width = left.shape[1] // groups
    total = jnp.zeros((left.shape[0], right.shape[1]), jnp.float32)
    for number in range(groups):
        partial_value = jnp.dot(left[:, number * width:(number + 1) * width], right[number * width:(number + 1) * width], preferred_element_type=jnp.float32)
        rounded = lax.optimization_barrier(partial_value.astype(jnp.bfloat16))
        total = total + rounded.astype(jnp.float32)
    return total

def window_attend(queries, keys_all, values_all):
    length = queries.shape[0]
    block = min(512, N_BLK * T1)
    head_size = D1 // H1
    padded_keys = jnp.concatenate([jnp.zeros((WIN, D1), jnp.bfloat16), keys_all], axis=0)
    padded_values = jnp.concatenate([jnp.zeros((WIN, D1), jnp.bfloat16), values_all], axis=0)

    def one_block(block_index):
        first = (block_index * block).astype(jnp.int32)
        query_block = lax.dynamic_slice_in_dim(queries, first, block).reshape(block, H1, head_size).astype(jnp.float32)
        key_block = lax.dynamic_slice_in_dim(padded_keys, first, block + WIN).reshape(block + WIN, H1, head_size).astype(jnp.float32)
        value_block = lax.dynamic_slice_in_dim(padded_values, first, block + WIN).reshape(block + WIN, H1, head_size).astype(jnp.float32)
        scores = jnp.einsum('qhd,khd->hqk', query_block, key_block) * head_size ** (-0.5)
        query_pos = first + jnp.arange(block, dtype=jnp.int32)
        key_pos = first - WIN + jnp.arange(block + WIN, dtype=jnp.int32)
        allowed = (key_pos[None, :] <= query_pos[:, None]) & (key_pos[None, :] > query_pos[:, None] - WIN) & (key_pos[None, :] >= 0)
        scores = jnp.where(allowed[None], scores, -1e+30)
        largest = lax.optimization_barrier(jnp.max(scores, axis=-1, keepdims=True))
        weights = jnp.where(allowed[None], jnp.exp(scores - largest), 0.0)
        totals = lax.optimization_barrier(jnp.sum(weights, axis=-1))
        rounded = lax.optimization_barrier(weights.astype(jnp.bfloat16)).astype(jnp.float32)
        mixed = jnp.einsum('hqk,khd->qhd', rounded, value_block) / totals.T[:, :, None]
        return mixed.astype(jnp.bfloat16).reshape(block, D1)
    blocks = lax.map(one_block, jnp.arange(length // block, dtype=jnp.int32))
    return blocks.reshape(length, D1)

def causal_attend(queries, keys_all, values_all, validity):
    total_rows = queries.shape[0]
    head_size = D2 // H2
    query_heads = queries.reshape(total_rows, H2, head_size).transpose(1, 0, 2)
    key_heads = keys_all.reshape(total_rows, H2, head_size).transpose(1, 0, 2)
    value_heads = values_all.reshape(total_rows, H2, head_size).transpose(1, 0, 2)
    positions = jnp.arange(total_rows, dtype=jnp.int32)
    allowed = (positions[None, :] <= positions[:, None]) & (validity[None, :] > 0.5)

    def one_head(stacked):
        query_head, key_head, value_head = stacked
        scores = jnp.dot(query_head, key_head.T, preferred_element_type=jnp.float32) * head_size ** (-0.5)
        scores = jnp.where(allowed, scores, -1e+30)
        largest = lax.optimization_barrier(jnp.max(scores, axis=-1, keepdims=True))
        weights = jnp.where(allowed, jnp.exp(scores - largest), 0.0)
        totals = lax.optimization_barrier(jnp.sum(weights, axis=-1))
        mixed = jnp.dot(weights, value_head.astype(jnp.float32), precision=lax.Precision.HIGHEST, preferred_element_type=jnp.float32) / totals[:, None]
        return mixed.astype(jnp.bfloat16)
    heads = lax.map(one_head, (query_heads, key_heads, value_heads))
    return heads.transpose(1, 0, 2).reshape(total_rows, D2)

def reference(tokens, boundary, heads_in, heads_out, gate_up, down_weight, widen, heads_in_two, heads_out_two):
    group_rows = N_BLK * T1
    capacity = group_rows // 2
    total_slots = capacity * N_SEQ
    normed = normalize(tokens).astype(jnp.bfloat16)
    queries = jnp.dot(normed, heads_in[:, 0, :], preferred_element_type=jnp.float32).astype(jnp.bfloat16)
    keys_all = jnp.dot(normed, heads_in[:, 1, :], preferred_element_type=jnp.float32).astype(jnp.bfloat16)
    values_all = jnp.dot(normed, heads_in[:, 2, :], preferred_element_type=jnp.float32).astype(jnp.bfloat16)
    attended = window_attend(queries, keys_all, values_all)
    mid_stream = (tokens.astype(jnp.float32) + grouped(attended, heads_out, N_BLK)).astype(jnp.bfloat16)
    normed_mid = normalize(mid_stream).astype(jnp.bfloat16)
    gate_proj = jnp.dot(normed_mid, gate_up[:, 0, :], preferred_element_type=jnp.float32)
    up_proj = jnp.dot(normed_mid, gate_up[:, 1, :], preferred_element_type=jnp.float32)
    hidden = (jax.nn.silu(gate_proj) * up_proj).astype(jnp.bfloat16)
    level_one = (mid_stream.astype(jnp.float32) + grouped(hidden, down_weight, N_BLK)).astype(jnp.bfloat16)
    marks = boundary.reshape(N_SEQ, group_rows)
    slot_ids = (jnp.cumsum(marks, axis=1) - 1).astype(jnp.int32)
    span_count = lax.optimization_barrier(jnp.sum(marks, axis=1)).astype(jnp.int32)
    block_base = (jnp.arange(N_SEQ, dtype=jnp.int32) * capacity)[:, None]
    targets = jnp.where(marks == 1, block_base + slot_ids, total_slots).reshape(-1).astype(jnp.int32)
    pooled = jnp.zeros((total_slots, D1), jnp.bfloat16).at[targets].set(level_one, mode='drop')
    validity = (jnp.arange(capacity, dtype=jnp.int32)[None, :] < span_count[:, None]).reshape(-1).astype(jnp.float32)
    wide = jnp.dot(pooled, widen, preferred_element_type=jnp.float32).astype(jnp.bfloat16)
    normed_two = normalize(wide).astype(jnp.bfloat16)
    queries_two = jnp.dot(normed_two, heads_in_two[:, 0, :], preferred_element_type=jnp.float32).astype(jnp.bfloat16)
    keys_two = jnp.dot(normed_two, heads_in_two[:, 1, :], preferred_element_type=jnp.float32).astype(jnp.bfloat16)
    values_two = jnp.dot(normed_two, heads_in_two[:, 2, :], preferred_element_type=jnp.float32).astype(jnp.bfloat16)
    attended_two = causal_attend(queries_two, keys_two, values_two, validity)
    level_two = ((wide.astype(jnp.float32) + grouped(attended_two, heads_out_two, N_BLK)) * validity[:, None]).astype(jnp.bfloat16)
    return (level_one, level_two)
```

```python
import jax
import jax.numpy as jnp
from jax import lax
from jax.experimental import pallas as pl
from jax.experimental.pallas import tpu as pltpu
from jax.sharding import PartitionSpec as P

D1 = 1536
H1 = 24
D2 = 4096
H2 = 32
WIN = 512
EXT = 16
BF16 = jnp.bfloat16
F32 = jnp.float32
MASKED = -1e30

PLACES = ((0, 0), (1, 0), (0, 1), (0, 3), (0, 2), (1, 2), (1, 1), (1, 3))


def flip_x(value):
    return lax.ppermute(value, "blk", [(i, i ^ 4) for i in range(8)])


def turn_z(value, steps):
    return lax.ppermute(value, "blk", [(i, (i & 4) | ((i + steps) & 3)) for i in range(8)])


def gather_blk(own):
    count = own.shape[0]
    across = flip_x(own)
    behind = turn_z(own, 1)
    ahead = turn_z(own, 3)
    near = jnp.concatenate([own, across, ahead, behind], axis=0)
    opposite = turn_z(near[: 2 * count], 2)
    diagonal = flip_x(near[2 * count :])
    far = jnp.concatenate([opposite, diagonal], axis=0)
    return near, far


def reduce_blk(near, far):
    count = near.shape[0] // 4
    opposite = turn_z(far[: 2 * count], 2)
    diagonal = flip_x(far[2 * count :])

    def plus(block, other):
        return near[block * count : (block + 1) * count].astype(F32) + other.astype(F32)

    across = flip_x(plus(1, opposite[count:]).astype(BF16))
    behind = turn_z(plus(2, diagonal[:count]).astype(BF16), 1)
    ahead = turn_z(plus(3, diagonal[count:]).astype(BF16), 3)
    return (
        plus(0, opposite[:count])
        + across.astype(F32)
        + behind.astype(F32)
        + ahead.astype(F32)
    )


def normalize(values):
    floats = values.astype(F32)
    return floats * lax.rsqrt(jnp.mean(floats * floats, axis=-1, keepdims=True) + 1e-06)


def dot(left, right):
    return jnp.dot(left, right, preferred_element_type=F32)


def window_kernel(info, qkv, halo, out):
    rows, width, size, stride = 128, D1 // 8, D1 // H1, 128 + EXT
    key_count = WIN + rows
    i = lax.broadcasted_iota(jnp.int32, (rows, key_count), 0)
    j = lax.broadcasted_iota(jnp.int32, (rows, key_count), 1)
    band = (j > i) & (j <= i + WIN)
    seq_position = info[8]
    for n in range(8):
        place = info[n]
        keys, values = [], []
        for k in range(n - 4, n + 1):
            if k >= 0:
                start = pl.multiple_of(info[k] * stride, 16)
                block = qkv[pl.ds(start, rows), :]
                keys.append(block[:, width : 2 * width])
                values.append(block[:, 2 * width :])
            else:
                block = halo[(k + 4) * rows : (k + 5) * rows, :]
                keys.append(block[:, :width])
                values.append(block[:, width:])
        keys = jnp.concatenate(keys, axis=0)
        values = jnp.concatenate(values, axis=0)
        queries = qkv[pl.ds(pl.multiple_of(place * stride, 16), rows), :width]
        allowed = band
        if n < 4:
            allowed = band & (j + ((n - 4) * rows + seq_position * 1024) >= 0)
        parts = []
        for h in range(width // size):
            cut = slice(h * size, (h + 1) * size)
            scores = lax.dot_general(
                queries[:, cut], keys[:, cut], (((1,), (1,)), ((), ())),
                preferred_element_type=F32,
            ) * size ** (-0.5)
            scores = jnp.where(allowed, scores, MASKED)
            largest = jnp.max(scores, axis=-1, keepdims=True)
            weights = jnp.exp(scores - largest)
            total = jnp.sum(weights, axis=-1, keepdims=True)
            parts.append(dot(weights.astype(BF16), values[:, cut]) / total)
        out[pl.ds(pl.multiple_of(place * rows, 16), rows), :] = jnp.concatenate(
            parts, axis=1
        ).astype(BF16)


def window_attend(info, qkv, halo):
    vmem = pl.BlockSpec(memory_space=pltpu.VMEM)
    return pl.pallas_call(
        window_kernel,
        out_shape=jax.ShapeDtypeStruct((1024, D1 // 8), BF16),
        in_specs=[pl.BlockSpec(memory_space=pltpu.SMEM), vmem, vmem],
        out_specs=vmem,
        compiler_params=pltpu.CompilerParams(vmem_limit_bytes=40 * 2**20),
        cost_estimate=pl.CostEstimate(
            flops=24 * 128 * 640 * 256, bytes_accessed=2 * 2**20, transcendentals=24 * 128 * 640
        ),
        name="window_attend",
    )(info, qkv, halo)


def project_kernel(info, wide_near, wide_far, weights, out, total, scale):
    step = pl.program_id(0)

    @pl.when(step == 0)
    def _():
        squares = jnp.zeros((512, 1), F32)
        for source in (wide_near, wide_far):
            for k in range(4):
                block = source[k * 512 : (k + 1) * 512, :].astype(F32)
                squares += jnp.sum(block * block, axis=-1, keepdims=True)
        scale[...] = jnp.broadcast_to(lax.rsqrt(squares / D2 + 1e-06), scale.shape)
        total[...] = jnp.zeros_like(total)

    def absorb(source, k):
        start = pl.multiple_of(k * 512, 512)
        block = source[pl.ds(start, 512), :].astype(F32) * scale[:, :1]
        total[...] += dot(block.astype(BF16), weights[...])

    @pl.when(step < 4)
    def _():
        absorb(wide_near, step)

    @pl.when(step >= 4)
    def _():
        absorb(wide_far, step - 4)

    @pl.when(step == 7)
    def _():
        out[...] = total[...].astype(BF16)


def project_two(block_of, wide_near, wide_far, weights):
    return pl.pallas_call(
        project_kernel,
        out_shape=jax.ShapeDtypeStruct((512, 1536), BF16),
        grid_spec=pltpu.PrefetchScalarGridSpec(
            num_scalar_prefetch=1,
            grid=(8,),
            in_specs=[
                pl.BlockSpec((2048, 512), lambda s, info: (0, 0)),
                pl.BlockSpec((2048, 512), lambda s, info: (0, 0)),
                pl.BlockSpec((512, 1536), lambda s, info: (info[s], 0)),
            ],
            out_specs=pl.BlockSpec((512, 1536), lambda s, info: (0, 0)),
            scratch_shapes=[pltpu.VMEM((512, 1536), F32), pltpu.VMEM((512, 128), F32)],
        ),
        compiler_params=pltpu.CompilerParams(vmem_limit_bytes=48 * 2**20),
        cost_estimate=pl.CostEstimate(
            flops=2 * 512 * 4096 * 1536, bytes_accessed=18 * 2**20, transcendentals=512
        ),
        name="project_two",
    )(block_of, wide_near, wide_far, weights)


def causal_kernel(info, queries, kv, out):
    half, core, y = info[0], info[1], info[2]
    slot = pl.program_id(0)
    own_group = half * 8 + ((y + slot) & 3) * 2 + core
    factor = 128 ** (-0.5) * 1.4426950408889634
    parts, rows = 2, 256
    query = [queries[0, p * rows : (p + 1) * rows, :] for p in range(parts)]

    def tile(group, carry, diagonal):
        other_x = (group >> 3) ^ half
        other_core = (group & 1) ^ core
        offset = ((group >> 1) - y) & 3
        block = (other_core * 2 + other_x) * 4 + offset
        keys = kv[block, :512, :128]
        values = kv[block, :512, 128:]
        valid = kv[block, 512 : 512 + EXT, :128].astype(F32)
        bias = jnp.concatenate([(valid[p : p + 1] - 1.0) * 1e30 for p in range(4)], axis=1)
        result = []
        for p in range(parts):
            largest, total, sums = carry[p]
            scores = lax.dot_general(
                query[p], keys, (((1,), (1,)), ((), ())), preferred_element_type=F32
            ) * factor + bias
            if diagonal:
                i = lax.broadcasted_iota(jnp.int32, scores.shape, 0) + p * rows
                j = lax.broadcasted_iota(jnp.int32, scores.shape, 1)
                scores = jnp.where(j <= i, scores, MASKED)
            new_largest = jnp.maximum(largest, jnp.max(scores, axis=-1, keepdims=True))
            decay = jnp.exp2(largest - new_largest)
            weights = jnp.exp2(scores - new_largest)
            total = total * decay + jnp.sum(weights, axis=-1, keepdims=True)
            sums = sums * decay + dot(weights.astype(BF16), values)
            result.append((new_largest, total, sums))
        return tuple(result)

    first = tuple(
        (jnp.full((rows, 1), MASKED, F32), jnp.zeros((rows, 1), F32), jnp.zeros((rows, 128), F32))
        for _ in range(parts)
    )
    carry = lax.fori_loop(0, own_group, lambda g, c: tile(g, c, False), first)
    carry = tile(own_group, carry, True)
    for p in range(parts):
        _, total, sums = carry[p]
        out[0, p * rows : (p + 1) * rows, :] = (sums / total).astype(BF16)


def causal_attend(info, queries, kv):
    return pl.pallas_call(
        causal_kernel,
        out_shape=jax.ShapeDtypeStruct((4, 512, 128), BF16),
        grid_spec=pltpu.PrefetchScalarGridSpec(
            num_scalar_prefetch=1,
            grid=(4,),
            in_specs=[
                pl.BlockSpec((1, 512, 128), lambda s, info: (s, 0, 0)),
                pl.BlockSpec((16, 512 + EXT, 256), lambda s, info: (0, 0, 0)),
            ],
            out_specs=pl.BlockSpec((1, 512, 128), lambda s, info: (s, 0, 0)),
        ),
        compiler_params=pltpu.CompilerParams(vmem_limit_bytes=48 * 2**20),
        cost_estimate=pl.CostEstimate(
            flops=36 * 512 * 512 * 512, bytes_accessed=6 * 2**20, transcendentals=36 * 2**18
        ),
        name="causal_attend",
    )(info, queries, kv)


def turn_y(value, steps):
    return lax.ppermute(
        value, "seq", [(i, (i & 9) | ((i + 2 * steps) & 6)) for i in range(16)]
    )


def flip_seq(value, bit):
    return lax.ppermute(value, "seq", [(i, i ^ bit) for i in range(16)])


def per_device(
    tokens, boundary, heads_in, heads_out, gate_up, down_weight, widen, heads_in_two, heads_out_two
):
    seq_position = lax.axis_index("seq")
    me = lax.axis_index("blk")
    rows = tokens.shape[0]
    capacity = 512
    width = D1 // 8
    block_of = jnp.stack([((me ^ (4 * x)) & 4) | ((me + z) & 3) for x, z in PLACES])
    numbers = jnp.arange(8, dtype=jnp.int32)
    place_of = jnp.sum(
        jnp.where(block_of[None, :] == numbers[:, None], numbers[None, :], 0), axis=1
    )

    heads_in_flat, gate_flat, up_flat, heads_two_flat = lax.optimization_barrier(
        (
            heads_in.reshape(D1, 3 * width),
            gate_up[:, 0, :],
            gate_up[:, 1, :],
            heads_in_two.reshape(D2, 1536),
        )
    )

    normed = normalize(tokens).astype(BF16)
    marks_row = jnp.pad(boundary.astype(BF16)[None, :], ((0, EXT - 1), (0, D1 - rows)))
    near, far = gather_blk(jnp.concatenate([normed, marks_row], axis=0))
    marks = jnp.concatenate([near, far], axis=0).reshape(8, rows + EXT, D1)[:, rows, :rows]
    qkv = jnp.concatenate(
        [dot(near, heads_in_flat).astype(BF16), dot(far, heads_in_flat).astype(BF16)], axis=0
    )
    edge = jnp.concatenate(
        [
            lax.dynamic_slice(qkv, (place_of[n] * (rows + EXT), width), (rows, 2 * width))
            for n in range(4, 8)
        ],
        axis=0,
    )
    halo = lax.ppermute(edge, "seq", [(i, i + 1) for i in range(15)])
    info = jnp.concatenate([place_of, seq_position[None]]).astype(jnp.int32)
    attended = window_attend(info, qkv, halo)
    attn_near = dot(attended[: 4 * rows], heads_out).astype(BF16)
    attn_far = dot(attended[4 * rows :], heads_out).astype(BF16)
    mid_stream = (tokens.astype(F32) + reduce_blk(attn_near, attn_far)).astype(BF16)

    normed_mid = normalize(mid_stream).astype(BF16)

    def mlp(block):
        hidden = jax.nn.silu(dot(block, gate_flat)) * dot(block, up_flat)
        return dot(hidden.astype(BF16), down_weight).astype(BF16)

    near, far = gather_blk(normed_mid)
    mlp_near, mlp_far = mlp(near), mlp(far)
    level_one = (mid_stream.astype(F32) + reduce_blk(mlp_near, mlp_far)).astype(BF16)

    marks = marks.astype(F32)
    counts = jnp.sum(marks, axis=1)
    before = jnp.sum(
        jnp.where(block_of[None, :] < block_of[:, None], counts[None, :], 0.0), axis=1
    )
    steps = jnp.arange(rows)
    running = dot(marks.astype(BF16), (steps[:, None] <= steps[None, :]).astype(BF16))
    slots = jnp.where(marks > 0.5, before[:, None] + running - 1.0, -1.0).astype(jnp.int32)
    span_count = jnp.sum(counts).astype(jnp.int32)
    selector = (
        slots.reshape(1, 8 * rows) == jnp.arange(capacity, dtype=jnp.int32)[:, None]
    ).astype(BF16)
    near, far = gather_blk(level_one)
    pooled = (dot(selector[:, : 4 * rows], near) + dot(selector[:, 4 * rows :], far)).astype(BF16)
    wide_cols = dot(pooled, widen).astype(BF16)

    wide_near, wide_far = gather_blk(wide_cols)
    qkv_two = project_two(block_of.astype(jnp.int32), wide_near, wide_far, heads_two_flat)
    validity = (jnp.arange(capacity, dtype=jnp.int32) < span_count).astype(F32)
    valid_rows = jnp.pad(
        validity.reshape(4, 128).astype(BF16), ((0, EXT - 4), (0, 0))
    )
    zero_rows = jnp.zeros((EXT, 128), BF16)
    core, y, half = seq_position & 1, (seq_position >> 1) & 3, seq_position >> 3

    def chunk(offset):
        head = (y + offset) & 3
        parts = [
            lax.dynamic_slice(qkv_two, (0, (4 * i + head) * 128), (capacity, 128))
            for i in range(3)
        ]
        parts = [
            jnp.concatenate([part, extra], axis=0)
            for part, extra in zip(parts, (zero_rows, valid_rows, zero_rows), strict=True)
        ]
        return jnp.concatenate(parts, axis=1)

    from_behind = turn_y(chunk(1), 1)
    from_ahead = turn_y(chunk(3), 3)
    from_opposite = turn_y(chunk(2), 2)
    mine = jnp.stack([chunk(0), from_ahead, from_opposite, from_behind])
    own_kv = mine[:, :, 128:]
    kv_pair = jnp.stack([own_kv, flip_seq(own_kv, 8)])
    kv_all = jnp.stack([kv_pair, flip_seq(kv_pair, 1)]).reshape(16, capacity + EXT, 256)
    info_two = jnp.stack([half, core, y]).astype(jnp.int32)
    mixed = causal_attend(info_two, mine[:, :capacity, :128], kv_all)
    back = [mixed[0], turn_y(mixed[3], 3), turn_y(mixed[2], 2), turn_y(mixed[1], 1)]
    heads = jnp.concatenate([back[0], back[1], back[2], back[3]] * 2, axis=1)
    attended_two = lax.dynamic_slice(heads, (0, ((4 - y) & 3) * 128), (capacity, 512))

    def columns(place):
        part = lax.dynamic_slice(heads_out_two, (0, block_of[place] * 512), (512, 512))
        return dot(attended_two, part).astype(BF16)

    out_far = jnp.concatenate([columns(place) for place in range(4, 8)], axis=0)
    out_near = jnp.concatenate([columns(place) for place in range(4)], axis=0)
    level_two = (
        (wide_cols.astype(F32) + reduce_blk(out_near, out_far)) * validity[:, None]
    ).astype(BF16)
    return (level_one, level_two)


def solution(mesh):
    placed = (
        P(("seq", "blk"), None),
        P(("seq", "blk")),
        P(None, None, "blk"),
        P("blk", None),
        P(None, None, "blk"),
        P("blk", None),
        P(None, "blk"),
        P(None, None, "blk"),
        P("blk", None),
    )
    return jax.shard_map(
        per_device,
        mesh=mesh,
        in_specs=placed,
        out_specs=(P(("seq", "blk"), None), P("seq", "blk")),
        check_vma=False,
    )
```

```python
import jax
import jax.numpy as jnp
from jax import lax
from jax.experimental import pallas as pl
from jax.experimental.pallas import tpu as pltpu
from jax.sharding import PartitionSpec as P

D1 = 1536
H1 = 24
D2 = 4096
H2 = 32
WIN = 512
EXT = 16
BF16 = jnp.bfloat16
F32 = jnp.float32
MASKED = -1e30
SCORE_FACTOR = 128 ** (-0.5) * 1.4426950408889634

PLACES = ((0, 0), (1, 0), (0, 1), (0, 3), (0, 2), (1, 2), (1, 1), (1, 3))


def flip_x(value):
    return lax.ppermute(value, "blk", [(i, i ^ 4) for i in range(8)])


def turn_z(value, steps):
    return lax.ppermute(value, "blk", [(i, (i & 4) | ((i + steps) & 3)) for i in range(8)])


def gather_blk(own):
    across = flip_x(own)
    behind = turn_z(own, 1)
    ahead = turn_z(own, 3)
    first = jnp.concatenate([own, across], axis=0)
    second = jnp.concatenate([ahead, behind], axis=0)
    opposite = turn_z(first, 2)
    diagonal = flip_x(second)
    near = jnp.concatenate([first, second], axis=0)
    far = jnp.concatenate([opposite, diagonal], axis=0)
    return near, far


def reduce_blk(near, far):
    count = near.shape[0] // 4
    opposite = turn_z(far[: 2 * count], 2)
    diagonal = flip_x(far[2 * count :])

    def plus(block, other):
        return near[block * count : (block + 1) * count].astype(F32) + other.astype(F32)

    across = flip_x(plus(1, opposite[count:]).astype(BF16))
    behind = turn_z(plus(2, diagonal[:count]).astype(BF16), 1)
    ahead = turn_z(plus(3, diagonal[count:]).astype(BF16), 3)
    return (
        plus(0, opposite[:count])
        + across.astype(F32)
        + behind.astype(F32)
        + ahead.astype(F32)
    )


def normalize(values):
    floats = values.astype(F32)
    return floats * lax.rsqrt(jnp.mean(floats * floats, axis=-1, keepdims=True) + 1e-06)


def dot(left, right):
    return jnp.dot(left, right, preferred_element_type=F32)


def dot_t(left, right):
    return lax.dot_general(left, right, (((1,), (1,)), ((), ())), preferred_element_type=F32)


def window_kernel(info, qkv, halo, out):
    rows, width, size, stride = 128, D1 // 8, D1 // H1, 128 + EXT
    key_count = WIN + rows
    i = lax.broadcasted_iota(jnp.int32, (rows, key_count), 0)
    j = lax.broadcasted_iota(jnp.int32, (rows, key_count), 1)
    band = (j > i) & (j <= i + WIN)
    seq_position = info[8]
    for n in range(8):
        place = info[n]
        keys, values = [], []
        for k in range(n - 4, n + 1):
            if k >= 0:
                start = pl.multiple_of(info[k] * stride, 16)
                block = qkv[pl.ds(start, rows), :]
                keys.append(block[:, width : 2 * width])
                values.append(block[:, 2 * width :])
            else:
                block = halo[(k + 4) * rows : (k + 5) * rows, :]
                keys.append(block[:, :width])
                values.append(block[:, width:])
        keys = jnp.concatenate(keys, axis=0)
        values = jnp.concatenate(values, axis=0)
        queries = qkv[pl.ds(pl.multiple_of(place * stride, 16), rows), :width]
        allowed = band
        if n < 4:
            allowed = band & (j + ((n - 4) * rows + seq_position * 1024) >= 0)
        parts = []
        for h in range(width // size):
            cut = slice(h * size, (h + 1) * size)
            scores = lax.dot_general(
                queries[:, cut], keys[:, cut], (((1,), (1,)), ((), ())),
                preferred_element_type=F32,
            ) * size ** (-0.5)
            scores = jnp.where(allowed, scores, MASKED)
            largest = jnp.max(scores, axis=-1, keepdims=True)
            weights = jnp.exp(scores - largest)
            total = jnp.sum(weights, axis=-1, keepdims=True)
            parts.append(dot(weights.astype(BF16), values[:, cut]) / total)
        out[pl.ds(pl.multiple_of(place * rows, 16), rows), :] = jnp.concatenate(
            parts, axis=1
        ).astype(BF16)


def window_attend(info, qkv, halo):
    vmem = pl.BlockSpec(memory_space=pltpu.VMEM)
    return pl.pallas_call(
        window_kernel,
        out_shape=jax.ShapeDtypeStruct((1024, D1 // 8), BF16),
        in_specs=[pl.BlockSpec(memory_space=pltpu.SMEM), vmem, vmem],
        out_specs=vmem,
        compiler_params=pltpu.CompilerParams(vmem_limit_bytes=40 * 2**20),
        cost_estimate=pl.CostEstimate(
            flops=24 * 128 * 640 * 256, bytes_accessed=2 * 2**20, transcendentals=24 * 128 * 640
        ),
        name="window_attend",
    )(info, qkv, halo)


def project_kernel(info, pooled, widen, weights, valid, chunks, wide_own, total, squares):
    step = pl.program_id(0)
    me, y = info[8], info[9]

    @pl.when(step == 0)
    def _():
        total[...] = jnp.zeros_like(total)
        squares[...] = jnp.zeros_like(squares)

    wide = dot(pooled[...], widen[...]).astype(BF16)
    floats = wide.astype(F32)
    squares[...] += jnp.broadcast_to(
        jnp.sum(floats * floats, axis=-1, keepdims=True), squares.shape
    )
    for i in range(3):
        total[:, i * 512 : (i + 1) * 512] += dot(wide, weights[i])

    @pl.when(step == me)
    def _():
        for p in range(8):
            start = pl.multiple_of(info[p] * 64, 64)
            wide_own[pl.ds(start, 64), :] = wide[p * 64 : (p + 1) * 64]

    @pl.when(step == 7)
    def _():
        scale = lax.rsqrt(squares[...] / D2 + 1e-06)
        for k in range(4):
            head = (y + k) & 3
            for i in range(3):
                cut = slice(i * 128, (i + 1) * 128)
                lanes = pl.ds(pl.multiple_of(i * 512 + head * 128, 128), 128)
                part = total[:, lanes] * (scale * SCORE_FACTOR if i == 0 else scale)
                part = part.astype(BF16)
                for p in range(8):
                    start = pl.multiple_of(info[p] * 64, 64)
                    chunks[k, pl.ds(start, 64), cut] = part[p * 64 : (p + 1) * 64]
                chunks[k, 512:, cut] = valid[...]


def project_two(info, pooled, widen, weights, valid):
    return pl.pallas_call(
        project_kernel,
        out_shape=(
            jax.ShapeDtypeStruct((4, 512 + EXT, 384), BF16),
            jax.ShapeDtypeStruct((512, 512), BF16),
        ),
        grid_spec=pltpu.PrefetchScalarGridSpec(
            num_scalar_prefetch=1,
            grid=(8,),
            in_specs=[
                pl.BlockSpec((512, D1), lambda s, info: (0, 0)),
                pl.BlockSpec((D1, 512), lambda s, info: (0, s)),
                pl.BlockSpec((3, 512, 512), lambda s, info: (0, s, 0)),
                pl.BlockSpec((EXT, 128), lambda s, info: (0, 0)),
            ],
            out_specs=(
                pl.BlockSpec((4, 512 + EXT, 384), lambda s, info: (0, 0, 0)),
                pl.BlockSpec((512, 512), lambda s, info: (0, 0)),
            ),
            scratch_shapes=[pltpu.VMEM((512, 1536), F32), pltpu.VMEM((512, 128), F32)],
        ),
        compiler_params=pltpu.CompilerParams(vmem_limit_bytes=40 * 2**20),
        cost_estimate=pl.CostEstimate(
            flops=4 * 512 * 4096 * 1536, bytes_accessed=28 * 2**20, transcendentals=512
        ),
        name="project_two",
    )(info, pooled, widen, weights, valid)


def causal_kernel(own_part, info, queries, kv, start, start_stats, out, out_stats, keys, values, even, odd):
    half, core, y = info[0], info[1], info[2]
    slot = pl.program_id(0)
    own_pair = (y + slot) & 3

    @pl.when(slot == 0)
    def _():
        def prepare(block, _):
            count = jnp.sum(kv[block, 512 : 512 + EXT, :128].astype(F32))
            row = lax.broadcasted_iota(jnp.int32, (512, 128), 0).astype(F32)
            lane = lax.broadcasted_iota(jnp.int32, (512, 128), 1)
            keys[block, :, :128] = kv[block, :512, :128]
            keys[block, :, 128:] = jnp.where((lane == 0) & (row >= count), MASKED, 0.0).astype(BF16)
            values[block] = kv[block, :512, 128:].T
            return 0

        lax.fori_loop(0, 8, prepare, 0)

    lane = lax.broadcasted_iota(jnp.int32, (512, 128), 1)
    query = jnp.concatenate([queries[0], jnp.where(lane == 0, 1.0, 0.0).astype(BF16)], axis=1)

    def block_of(pair, which):
        return (which ^ core) * 4 + ((pair - y) & 3)

    def scores_of(pair, which):
        return lax.dot_general(
            keys[block_of(pair, which)], query, (((1,), (1,)), ((), ())), preferred_element_type=F32
        )

    def absorb(scores, pair, which, carry, edge):
        largest, total, sums = carry
        if edge:
            key = lax.broadcasted_iota(jnp.int32, scores.shape, 0) + which * 512
            own = lax.broadcasted_iota(jnp.int32, scores.shape, 1) + core * 512
            scores = jnp.where(key <= own, scores, MASKED)
        new_largest = jnp.maximum(largest, jnp.max(scores, axis=0, keepdims=True))
        decay = jnp.exp2(largest - new_largest)
        weights = jnp.exp2(scores - new_largest)
        total = total * decay + jnp.sum(weights, axis=0, keepdims=True)
        sums = sums * decay + dot(values[block_of(pair, which)], weights.astype(BF16))
        return new_largest, total, sums

    even[...] = scores_of(0, 0)

    def both(pair, carry, edge=False):
        odd[...] = scores_of(pair, 1)
        carry = absorb(even[...], pair, 0, carry, edge)
        if not edge:
            even[...] = scores_of((pair + 1) & 3, 0)
        return absorb(odd[...], pair, 1, carry, edge)

    if own_part:
        carry = (
            jnp.full((1, 512), MASKED, F32), jnp.zeros((1, 512), F32), jnp.zeros((128, 512), F32)
        )
        carry = lax.fori_loop(0, own_pair, both, carry)
        largest, total, sums = both(own_pair, carry, True)
        out[0] = sums
        out_stats[0] = jnp.concatenate([largest, total, jnp.zeros((6, 512), F32)], axis=0)
    else:
        carry = (start_stats[0, 0:1], start_stats[0, 1:2], start[0])
        _, total, sums = lax.fori_loop(0, half * 4, both, carry)
        out[0] = (sums / total).T.astype(BF16)


def causal_attend(own_part, info, queries, kv, start=None):
    def by_slot(*shape):
        return pl.BlockSpec((1, *shape), lambda s, info: (s, 0, 0))

    sums_shape = jax.ShapeDtypeStruct((4, 128, 512), F32)
    stats_shape = jax.ShapeDtypeStruct((4, 8, 512), F32)
    in_specs = [by_slot(512, 128), pl.BlockSpec((8, 512 + EXT, 256), lambda s, info: (0, 0, 0))]
    operands = [queries, kv]
    if own_part:
        def kernel(info, queries, kv, out, out_stats, *scratch):
            causal_kernel(True, info, queries, kv, None, None, out, out_stats, *scratch)

        out_shape = (sums_shape, stats_shape)
        out_specs = (by_slot(128, 512), by_slot(8, 512))
        tiles = 18
    else:
        def kernel(info, queries, kv, start, start_stats, out, *scratch):
            causal_kernel(False, info, queries, kv, start, start_stats, out, None, *scratch)

        out_shape = jax.ShapeDtypeStruct((4, 512, 128), BF16)
        out_specs = by_slot(512, 128)
        in_specs += [by_slot(128, 512), by_slot(8, 512)]
        operands += list(start)
        tiles = 32
    return pl.pallas_call(
        kernel,
        out_shape=out_shape,
        grid_spec=pltpu.PrefetchScalarGridSpec(
            num_scalar_prefetch=1,
            grid=(4,),
            in_specs=in_specs,
            out_specs=out_specs,
            scratch_shapes=[
                pltpu.VMEM((8, 512, 256), BF16),
                pltpu.VMEM((8, 128, 512), BF16),
                pltpu.VMEM((512, 512), F32),
                pltpu.VMEM((512, 512), F32),
            ],
        ),
        compiler_params=pltpu.CompilerParams(vmem_limit_bytes=40 * 2**20),
        cost_estimate=pl.CostEstimate(
            flops=tiles * 512 * 512 * 512, bytes_accessed=4 * 2**20, transcendentals=tiles * 2**18
        ),
        name="causal_own" if own_part else "causal_first_half",
    )(info, *operands)


def turn_y(value, steps):
    return lax.ppermute(
        value, "seq", [(i, (i & 9) | ((i + 2 * steps) & 6)) for i in range(16)]
    )


def flip_seq(value, bit):
    return lax.ppermute(value, "seq", [(i, i ^ bit) for i in range(16)])


def per_device(
    tokens, boundary, heads_in, heads_out, gate_up, down_weight, widen, heads_in_two, heads_out_two
):
    seq_position = lax.axis_index("seq")
    me = lax.axis_index("blk")
    rows = tokens.shape[0]
    capacity = 512
    width = D1 // 8
    block_of = jnp.stack([((me ^ (4 * x)) & 4) | ((me + z) & 3) for x, z in PLACES])
    numbers = jnp.arange(8, dtype=jnp.int32)
    place_of = jnp.sum(
        jnp.where(block_of[None, :] == numbers[:, None], numbers[None, :], 0), axis=1
    )

    heads_in_flat = heads_in.transpose(1, 2, 0).reshape(3 * width, D1)
    gate_flat, up_flat = lax.optimization_barrier((gate_up[:, 0, :], gate_up[:, 1, :]))
    share = D1 // 16
    widen_rows = lax.dynamic_slice(widen, (seq_position * share, 0), (share, 512))
    widen_rows = lax.all_gather(widen_rows, "blk", axis=1, tiled=True)
    widen_whole = lax.all_gather(widen_rows, "seq", axis=0, tiled=True)

    normed = normalize(tokens).astype(BF16)
    marks_row = jnp.pad(boundary.astype(BF16)[None, :], ((0, EXT - 1), (0, D1 - rows)))
    near, far = gather_blk(jnp.concatenate([normed, marks_row], axis=0))
    marks = jnp.concatenate([near, far], axis=0).reshape(8, rows + EXT, D1)[:, rows, :rows]
    qkv = jnp.concatenate(
        [dot_t(near, heads_in_flat).astype(BF16), dot_t(far, heads_in_flat).astype(BF16)], axis=0
    )
    edge = jnp.concatenate(
        [
            lax.dynamic_slice(qkv, (place_of[n] * (rows + EXT), width), (rows, 2 * width))
            for n in range(4, 8)
        ],
        axis=0,
    )
    halo = lax.ppermute(edge, "seq", [(i, i + 1) for i in range(15)])
    info = jnp.concatenate([place_of, seq_position[None]]).astype(jnp.int32)
    attended = window_attend(info, qkv, halo)
    attn_near = dot(attended[: 4 * rows], heads_out).astype(BF16)
    attn_far = dot(attended[4 * rows :], heads_out).astype(BF16)
    mid_stream = (tokens.astype(F32) + reduce_blk(attn_near, attn_far)).astype(BF16)

    normed_mid = normalize(mid_stream).astype(BF16)

    def mlp(block):
        hidden = jax.nn.silu(dot(block, gate_flat)) * dot(block, up_flat)
        return dot(hidden.astype(BF16), down_weight).astype(BF16)

    near, far = gather_blk(normed_mid)
    mlp_near, mlp_far = mlp(near), mlp(far)
    marks = marks.astype(F32)
    counts = jnp.sum(marks, axis=1)
    before = jnp.sum(
        jnp.where(block_of[None, :] < block_of[:, None], counts[None, :], 0.0), axis=1
    )
    steps = jnp.arange(rows)
    running = dot(marks.astype(BF16), (steps[:, None] <= steps[None, :]).astype(BF16))
    slots = jnp.where(marks > 0.5, before[:, None] + running - 1.0, -1.0).astype(jnp.int32)
    span_count = jnp.sum(counts).astype(jnp.int32)
    targets = (block_of[:, None] * 64 + jnp.arange(64)[None, :]).reshape(capacity, 1)
    selector = (slots.reshape(1, 8 * rows) == targets).astype(BF16)
    placed = (
        dot(selector[:, : 4 * rows], mlp_near)
        + dot(selector[:, 4 * rows :], mlp_far)
        + dot(selector[:, :rows], mid_stream)
    ).astype(BF16)
    pooled_own = reduce_blk(placed[:256], placed[256:]).astype(BF16)
    pooled = jnp.concatenate(gather_blk(pooled_own), axis=0)

    level_one = (mid_stream.astype(F32) + reduce_blk(mlp_near, mlp_far)).astype(BF16)

    validity = (jnp.arange(capacity, dtype=jnp.int32) < span_count).astype(F32)
    valid_rows = jnp.pad(
        validity.reshape(4, 128).astype(BF16), ((0, EXT - 4), (0, 0))
    )
    core, y, half = seq_position & 1, (seq_position >> 1) & 3, seq_position >> 3
    info_one = jnp.concatenate([block_of, me[None], y[None]]).astype(jnp.int32)
    chunks, wide_cols = project_two(
        info_one, pooled, widen_whole, heads_in_two.transpose(1, 0, 2), valid_rows
    )
    from_behind = turn_y(chunks[1], 1)
    from_ahead = turn_y(chunks[3], 3)
    from_opposite = turn_y(chunks[2], 2)
    mine = jnp.stack([chunks[0], from_ahead, from_opposite, from_behind])
    queries, own_kv = mine[:, :capacity, :128], mine[:, :, 128:]
    first_kv = lax.ppermute(own_kv, "seq", [(i, i + 8) for i in range(8)])
    own_pair = jnp.concatenate([own_kv, flip_seq(own_kv, 1)], axis=0)
    first_pair = jnp.concatenate([first_kv, flip_seq(first_kv, 1)], axis=0)
    info_two = jnp.stack([half, core, y]).astype(jnp.int32)
    running = causal_attend(True, info_two, queries, own_pair)
    mixed = causal_attend(False, info_two, queries, first_pair, running)
    back = [mixed[0], turn_y(mixed[3], 3), turn_y(mixed[2], 2), turn_y(mixed[1], 1)]
    heads = jnp.concatenate([back[0], back[1], back[2], back[3]] * 2, axis=1)
    attended_two = lax.dynamic_slice(heads, (0, ((4 - y) & 3) * 128), (capacity, 512))

    def columns(place):
        part = lax.dynamic_slice(heads_out_two, (0, block_of[place] * 512), (512, 512))
        return dot(attended_two, part).astype(BF16)

    out_far = jnp.concatenate([columns(place) for place in range(4, 8)], axis=0)
    out_near = jnp.concatenate([columns(place) for place in range(4)], axis=0)
    level_two = (
        (wide_cols.astype(F32) + reduce_blk(out_near, out_far)) * validity[:, None]
    ).astype(BF16)
    return (level_one, level_two)


def solution(mesh):
    placed = (
        P(("seq", "blk"), None),
        P(("seq", "blk")),
        P(None, None, "blk"),
        P("blk", None),
        P(None, None, "blk"),
        P("blk", None),
        P(None, "blk"),
        P(None, None, "blk"),
        P("blk", None),
    )
    return jax.shard_map(
        per_device,
        mesh=mesh,
        in_specs=placed,
        out_specs=(P(("seq", "blk"), None), P("seq", "blk")),
        check_vma=False,
    )
```

```python
import jax
import jax.numpy as jnp
from jax import lax
from jax.experimental import pallas as pl
from jax.experimental.pallas import tpu as pltpu
from jax.sharding import PartitionSpec as P

D1 = 1536
H1 = 24
D2 = 4096
H2 = 32
WIN = 512
EXT = 16
SENT = 128 + EXT + 32
BF16 = jnp.bfloat16
F32 = jnp.float32
MASKED = -1e30
SCORE_FACTOR = 128 ** (-0.5) * 1.4426950408889634

PLACES = ((0, 0), (1, 0), (0, 1), (0, 3), (0, 2), (1, 2), (1, 1), (1, 3))


def flip_x(value):
    return lax.ppermute(value, "blk", [(i, i ^ 4) for i in range(8)])


def turn_z(value, steps):
    return lax.ppermute(value, "blk", [(i, (i & 4) | ((i + steps) & 3)) for i in range(8)])


def gather_blk(own):
    across = flip_x(own)
    behind = turn_z(own, 1)
    ahead = turn_z(own, 3)
    first = jnp.concatenate([own, across], axis=0)
    second = jnp.concatenate([ahead, behind], axis=0)
    opposite = turn_z(first, 2)
    diagonal = flip_x(second)
    near = jnp.concatenate([first, second], axis=0)
    far = jnp.concatenate([opposite, diagonal], axis=0)
    return near, far


def reduce_blk(near, far):
    count = near.shape[0] // 4
    opposite = turn_z(far[: 2 * count], 2)
    diagonal = flip_x(far[2 * count :])

    def plus(block, other):
        return near[block * count : (block + 1) * count].astype(F32) + other.astype(F32)

    across = flip_x(plus(1, opposite[count:]).astype(BF16))
    behind = turn_z(plus(2, diagonal[:count]).astype(BF16), 1)
    ahead = turn_z(plus(3, diagonal[count:]).astype(BF16), 3)
    return (
        plus(0, opposite[:count])
        + across.astype(F32)
        + behind.astype(F32)
        + ahead.astype(F32)
    )


def normalize(values):
    floats = values.astype(F32)
    return floats * lax.rsqrt(jnp.mean(floats * floats, axis=-1, keepdims=True) + 1e-06)


def dot(left, right):
    return jnp.dot(left, right, preferred_element_type=F32)


def dot_t(left, right):
    return lax.dot_general(left, right, (((1,), (1,)), ((), ())), preferred_element_type=F32)


def window_kernel(blocks, info, qkv, halo, before, out):
    rows, width, size, stride = 128, D1 // 8, D1 // H1, SENT
    key_count = WIN + rows
    i = lax.broadcasted_iota(jnp.int32, (rows, key_count), 0)
    j = lax.broadcasted_iota(jnp.int32, (rows, key_count), 1)
    band = (j > i) & (j <= i + WIN)
    seq_position = info[8]
    if before is not None:
        out[...] = before[...]
    for n in blocks:
        place = info[n]
        keys, values = [], []
        for k in range(n - 4, n + 1):
            if k >= 0:
                start = pl.multiple_of(info[k] * stride, 16)
                block = qkv[pl.ds(start, rows), :]
                keys.append(block[:, width : 2 * width])
                values.append(block[:, 2 * width :])
            else:
                block = halo[(k + 4) * rows : (k + 5) * rows, :]
                keys.append(block[:, :width])
                values.append(block[:, width:])
        keys = jnp.concatenate(keys, axis=0)
        values = jnp.concatenate(values, axis=0)
        queries = qkv[pl.ds(pl.multiple_of(place * stride, 16), rows), :width]
        allowed = band
        if n < 4:
            allowed = band & (j + ((n - 4) * rows + seq_position * 1024) >= 0)
        parts = []
        for h in range(width // size):
            cut = slice(h * size, (h + 1) * size)
            scores = lax.dot_general(
                queries[:, cut], keys[:, cut], (((1,), (1,)), ((), ())),
                preferred_element_type=F32,
            ) * size ** (-0.5)
            scores = jnp.where(allowed, scores, MASKED)
            largest = jnp.max(scores, axis=-1, keepdims=True)
            weights = jnp.exp(scores - largest)
            total = jnp.sum(weights, axis=-1, keepdims=True)
            parts.append(dot(weights.astype(BF16), values[:, cut]) / total)
        out[pl.ds(pl.multiple_of(place * rows, 16), rows), :] = jnp.concatenate(
            parts, axis=1
        ).astype(BF16)


def window_attend(info, qkv, halo=None, before=None):
    if halo is None:
        def kernel(info, qkv, out):
            window_kernel(range(4, 8), info, qkv, None, None, out)

        operands = (info, qkv)
    else:
        def kernel(info, qkv, halo, before, out):
            window_kernel(range(4), info, qkv, halo, before, out)

        operands = (info, qkv, halo, before)
    vmem = pl.BlockSpec(memory_space=pltpu.VMEM)
    return pl.pallas_call(
        kernel,
        out_shape=jax.ShapeDtypeStruct((1024, D1 // 8), BF16),
        in_specs=[pl.BlockSpec(memory_space=pltpu.SMEM)] + [vmem] * (len(operands) - 1),
        out_specs=vmem,
        compiler_params=pltpu.CompilerParams(vmem_limit_bytes=32 * 2**20),
        cost_estimate=pl.CostEstimate(
            flops=12 * 128 * 640 * 256, bytes_accessed=2 * 2**20, transcendentals=12 * 128 * 640
        ),
        name="window_late" if halo is None else "window_early",
    )(*operands)


def prepare_kernel(tokens, marks, piece, out):
    floats = tokens[...].astype(F32)
    scale = lax.rsqrt(jnp.mean(floats * floats, axis=-1, keepdims=True) + 1e-06)
    out[:128, :] = (floats * scale).astype(BF16)
    out[128 : 128 + EXT, :] = jnp.zeros((EXT, D1), BF16)
    out[128 : 128 + EXT, :128] = jnp.broadcast_to(marks[...].astype(F32), (EXT, 128)).astype(BF16)
    for j in range(3):
        out[128 + EXT :, j * 512 : (j + 1) * 512] = piece[j * 32 : (j + 1) * 32, :]


def prepare(tokens, marks, piece):
    return pl.pallas_call(
        prepare_kernel,
        out_shape=jax.ShapeDtypeStruct((SENT, D1), BF16),
        in_specs=[pl.BlockSpec(memory_space=pltpu.VMEM)] * 3,
        out_specs=pl.BlockSpec(memory_space=pltpu.VMEM),
        name="prepare",
    )(tokens, marks, piece)


def mlp_kernel(rows, gate, up, down, out):
    def some(step, _):
        cut = pl.ds(pl.multiple_of(step * 256, 256), 256)
        block = rows[cut, :]
        gated = dot(block, gate[...])
        hidden = gated / (1.0 + jnp.exp(-gated)) * dot(block, up[...])
        out[cut, :] = dot(hidden.astype(BF16), down[...]).astype(BF16)
        return 0

    lax.fori_loop(0, rows.shape[0] // 256, some, 0)


def mlp(rows, gate, up, down):
    return pl.pallas_call(
        mlp_kernel,
        out_shape=jax.ShapeDtypeStruct(rows.shape, BF16),
        in_specs=[pl.BlockSpec(memory_space=pltpu.VMEM)] * 4,
        out_specs=pl.BlockSpec(memory_space=pltpu.VMEM),
        compiler_params=pltpu.CompilerParams(vmem_limit_bytes=32 * 2**20),
        cost_estimate=pl.CostEstimate(
            flops=2 * 512 * 1536 * 1536, bytes_accessed=8 * 2**20, transcendentals=512 * 512
        ),
        name="mlp",
    )(rows, gate, up, down)


def project_kernel(info, pooled, widen, weights, valid, chunks, wide_own, total, squares):
    step = pl.program_id(0)
    y = info[8]

    @pl.when(step == 0)
    def _():
        total[...] = jnp.zeros_like(total)
        squares[...] = jnp.zeros_like(squares)

    wide = dot(pooled[...], widen[...]).astype(BF16)
    floats = wide.astype(F32)
    squares[...] += jnp.broadcast_to(
        jnp.sum(floats * floats, axis=-1, keepdims=True), squares.shape
    )
    for i in range(3):
        total[:, i * 512 : (i + 1) * 512] += dot(wide, weights[i])

    @pl.when(step == 0)
    def _():
        for p in range(8):
            start = pl.multiple_of(info[p] * 64, 64)
            wide_own[pl.ds(start, 64), :] = wide[p * 64 : (p + 1) * 64]

    @pl.when(step == 7)
    def _():
        scale = lax.rsqrt(squares[...] / D2 + 1e-06)
        for k in range(4):
            head = (y + k) & 3
            for i in range(3):
                cut = slice(i * 128, (i + 1) * 128)
                lanes = pl.ds(pl.multiple_of(i * 512 + head * 128, 128), 128)
                part = total[:, lanes] * (scale * SCORE_FACTOR if i == 0 else scale)
                part = part.astype(BF16)
                for p in range(8):
                    start = pl.multiple_of(info[p] * 64, 64)
                    chunks[k, pl.ds(start, 64), cut] = part[p * 64 : (p + 1) * 64]
                chunks[k, 512:, cut] = valid[...]


def project_two(info, pooled, widen, weights, valid):
    return pl.pallas_call(
        project_kernel,
        out_shape=(
            jax.ShapeDtypeStruct((4, 512 + EXT, 384), BF16),
            jax.ShapeDtypeStruct((512, 512), BF16),
        ),
        grid_spec=pltpu.PrefetchScalarGridSpec(
            num_scalar_prefetch=1,
            grid=(8,),
            in_specs=[
                pl.BlockSpec((512, D1), lambda s, info: (0, 0)),
                pl.BlockSpec((D1, 512), lambda s, info: (0, s)),
                pl.BlockSpec((3, 512, 512), lambda s, info: (0, info[s], 0)),
                pl.BlockSpec((EXT, 128), lambda s, info: (0, 0)),
            ],
            out_specs=(
                pl.BlockSpec((4, 512 + EXT, 384), lambda s, info: (0, 0, 0)),
                pl.BlockSpec((512, 512), lambda s, info: (0, 0)),
            ),
            scratch_shapes=[pltpu.VMEM((512, 1536), F32), pltpu.VMEM((512, 128), F32)],
        ),
        compiler_params=pltpu.CompilerParams(vmem_limit_bytes=40 * 2**20),
        cost_estimate=pl.CostEstimate(
            flops=4 * 512 * 4096 * 1536, bytes_accessed=28 * 2**20, transcendentals=512
        ),
        name="project_two",
    )(info, pooled, widen, weights, valid)


def causal_kernel(own_part, info, queries, kv, start, start_stats, out, out_stats, keys, values, even, odd):
    half, core, y = info[0], info[1], info[2]
    slot = pl.program_id(0)
    own_pair = (y + slot) & 3

    @pl.when(slot == 0)
    def _():
        def prepare(block, _):
            count = jnp.sum(kv[block, 512 : 512 + EXT, :128].astype(F32))
            row = lax.broadcasted_iota(jnp.int32, (512, 128), 0).astype(F32)
            lane = lax.broadcasted_iota(jnp.int32, (512, 128), 1)
            keys[block, :, :128] = kv[block, :512, :128]
            keys[block, :, 128:] = jnp.where((lane == 0) & (row >= count), MASKED, 0.0).astype(BF16)
            values[block] = kv[block, :512, 128:].T
            return 0

        lax.fori_loop(0, 8, prepare, 0)

    lane = lax.broadcasted_iota(jnp.int32, (512, 128), 1)
    query = jnp.concatenate([queries[0], jnp.where(lane == 0, 1.0, 0.0).astype(BF16)], axis=1)

    def block_of(pair, which):
        return (which ^ core) * 4 + ((pair - y) & 3)

    def scores_of(pair, which):
        return lax.dot_general(
            keys[block_of(pair, which)], query, (((1,), (1,)), ((), ())), preferred_element_type=F32
        )

    def absorb(scores, pair, which, carry, edge):
        largest, total, sums = carry
        if edge:
            key = lax.broadcasted_iota(jnp.int32, scores.shape, 0) + which * 512
            own = lax.broadcasted_iota(jnp.int32, scores.shape, 1) + core * 512
            scores = jnp.where(key <= own, scores, MASKED)
        new_largest = jnp.maximum(largest, jnp.max(scores, axis=0, keepdims=True))
        decay = jnp.exp2(largest - new_largest)
        weights = jnp.exp2(scores - new_largest)
        total = total * decay + jnp.sum(weights, axis=0, keepdims=True)
        sums = sums * decay + dot(values[block_of(pair, which)], weights.astype(BF16))
        return new_largest, total, sums

    even[...] = scores_of(0, 0)

    def both(pair, carry, edge=False):
        odd[...] = scores_of(pair, 1)
        carry = absorb(even[...], pair, 0, carry, edge)
        if not edge:
            even[...] = scores_of((pair + 1) & 3, 0)
        return absorb(odd[...], pair, 1, carry, edge)

    if own_part:
        carry = (
            jnp.full((1, 512), MASKED, F32), jnp.zeros((1, 512), F32), jnp.zeros((128, 512), F32)
        )
        carry = lax.fori_loop(0, own_pair, both, carry)
        largest, total, sums = both(own_pair, carry, True)
        out[0] = sums
        out_stats[0] = jnp.concatenate([largest, total, jnp.zeros((6, 512), F32)], axis=0)
    else:
        carry = (start_stats[0, 0:1], start_stats[0, 1:2], start[0])
        _, total, sums = lax.fori_loop(0, half * 4, both, carry)
        out[0] = (sums / total).T.astype(BF16)


def causal_attend(own_part, info, queries, kv, start=None):
    def by_slot(*shape):
        return pl.BlockSpec((1, *shape), lambda s, info: (s, 0, 0))

    sums_shape = jax.ShapeDtypeStruct((4, 128, 512), F32)
    stats_shape = jax.ShapeDtypeStruct((4, 8, 512), F32)
    in_specs = [by_slot(512, 128), pl.BlockSpec((8, 512 + EXT, 256), lambda s, info: (0, 0, 0))]
    operands = [queries, kv]
    if own_part:
        def kernel(info, queries, kv, out, out_stats, *scratch):
            causal_kernel(True, info, queries, kv, None, None, out, out_stats, *scratch)

        out_shape = (sums_shape, stats_shape)
        out_specs = (by_slot(128, 512), by_slot(8, 512))
        tiles = 18
    else:
        def kernel(info, queries, kv, start, start_stats, out, *scratch):
            causal_kernel(False, info, queries, kv, start, start_stats, out, None, *scratch)

        out_shape = jax.ShapeDtypeStruct((4, 512, 128), BF16)
        out_specs = by_slot(512, 128)
        in_specs += [by_slot(128, 512), by_slot(8, 512)]
        operands += list(start)
        tiles = 32
    return pl.pallas_call(
        kernel,
        out_shape=out_shape,
        grid_spec=pltpu.PrefetchScalarGridSpec(
            num_scalar_prefetch=1,
            grid=(4,),
            in_specs=in_specs,
            out_specs=out_specs,
            scratch_shapes=[
                pltpu.VMEM((8, 512, 256), BF16),
                pltpu.VMEM((8, 128, 512), BF16),
                pltpu.VMEM((512, 512), F32),
                pltpu.VMEM((512, 512), F32),
            ],
        ),
        compiler_params=pltpu.CompilerParams(vmem_limit_bytes=40 * 2**20),
        cost_estimate=pl.CostEstimate(
            flops=tiles * 512 * 512 * 512, bytes_accessed=4 * 2**20, transcendentals=tiles * 2**18
        ),
        name="causal_own" if own_part else "causal_first_half",
    )(info, *operands)


def turn_y(value, steps):
    return lax.ppermute(
        value, "seq", [(i, (i & 9) | ((i + 2 * steps) & 6)) for i in range(16)]
    )


def flip_seq(value, bit):
    return lax.ppermute(value, "seq", [(i, i ^ bit) for i in range(16)])


def per_device(
    tokens, boundary, heads_in, heads_out, gate_up, down_weight, widen, heads_in_two, heads_out_two
):
    seq_position = lax.axis_index("seq")
    me = lax.axis_index("blk")
    rows = tokens.shape[0]
    capacity = 512
    width = D1 // 8
    block_of = jnp.stack([((me ^ (4 * x)) & 4) | ((me + z) & 3) for x, z in PLACES])
    numbers = jnp.arange(8, dtype=jnp.int32)
    place_of = jnp.sum(
        jnp.where(block_of[None, :] == numbers[:, None], numbers[None, :], 0), axis=1
    )

    def later(number, value):
        return number + (value[0, 0].astype(F32) * 0.0).astype(jnp.int32)

    heads_in_flat = heads_in.transpose(1, 2, 0).reshape(3 * width, D1)
    gate_flat, up_flat = lax.optimization_barrier((gate_up[:, 0, :], gate_up[:, 1, :]))
    core, y, half = seq_position & 1, (seq_position >> 1) & 3, seq_position >> 3
    piece = lax.dynamic_slice(widen, (y * 384 + core * 192 + half * 96, 0), (96, 512))

    near, far = gather_blk(prepare(tokens, boundary[None, :], piece))
    near_parts, far_parts = near.reshape(4, SENT, D1), far.reshape(4, SENT, D1)
    marks = jnp.concatenate([near_parts[:, rows, :rows], far_parts[:, rows, :rows]], axis=0)

    def widen_columns(parts):
        parts = parts[:, rows + EXT :].reshape(4, 32, 3, 512)
        return parts.transpose(2, 1, 0, 3).reshape(96, 2048)

    def in_order(bit, own, other):
        return jnp.concatenate(
            [jnp.where(bit == 0, own, other), jnp.where(bit == 0, other, own)], axis=0
        )

    wider = jnp.concatenate([widen_columns(near_parts), widen_columns(far_parts)], axis=1)
    wider_x = flip_seq(wider, 8)
    qkv = jnp.concatenate(
        [dot_t(near, heads_in_flat).astype(BF16), dot_t(far, heads_in_flat).astype(BF16)], axis=0
    )
    edge = jnp.concatenate(
        [
            lax.dynamic_slice(qkv, (place_of[n] * SENT, width), (rows, 2 * width))
            for n in range(4, 8)
        ],
        axis=0,
    )
    halo = lax.ppermute(edge, "seq", [(i, i + 1) for i in range(15)])
    info = later(jnp.concatenate([place_of, seq_position[None]]).astype(jnp.int32), gate_flat)
    attended = window_attend(info, qkv, halo, window_attend(info, qkv))
    attn_near = dot(attended[: 4 * rows], heads_out).astype(BF16)
    attn_far = dot(attended[4 * rows :], heads_out).astype(BF16)
    wider = in_order(later(half, attended), wider, wider_x)
    wider = in_order(later(core, attn_near), wider, flip_seq(wider, 1))
    widen_whole = lax.all_gather(
        wider, "seq", axis=0, tiled=True,
        axis_index_groups=[[h * 8 + k * 2 + c for k in range(4)] for h in range(2) for c in range(2)],
    )
    mid_stream = (tokens.astype(F32) + reduce_blk(attn_near, attn_far)).astype(BF16)

    normed_mid = normalize(mid_stream).astype(BF16)

    near, far = gather_blk(normed_mid)
    mlp_near = mlp(near, gate_flat, up_flat, down_weight)
    mlp_far = mlp(far, gate_flat, up_flat, down_weight)
    marks = marks.astype(F32)
    counts = jnp.sum(marks, axis=1)
    before = jnp.sum(
        jnp.where(block_of[None, :] < block_of[:, None], counts[None, :], 0.0), axis=1
    )
    steps = jnp.arange(rows)
    running = dot(marks.astype(BF16), (steps[:, None] <= steps[None, :]).astype(BF16))
    slots = jnp.where(marks > 0.5, before[:, None] + running - 1.0, -1.0).astype(jnp.int32)
    span_count = jnp.sum(counts).astype(jnp.int32)
    targets = (block_of[:, None] * 64 + jnp.arange(64)[None, :]).reshape(capacity, 1)
    selector = (slots.reshape(1, 8 * rows) == targets).astype(BF16)
    placed = (
        dot(selector[:, : 4 * rows], mlp_near)
        + dot(selector[:, 4 * rows :], mlp_far)
        + dot(selector[:, :rows], mid_stream)
    ).astype(BF16)
    pooled_own = reduce_blk(placed[:256], placed[256:]).astype(BF16)
    pooled = jnp.concatenate(gather_blk(pooled_own), axis=0)

    level_one = (mid_stream.astype(F32) + reduce_blk(mlp_near, mlp_far)).astype(BF16)

    validity = (jnp.arange(capacity, dtype=jnp.int32) < span_count).astype(F32)
    valid_rows = jnp.pad(
        validity.reshape(4, 128).astype(BF16), ((0, EXT - 4), (0, 0))
    )
    info_one = jnp.concatenate([block_of, y[None]]).astype(jnp.int32)
    chunks, wide_cols = project_two(
        info_one, pooled, widen_whole, heads_in_two.transpose(1, 0, 2), valid_rows
    )
    from_behind = turn_y(chunks[1], 1)
    from_ahead = turn_y(chunks[3], 3)
    from_opposite = turn_y(chunks[2], 2)
    mine = jnp.stack([chunks[0], from_ahead, from_opposite, from_behind])
    queries, own_kv = mine[:, :capacity, :128], mine[:, :, 128:]
    first_kv = lax.ppermute(own_kv, "seq", [(i, i + 8) for i in range(8)])
    own_pair = jnp.concatenate([own_kv, flip_seq(own_kv, 1)], axis=0)
    info_two = jnp.stack([half, core, y]).astype(jnp.int32)
    running = causal_attend(True, info_two, queries, own_pair)
    unread = jnp.broadcast_to(running[1][0:1, 2:3, :128], (1, EXT, 128)).astype(BF16)
    first_kv = lax.dynamic_update_slice(first_kv, unread, (0, capacity, 128))
    first_pair = jnp.concatenate([first_kv, flip_seq(first_kv, 1)], axis=0)
    mixed = causal_attend(False, info_two, queries, first_pair, running)
    back = [mixed[0], turn_y(mixed[3], 3), turn_y(mixed[2], 2), turn_y(mixed[1], 1)]
    heads = jnp.concatenate([back[0], back[1], back[2], back[3]] * 2, axis=1)
    attended_two = lax.dynamic_slice(heads, (0, ((4 - y) & 3) * 128), (capacity, 512))

    def columns(place):
        part = lax.dynamic_slice(heads_out_two, (0, block_of[place] * 512), (512, 512))
        return dot(attended_two, part).astype(BF16)

    out_far = jnp.concatenate([columns(place) for place in range(4, 8)], axis=0)
    out_near = jnp.concatenate([columns(place) for place in range(4)], axis=0)
    level_two = (
        (wide_cols.astype(F32) + reduce_blk(out_near, out_far)) * validity[:, None]
    ).astype(BF16)
    return (level_one, level_two)


def solution(mesh):
    placed = (
        P(("seq", "blk"), None),
        P(("seq", "blk")),
        P(None, None, "blk"),
        P("blk", None),
        P(None, None, "blk"),
        P("blk", None),
        P(None, "blk"),
        P(None, None, "blk"),
        P("blk", None),
    )
    return jax.shard_map(
        per_device,
        mesh=mesh,
        in_specs=placed,
        out_specs=(P(("seq", "blk"), None), P("seq", "blk")),
        check_vma=False,
    )
```

```python
import jax
import jax.numpy as jnp
from jax import lax
from jax.experimental import pallas as pl
from jax.experimental.pallas import tpu as pltpu
from jax.sharding import PartitionSpec as P

D1 = 1536
H1 = 24
D2 = 4096
H2 = 32
WIN = 512
EXT = 16
SENT = 128 + EXT
BF16 = jnp.bfloat16
F32 = jnp.float32
MASKED = -1e30
SCORE_FACTOR = 128 ** (-0.5) * 1.4426950408889634

PLACES = ((0, 0), (1, 0), (0, 1), (0, 3), (0, 2), (1, 2), (1, 1), (1, 3))


def flip_x(value):
    return lax.ppermute(value, "blk", [(i, i ^ 4) for i in range(8)])


def turn_z(value, steps):
    return lax.ppermute(value, "blk", [(i, (i & 4) | ((i + steps) & 3)) for i in range(8)])


def gather_blk(own):
    across = flip_x(own)
    behind = turn_z(own, 1)
    ahead = turn_z(own, 3)
    first = jnp.concatenate([own, across], axis=0)
    second = jnp.concatenate([ahead, behind], axis=0)
    opposite = turn_z(first, 2)
    diagonal = flip_x(second)
    near = jnp.concatenate([first, second], axis=0)
    far = jnp.concatenate([opposite, diagonal], axis=0)
    return near, far


def reduce_first(far):
    count = far.shape[0] // 4
    return turn_z(far[: 2 * count], 2), flip_x(far[2 * count :])


def reduce_second(near, opposite, diagonal):
    count = near.shape[0] // 4

    def plus(block, other):
        return near[block * count : (block + 1) * count].astype(F32) + other.astype(F32)

    across = flip_x(plus(1, opposite[count:]).astype(BF16))
    behind = turn_z(plus(2, diagonal[:count]).astype(BF16), 1)
    ahead = turn_z(plus(3, diagonal[count:]).astype(BF16), 3)
    return (
        plus(0, opposite[:count])
        + across.astype(F32)
        + behind.astype(F32)
        + ahead.astype(F32)
    )


def reduce_blk(near, far):
    return reduce_second(near, *reduce_first(far))


def normalize(values):
    floats = values.astype(F32)
    return floats * lax.rsqrt(jnp.mean(floats * floats, axis=-1, keepdims=True) + 1e-06)


def dot(left, right):
    return jnp.dot(left, right, preferred_element_type=F32)


def dot_t(left, right):
    return lax.dot_general(left, right, (((1,), (1,)), ((), ())), preferred_element_type=F32)


def window_kernel(blocks, info, qkv, halo, before, out):
    rows, width, size, stride = 128, D1 // 8, D1 // H1, SENT
    key_count = WIN + rows
    i = lax.broadcasted_iota(jnp.int32, (rows, key_count), 0)
    j = lax.broadcasted_iota(jnp.int32, (rows, key_count), 1)
    band = (j > i) & (j <= i + WIN)
    seq_position = info[8]
    if before is not None:
        out[...] = before[...]
    for n in blocks:
        place = info[n]
        keys, values = [], []
        for k in range(n - 4, n + 1):
            if k >= 0:
                start = pl.multiple_of(info[k] * stride, 16)
                block = qkv[pl.ds(start, rows), :]
                keys.append(block[:, :width])
                values.append(block[:, width : 2 * width])
            else:
                block = halo[(k + 4) * rows : (k + 5) * rows, :]
                keys.append(block[:, :width])
                values.append(block[:, width:])
        keys = jnp.concatenate(keys, axis=0)
        values = jnp.concatenate(values, axis=0)
        queries = qkv[pl.ds(pl.multiple_of(place * stride, 16), rows), 2 * width :]
        allowed = band
        if n < 4:
            allowed = band & (j + ((n - 4) * rows + seq_position * 1024) >= 0)
        parts = []
        for h in range(width // size):
            cut = slice(h * size, (h + 1) * size)
            scores = lax.dot_general(
                queries[:, cut], keys[:, cut], (((1,), (1,)), ((), ())),
                preferred_element_type=F32,
            ) * size ** (-0.5)
            scores = jnp.where(allowed, scores, MASKED)
            largest = jnp.max(scores, axis=-1, keepdims=True)
            weights = jnp.exp(scores - largest)
            total = jnp.sum(weights, axis=-1, keepdims=True)
            parts.append(dot(weights.astype(BF16), values[:, cut]) / total)
        out[pl.ds(pl.multiple_of(place * rows, 16), rows), :] = jnp.concatenate(
            parts, axis=1
        ).astype(BF16)


def window_attend(info, qkv, halo=None, before=None):
    if halo is None:
        def kernel(info, qkv, out):
            window_kernel(range(4, 8), info, qkv, None, None, out)

        operands = (info, qkv)
    else:
        def kernel(info, qkv, halo, before, out):
            window_kernel(range(4), info, qkv, halo, before, out)

        operands = (info, qkv, halo, before)
    vmem = pl.BlockSpec(memory_space=pltpu.VMEM)
    return pl.pallas_call(
        kernel,
        out_shape=jax.ShapeDtypeStruct((1024, D1 // 8), BF16),
        in_specs=[pl.BlockSpec(memory_space=pltpu.SMEM)] + [vmem] * (len(operands) - 1),
        out_specs=vmem,
        compiler_params=pltpu.CompilerParams(vmem_limit_bytes=32 * 2**20),
        cost_estimate=pl.CostEstimate(
            flops=12 * 128 * 640 * 256, bytes_accessed=2 * 2**20, transcendentals=12 * 128 * 640
        ),
        name="window_late" if halo is None else "window_early",
    )(*operands)


def prepare_kernel(tokens, marks, out):
    floats = tokens[...].astype(F32)
    scale = lax.rsqrt(jnp.mean(floats * floats, axis=-1, keepdims=True) + 1e-06)
    out[:128, :] = (floats * scale).astype(BF16)
    out[128:, :] = jnp.zeros((EXT, D1), BF16)
    out[128:, :128] = jnp.broadcast_to(marks[...].astype(F32), (EXT, 128)).astype(BF16)


def prepare(tokens, marks):
    return pl.pallas_call(
        prepare_kernel,
        out_shape=jax.ShapeDtypeStruct((SENT, D1), BF16),
        in_specs=[pl.BlockSpec(memory_space=pltpu.VMEM)] * 2,
        out_specs=pl.BlockSpec(memory_space=pltpu.VMEM),
        name="prepare",
    )(tokens, marks)


def near_kernel(rows, weights, out):
    out[:, :384] = dot_t(rows[...], weights[192:, :]).astype(BF16)
    out[:, 384:] = dot_t(rows[...], weights[:192, :]).astype(BF16)


def far_kernel(info, near, rows, weights, out, edge):
    half = 4 * SENT
    out[:half, :] = near[...]
    out[half:, :384] = dot_t(rows[...], weights[192:, :]).astype(BF16)
    for k in range(4):
        start = pl.multiple_of(info[4 + k] * SENT, 16)
        edge[k * 128 : (k + 1) * 128, :] = out[pl.ds(start, 128), :384]
    out[half:, 384:] = dot_t(rows[...], weights[:192, :]).astype(BF16)


def project_one(rows, weights, info=None, near=None):
    vmem = pl.BlockSpec(memory_space=pltpu.VMEM)
    cost = pl.CostEstimate(flops=2 * 576 * 576 * D1, bytes_accessed=5 * 2**20, transcendentals=0)
    params = pltpu.CompilerParams(vmem_limit_bytes=24 * 2**20)
    if near is None:
        return pl.pallas_call(
            near_kernel,
            out_shape=jax.ShapeDtypeStruct((4 * SENT, 576), BF16),
            in_specs=[vmem] * 2,
            out_specs=vmem,
            compiler_params=params,
            cost_estimate=cost,
            name="project_near",
        )(rows, weights)
    return pl.pallas_call(
        far_kernel,
        out_shape=(
            jax.ShapeDtypeStruct((8 * SENT, 576), BF16), jax.ShapeDtypeStruct((WIN, 384), BF16)
        ),
        in_specs=[pl.BlockSpec(memory_space=pltpu.SMEM)] + [vmem] * 3,
        out_specs=(vmem, vmem),
        compiler_params=params,
        cost_estimate=cost,
        name="project_far",
    )(info, near, rows, weights)


def mlp_kernel(rows, gate, up, down, out):
    def some(step, _):
        cut = pl.ds(pl.multiple_of(step * 256, 256), 256)
        block = rows[cut, :]
        gated = dot(block, gate[...])
        hidden = gated / (1.0 + jnp.exp(-gated)) * dot(block, up[...])
        out[cut, :] = dot(hidden.astype(BF16), down[...]).astype(BF16)
        return 0

    lax.fori_loop(0, rows.shape[0] // 256, some, 0)


def mlp(rows, gate, up, down):
    return pl.pallas_call(
        mlp_kernel,
        out_shape=jax.ShapeDtypeStruct(rows.shape, BF16),
        in_specs=[pl.BlockSpec(memory_space=pltpu.VMEM)] * 4,
        out_specs=pl.BlockSpec(memory_space=pltpu.VMEM),
        compiler_params=pltpu.CompilerParams(vmem_limit_bytes=32 * 2**20),
        cost_estimate=pl.CostEstimate(
            flops=2 * 512 * 1536 * 1536, bytes_accessed=8 * 2**20, transcendentals=512 * 512
        ),
        name="mlp",
    )(rows, gate, up, down)


def project_kernel(info, pooled, *refs):
    pieces, (weights, valid, chunks, pairs, wide_own, total, squares) = refs[:16], refs[16:]
    step = pl.program_id(0)
    y = info[8]

    @pl.when(step == 0)
    def _():
        total[...] = jnp.zeros_like(total)
        squares[...] = jnp.zeros_like(squares)

    wide = jnp.zeros((512, 512), F32)
    for k in range(4):
        rows = jnp.concatenate([piece[...] for piece in pieces[4 * k : 4 * k + 4]], axis=0)
        wide += dot(pooled[:, k * 384 : (k + 1) * 384], rows)
    wide = wide.astype(BF16)
    floats = wide.astype(F32)
    squares[...] += jnp.broadcast_to(
        jnp.sum(floats * floats, axis=-1, keepdims=True), squares.shape
    )
    for i in range(3):
        total[:, i * 512 : (i + 1) * 512] += dot(wide, weights[i])

    @pl.when(step == 0)
    def _():
        for p in range(8):
            start = pl.multiple_of(info[p] * 64, 64)
            wide_own[pl.ds(start, 64), :] = wide[p * 64 : (p + 1) * 64]

    @pl.when(step == 7)
    def _():
        scale = lax.rsqrt(squares[...] / D2 + 1e-06)
        for k in range(4):
            head = (y + k) & 3
            for i in range(3):
                cut = slice(i * 128, (i + 1) * 128)
                lanes = pl.ds(pl.multiple_of(i * 512 + head * 128, 128), 128)
                part = total[:, lanes] * (scale * SCORE_FACTOR if i == 0 else scale)
                part = part.astype(BF16)
                for p in range(8):
                    start = pl.multiple_of(info[p] * 64, 64)
                    chunks[k, pl.ds(start, 64), cut] = part[p * 64 : (p + 1) * 64]
                    if i > 0:
                        pairs[k, pl.ds(start, 64), (i - 1) * 128 : i * 128] = part[p * 64 : (p + 1) * 64]
                chunks[k, 512:, cut] = valid[...]
                if i > 0:
                    pairs[k, 512:, (i - 1) * 128 : i * 128] = valid[...]


def project_two(info, pooled, pieces, weights, valid):
    return pl.pallas_call(
        project_kernel,
        out_shape=(
            jax.ShapeDtypeStruct((4, 512 + EXT, 384), BF16),
            jax.ShapeDtypeStruct((4, 512 + EXT, 256), BF16),
            jax.ShapeDtypeStruct((512, 512), BF16),
        ),
        grid_spec=pltpu.PrefetchScalarGridSpec(
            num_scalar_prefetch=1,
            grid=(8,),
            in_specs=[
                pl.BlockSpec((512, D1), lambda s, info: (0, 0)),
                *[pl.BlockSpec((96, 512), lambda s, info, h=h: (8 * h + s, 0)) for _ in range(8) for h in range(2)],
                pl.BlockSpec((3, 512, 512), lambda s, info: (0, info[s], 0)),
                pl.BlockSpec((EXT, 128), lambda s, info: (0, 0)),
            ],
            out_specs=(
                pl.BlockSpec((4, 512 + EXT, 384), lambda s, info: (0, 0, 0)),
                pl.BlockSpec((4, 512 + EXT, 256), lambda s, info: (0, 0, 0)),
                pl.BlockSpec((512, 512), lambda s, info: (0, 0)),
            ),
            scratch_shapes=[pltpu.VMEM((512, 1536), F32), pltpu.VMEM((512, 128), F32)],
        ),
        compiler_params=pltpu.CompilerParams(vmem_limit_bytes=40 * 2**20),
        cost_estimate=pl.CostEstimate(
            flops=4 * 512 * 4096 * 1536, bytes_accessed=28 * 2**20, transcendentals=512
        ),
        name="project_two",
    )(info, pooled, *[piece for piece in pieces for _ in range(2)], weights, valid)


def causal_kernel(own_part, info, queries, kv, start, start_stats, out, out_stats, keys, values, even, odd):
    half, core, y = info[0], info[1], info[2]
    slot = pl.program_id(0)
    own_pair = (y + slot) & 3

    @pl.when(slot == 0)
    def _():
        def prepare(block, _):
            count = jnp.sum(kv[block, 512 : 512 + EXT, :128].astype(F32))
            row = lax.broadcasted_iota(jnp.int32, (512, 128), 0).astype(F32)
            lane = lax.broadcasted_iota(jnp.int32, (512, 128), 1)
            keys[block, :, :128] = kv[block, :512, :128]
            keys[block, :, 128:] = jnp.where((lane == 0) & (row >= count), MASKED, 0.0).astype(BF16)
            values[block] = kv[block, :512, 128:].T
            return 0

        lax.fori_loop(0, 8, prepare, 0)

    lane = lax.broadcasted_iota(jnp.int32, (512, 128), 1)
    query = jnp.concatenate([queries[0], jnp.where(lane == 0, 1.0, 0.0).astype(BF16)], axis=1)

    def block_of(pair, which):
        return (which ^ core) * 4 + ((pair - y) & 3)

    def scores_of(pair, which):
        return lax.dot_general(
            keys[block_of(pair, which)], query, (((1,), (1,)), ((), ())), preferred_element_type=F32
        )

    def absorb(scores, pair, which, carry, edge):
        largest, total, sums = carry
        if edge:
            key = lax.broadcasted_iota(jnp.int32, scores.shape, 0) + which * 512
            own = lax.broadcasted_iota(jnp.int32, scores.shape, 1) + core * 512
            scores = jnp.where(key <= own, scores, MASKED)
        new_largest = jnp.maximum(largest, jnp.max(scores, axis=0, keepdims=True))
        decay = jnp.exp2(largest - new_largest)
        weights = jnp.exp2(scores - new_largest)
        total = total * decay + jnp.sum(weights, axis=0, keepdims=True)
        sums = sums * decay + dot(values[block_of(pair, which)], weights.astype(BF16))
        return new_largest, total, sums

    even[...] = scores_of(0, 0)

    def both(pair, carry, edge=False):
        odd[...] = scores_of(pair, 1)
        carry = absorb(even[...], pair, 0, carry, edge)
        if not edge:
            even[...] = scores_of((pair + 1) & 3, 0)
        return absorb(odd[...], pair, 1, carry, edge)

    if own_part:
        carry = (
            jnp.full((1, 512), MASKED, F32), jnp.zeros((1, 512), F32), jnp.zeros((128, 512), F32)
        )
        carry = lax.fori_loop(0, own_pair, both, carry)
        largest, total, sums = both(own_pair, carry, True)
        out[0] = sums
        out_stats[0] = jnp.concatenate([largest, total, jnp.zeros((6, 512), F32)], axis=0)
    else:
        carry = (start_stats[0, 0:1], start_stats[0, 1:2], start[0])
        _, total, sums = lax.fori_loop(0, half * 4, both, carry)
        out[0] = (sums / total).T.astype(BF16)


def causal_attend(own_part, info, queries, kv, start=None):
    def by_slot(*shape):
        return pl.BlockSpec((1, *shape), lambda s, info: (s, 0, 0))

    sums_shape = jax.ShapeDtypeStruct((4, 128, 512), F32)
    stats_shape = jax.ShapeDtypeStruct((4, 8, 512), F32)
    in_specs = [by_slot(512, 128), pl.BlockSpec((8, 512 + EXT, 256), lambda s, info: (0, 0, 0))]
    operands = [queries, kv]
    if own_part:
        def kernel(info, queries, kv, out, out_stats, *scratch):
            causal_kernel(True, info, queries, kv, None, None, out, out_stats, *scratch)

        out_shape = (sums_shape, stats_shape)
        out_specs = (by_slot(128, 512), by_slot(8, 512))
        tiles = 18
    else:
        def kernel(info, queries, kv, start, start_stats, out, *scratch):
            causal_kernel(False, info, queries, kv, start, start_stats, out, None, *scratch)

        out_shape = jax.ShapeDtypeStruct((4, 512, 128), BF16)
        out_specs = by_slot(512, 128)
        in_specs += [by_slot(128, 512), by_slot(8, 512)]
        operands += list(start)
        tiles = 32
    return pl.pallas_call(
        kernel,
        out_shape=out_shape,
        grid_spec=pltpu.PrefetchScalarGridSpec(
            num_scalar_prefetch=1,
            grid=(4,),
            in_specs=in_specs,
            out_specs=out_specs,
            scratch_shapes=[
                pltpu.VMEM((8, 512, 256), BF16),
                pltpu.VMEM((8, 128, 512), BF16),
                pltpu.VMEM((512, 512), F32),
                pltpu.VMEM((512, 512), F32),
            ],
        ),
        compiler_params=pltpu.CompilerParams(vmem_limit_bytes=40 * 2**20),
        cost_estimate=pl.CostEstimate(
            flops=tiles * 512 * 512 * 512, bytes_accessed=4 * 2**20, transcendentals=tiles * 2**18
        ),
        name="causal_own" if own_part else "causal_first_half",
    )(info, *operands)


def turn_y(value, steps, first=0):
    return lax.ppermute(
        value, "seq", [(i, (i & 9) | ((i + 2 * steps) & 6)) for i in range(first, 16)]
    )


def flip_seq(value, bit):
    return lax.ppermute(value, "seq", [(i, i ^ bit) for i in range(16)])


def per_device(
    tokens, boundary, heads_in, heads_out, gate_up, down_weight, widen, heads_in_two, heads_out_two
):
    seq_position = lax.axis_index("seq")
    me = lax.axis_index("blk")
    rows = tokens.shape[0]
    capacity = 512
    width = D1 // 8
    block_of = jnp.stack([((me ^ (4 * x)) & 4) | ((me + z) & 3) for x, z in PLACES])
    numbers = jnp.arange(8, dtype=jnp.int32)
    place_of = jnp.sum(
        jnp.where(block_of[None, :] == numbers[:, None], numbers[None, :], 0), axis=1
    )

    def later(number, value):
        return number + (value[0, 0].astype(F32) * 0.0).astype(number.dtype)

    heads_in_flat = heads_in.transpose(1, 2, 0).reshape(3 * width, D1)
    gate_flat, up_flat = lax.optimization_barrier((gate_up[:, 0, :], gate_up[:, 1, :]))
    core, y, half = seq_position & 1, (seq_position >> 1) & 3, seq_position >> 3
    piece = lax.dynamic_slice(widen, (seq_position * 96, 0), (96, 512))

    near, far = gather_blk(prepare(tokens, boundary[None, :]))
    piece_here = jnp.concatenate(gather_blk(piece), axis=0)
    piece_across = flip_seq(piece_here, 8)
    marks = jnp.concatenate(
        [part.reshape(4, SENT, D1)[:, rows, :rows] for part in (near, far)], axis=0
    )
    info = later(jnp.concatenate([place_of, seq_position[None]]).astype(jnp.int32), gate_flat)
    qkv, edge = project_one(far, heads_in_flat, info, project_one(near, heads_in_flat))
    halo = lax.ppermute(edge, "seq", [(i, i + 1) for i in range(15)])
    attended = window_attend(info, qkv, halo, window_attend(info, qkv))
    attn_near = dot(attended[: 4 * rows], heads_out).astype(BF16)
    attn_far = dot(attended[4 * rows :], heads_out).astype(BF16)
    piece_pair = later(
        jnp.concatenate([piece_here, piece_across, jnp.zeros((EXT, 512), BF16)], axis=0), attended
    )
    pieces = [piece_pair, turn_y(piece_pair, 3), turn_y(piece_pair, 2), turn_y(piece_pair, 1)]
    mid_stream = (tokens.astype(F32) + reduce_blk(attn_near, attn_far)).astype(BF16)

    normed_mid = normalize(mid_stream).astype(BF16)

    near, far = gather_blk(normed_mid)
    mlp_near = mlp(near, gate_flat, up_flat, down_weight)
    mlp_far = mlp(far, gate_flat, up_flat, down_weight)
    marks = marks.astype(F32)
    counts = jnp.sum(marks, axis=1)
    before = jnp.sum(
        jnp.where(block_of[None, :] < block_of[:, None], counts[None, :], 0.0), axis=1
    )
    steps = jnp.arange(rows)
    running = dot(marks.astype(BF16), (steps[:, None] <= steps[None, :]).astype(BF16))
    slots = jnp.where(marks > 0.5, before[:, None] + running - 1.0, -1.0).astype(jnp.int32)
    span_count = jnp.sum(counts).astype(jnp.int32)
    targets = (block_of[:, None] * 64 + jnp.arange(64)[None, :]).reshape(capacity, 1)
    selector = (slots.reshape(1, 8 * rows) == targets).astype(BF16)
    placed = (
        dot(selector[:, : 4 * rows], mlp_near)
        + dot(selector[:, 4 * rows :], mlp_far)
        + dot(selector[:, :rows], mid_stream)
    ).astype(BF16)
    pooled_own = reduce_blk(placed[:256], placed[256:]).astype(BF16)
    unread = later(jnp.zeros((EXT, 512), BF16), pooled_own)
    pieces[1:] = [lax.dynamic_update_slice(part, unread, (1536, 0)) for part in pieces[1:]]
    pieces = [part for own in pieces for part in (own, flip_seq(own, 1))]
    pooled_own = jnp.concatenate(
        [
            lax.dynamic_slice(
                pooled_own, (0, 96 * ((half ^ h) * 8 + ((y + k) & 3) * 2 + (core ^ c))), (64, 96)
            )
            for k in range(4)
            for c in range(2)
            for h in range(2)
        ],
        axis=1,
    )
    pooled = jnp.concatenate(gather_blk(pooled_own), axis=0)

    far = later(mlp_far, pooled)
    opposite, diagonal = reduce_first(far)
    level_one = (mid_stream.astype(F32) + reduce_second(mlp_near, opposite, diagonal)).astype(BF16)

    validity = (jnp.arange(capacity, dtype=jnp.int32) < span_count).astype(F32)
    valid_rows = jnp.pad(
        validity.reshape(4, 128).astype(BF16), ((0, EXT - 4), (0, 0))
    )
    info_one = jnp.concatenate([block_of, y[None]]).astype(jnp.int32)
    chunks, pairs, wide_cols = project_two(
        info_one, pooled, pieces, heads_in_two.transpose(1, 0, 2), valid_rows
    )
    from_behind = turn_y(chunks[1], 1)
    from_ahead = turn_y(chunks[3], 3)
    from_opposite = turn_y(chunks[2], 2)
    first = lax.ppermute(pairs, "seq", [(i, i + 8) for i in range(8)])
    mine = jnp.stack([chunks[0], from_ahead, from_opposite, from_behind])
    queries, own_kv = mine[:, :capacity, :128], mine[:, :, 128:]
    own_pair = jnp.concatenate([own_kv, flip_seq(own_kv, 1)], axis=0)
    first_kv = jnp.stack(
        [first[0], turn_y(first[3], 3, 8), turn_y(first[2], 2, 8), turn_y(first[1], 1, 8)]
    )
    info_two = jnp.stack([half, core, y]).astype(jnp.int32)
    running = causal_attend(True, later(info_two, opposite), queries, own_pair)
    unread = jnp.broadcast_to(running[1][0:1, 2:3, :128], (1, EXT, 128)).astype(BF16)
    first_kv = lax.dynamic_update_slice(first_kv, unread, (0, capacity, 128))
    first_pair = jnp.concatenate([first_kv, flip_seq(first_kv, 1)], axis=0)
    mixed = causal_attend(False, later(info_two, level_one), queries, first_pair, running)
    back = [mixed[0], turn_y(mixed[3], 3), turn_y(mixed[2], 2), turn_y(mixed[1], 1)]
    heads = jnp.concatenate([back[0], back[1], back[2], back[3]] * 2, axis=1)
    attended_two = lax.dynamic_slice(heads, (0, ((4 - y) & 3) * 128), (capacity, 512))

    def columns(place):
        part = lax.dynamic_slice(heads_out_two, (0, block_of[place] * 512), (512, 512))
        return dot(attended_two, part).astype(BF16)

    out_far = jnp.concatenate([columns(place) for place in range(4, 8)], axis=0)
    out_near = jnp.concatenate([columns(place) for place in range(4)], axis=0)
    level_two = (
        (wide_cols.astype(F32) + reduce_blk(out_near, out_far)) * validity[:, None]
    ).astype(BF16)
    return (level_one, level_two)


def solution(mesh):
    placed = (
        P(("seq", "blk"), None),
        P(("seq", "blk")),
        P(None, None, "blk"),
        P("blk", None),
        P(None, None, "blk"),
        P("blk", None),
        P(None, "blk"),
        P(None, None, "blk"),
        P("blk", None),
    )
    return jax.shard_map(
        per_device,
        mesh=mesh,
        in_specs=placed,
        out_specs=(P(("seq", "blk"), None), P("seq", "blk")),
        check_vma=False,
    )
```

```python
import jax
import jax.numpy as jnp
from jax import lax
from jax.experimental import pallas as pl
from jax.experimental.pallas import tpu as pltpu
from jax.sharding import PartitionSpec as P

D1 = 1536
H1 = 24
D2 = 4096
H2 = 32
WIN = 512
EXT = 16
SENT = 128 + EXT
BF16 = jnp.bfloat16
F32 = jnp.float32
MASKED = -1e30
SCORE_FACTOR = 128 ** (-0.5) * 1.4426950408889634

PLACES = ((0, 0), (1, 0), (0, 1), (0, 3), (0, 2), (1, 2), (1, 1), (1, 3))


def flip_x(value):
    return lax.ppermute(value, "blk", [(i, i ^ 4) for i in range(8)])


def turn_z(value, steps):
    return lax.ppermute(value, "blk", [(i, (i & 4) | ((i + steps) & 3)) for i in range(8)])


def gather_blk(own):
    across = flip_x(own)
    behind = turn_z(own, 1)
    ahead = turn_z(own, 3)
    first = jnp.concatenate([own, across], axis=0)
    second = jnp.concatenate([ahead, behind], axis=0)
    opposite = turn_z(first, 2)
    diagonal = flip_x(second)
    near = jnp.concatenate([first, second], axis=0)
    far = jnp.concatenate([opposite, diagonal], axis=0)
    return near, far


def reduce_first(far):
    count = far.shape[0] // 4
    return turn_z(far[: 2 * count], 2), flip_x(far[2 * count :])


def reduce_second(near, opposite, diagonal):
    count = near.shape[0] // 4

    def plus(block, other):
        return near[block * count : (block + 1) * count].astype(F32) + other.astype(F32)

    across = flip_x(plus(1, opposite[count:]).astype(BF16))
    behind = turn_z(plus(2, diagonal[:count]).astype(BF16), 1)
    ahead = turn_z(plus(3, diagonal[count:]).astype(BF16), 3)
    return (
        plus(0, opposite[:count])
        + across.astype(F32)
        + behind.astype(F32)
        + ahead.astype(F32)
    )


def reduce_blk(near, far):
    return reduce_second(near, *reduce_first(far))


def normalize(values):
    floats = values.astype(F32)
    return floats * lax.rsqrt(jnp.mean(floats * floats, axis=-1, keepdims=True) + 1e-06)


def dot(left, right):
    return jnp.dot(left, right, preferred_element_type=F32)


def dot_t(left, right):
    return lax.dot_general(left, right, (((1,), (1,)), ((), ())), preferred_element_type=F32)


def window_kernel(blocks, info, qkv, halo, before, out):
    rows, width, size, stride = 128, D1 // 8, D1 // H1, SENT
    key_count = WIN + rows
    i = lax.broadcasted_iota(jnp.int32, (rows, key_count), 0)
    j = lax.broadcasted_iota(jnp.int32, (rows, key_count), 1)
    band = (j > i) & (j <= i + WIN)
    seq_position = info[8]
    if before is not None:
        out[...] = before[...]
    for n in blocks:
        place = info[n]
        keys, values = [], []
        for k in range(n - 4, n + 1):
            if k >= 0:
                start = pl.multiple_of(info[k] * stride, 16)
                block = qkv[pl.ds(start, rows), :]
                keys.append(block[:, :width])
                values.append(block[:, width : 2 * width])
            else:
                block = halo[(k + 4) * rows : (k + 5) * rows, :]
                keys.append(block[:, :width])
                values.append(block[:, width:])
        keys = jnp.concatenate(keys, axis=0)
        values = jnp.concatenate(values, axis=0)
        queries = qkv[pl.ds(pl.multiple_of(place * stride, 16), rows), 2 * width :]
        allowed = band
        if n < 4:
            allowed = band & (j + ((n - 4) * rows + seq_position * 1024) >= 0)
        parts = []
        for h in range(width // size):
            cut = slice(h * size, (h + 1) * size)
            scores = lax.dot_general(
                queries[:, cut], keys[:, cut], (((1,), (1,)), ((), ())),
                preferred_element_type=F32,
            ) * size ** (-0.5)
            scores = jnp.where(allowed, scores, MASKED)
            largest = jnp.max(scores, axis=-1, keepdims=True)
            weights = jnp.exp(scores - largest)
            total = jnp.sum(weights, axis=-1, keepdims=True)
            parts.append(dot(weights.astype(BF16), values[:, cut]) / total)
        out[pl.ds(pl.multiple_of(place * rows, 16), rows), :] = jnp.concatenate(
            parts, axis=1
        ).astype(BF16)


def window_attend(info, qkv, halo=None, before=None):
    if halo is None:
        def kernel(info, qkv, out):
            window_kernel(range(4, 8), info, qkv, None, None, out)

        operands = (info, qkv)
    else:
        def kernel(info, qkv, halo, before, out):
            window_kernel(range(4), info, qkv, halo, before, out)

        operands = (info, qkv, halo, before)
    vmem = pl.BlockSpec(memory_space=pltpu.VMEM)
    return pl.pallas_call(
        kernel,
        out_shape=jax.ShapeDtypeStruct((1024, D1 // 8), BF16),
        in_specs=[pl.BlockSpec(memory_space=pltpu.SMEM)] + [vmem] * (len(operands) - 1),
        out_specs=vmem,
        compiler_params=pltpu.CompilerParams(vmem_limit_bytes=32 * 2**20),
        cost_estimate=pl.CostEstimate(
            flops=12 * 128 * 640 * 256, bytes_accessed=2 * 2**20, transcendentals=12 * 128 * 640
        ),
        name="window_late" if halo is None else "window_early",
    )(*operands)


def prepare_kernel(tokens, marks, out):
    floats = tokens[...].astype(F32)
    scale = lax.rsqrt(jnp.mean(floats * floats, axis=-1, keepdims=True) + 1e-06)
    out[:128, :] = (floats * scale).astype(BF16)
    out[128:, :] = jnp.zeros((EXT, D1), BF16)
    out[128:, :128] = jnp.broadcast_to(marks[...].astype(F32), (EXT, 128)).astype(BF16)


def prepare(tokens, marks):
    return pl.pallas_call(
        prepare_kernel,
        out_shape=jax.ShapeDtypeStruct((SENT, D1), BF16),
        in_specs=[pl.BlockSpec(memory_space=pltpu.VMEM)] * 2,
        out_specs=pl.BlockSpec(memory_space=pltpu.VMEM),
        name="prepare",
    )(tokens, marks)


def near_kernel(rows, weights, out):
    out[:, :384] = dot_t(rows[...], weights[192:, :]).astype(BF16)
    out[:, 384:] = dot_t(rows[...], weights[:192, :]).astype(BF16)


def far_kernel(info, near, rows, weights, out, edge):
    half = 4 * SENT
    out[:half, :] = near[...]
    out[half:, :384] = dot_t(rows[...], weights[192:, :]).astype(BF16)
    for k in range(4):
        start = pl.multiple_of(info[4 + k] * SENT, 16)
        edge[k * 128 : (k + 1) * 128, :] = out[pl.ds(start, 128), :384]
    out[half:, 384:] = dot_t(rows[...], weights[:192, :]).astype(BF16)


def project_one(rows, weights, info=None, near=None):
    vmem = pl.BlockSpec(memory_space=pltpu.VMEM)
    cost = pl.CostEstimate(flops=2 * 576 * 576 * D1, bytes_accessed=5 * 2**20, transcendentals=0)
    params = pltpu.CompilerParams(vmem_limit_bytes=24 * 2**20)
    if near is None:
        return pl.pallas_call(
            near_kernel,
            out_shape=jax.ShapeDtypeStruct((4 * SENT, 576), BF16),
            in_specs=[vmem] * 2,
            out_specs=vmem,
            compiler_params=params,
            cost_estimate=cost,
            name="project_near",
        )(rows, weights)
    return pl.pallas_call(
        far_kernel,
        out_shape=(
            jax.ShapeDtypeStruct((8 * SENT, 576), BF16), jax.ShapeDtypeStruct((WIN, 384), BF16)
        ),
        in_specs=[pl.BlockSpec(memory_space=pltpu.SMEM)] + [vmem] * 3,
        out_specs=(vmem, vmem),
        compiler_params=params,
        cost_estimate=cost,
        name="project_far",
    )(info, near, rows, weights)


def mlp_kernel(rows, gate, up, down, out):
    def some(step, _):
        cut = pl.ds(pl.multiple_of(step * 256, 256), 256)
        block = rows[cut, :]
        gated = dot(block, gate[...])
        hidden = gated / (1.0 + jnp.exp(-gated)) * dot(block, up[...])
        out[cut, :] = dot(hidden.astype(BF16), down[...]).astype(BF16)
        return 0

    lax.fori_loop(0, rows.shape[0] // 256, some, 0)


def mlp(rows, gate, up, down):
    return pl.pallas_call(
        mlp_kernel,
        out_shape=jax.ShapeDtypeStruct(rows.shape, BF16),
        in_specs=[pl.BlockSpec(memory_space=pltpu.VMEM)] * 4,
        out_specs=pl.BlockSpec(memory_space=pltpu.VMEM),
        compiler_params=pltpu.CompilerParams(vmem_limit_bytes=32 * 2**20),
        cost_estimate=pl.CostEstimate(
            flops=2 * 512 * 1536 * 1536, bytes_accessed=8 * 2**20, transcendentals=512 * 512
        ),
        name="mlp",
    )(rows, gate, up, down)


def project_kernel(info, pooled, *refs):
    pieces, (weights, valid, chunks, pairs, wide_own, total, squares) = refs[:8], refs[8:]
    step = pl.program_id(0)
    y = info[8]

    @pl.when(step == 0)
    def _():
        total[...] = jnp.zeros_like(total)
        squares[...] = jnp.zeros_like(squares)

    wide = dot(pooled[...], jnp.concatenate([piece[...] for piece in pieces], axis=0)).astype(BF16)
    floats = wide.astype(F32)
    squares[...] += jnp.broadcast_to(
        jnp.sum(floats * floats, axis=-1, keepdims=True), squares.shape
    )
    for i in range(3):
        total[:, i * 512 : (i + 1) * 512] += dot(wide, weights[i])

    @pl.when(step == 0)
    def _():
        for p in range(8):
            start = pl.multiple_of(info[p] * 64, 64)
            wide_own[pl.ds(start, 64), :] = wide[p * 64 : (p + 1) * 64]

    @pl.when(step == 7)
    def _():
        scale = lax.rsqrt(squares[...] / D2 + 1e-06)
        for k in range(4):
            head = (y + k) & 3
            for i in range(3):
                cut = slice(i * 128, (i + 1) * 128)
                lanes = pl.ds(pl.multiple_of(i * 512 + head * 128, 128), 128)
                part = total[:, lanes] * (scale * SCORE_FACTOR if i == 0 else scale)
                part = part.astype(BF16)
                for p in range(8):
                    start = pl.multiple_of(info[p] * 64, 64)
                    chunks[k, pl.ds(start, 64), cut] = part[p * 64 : (p + 1) * 64]
                    if i > 0:
                        pairs[k, pl.ds(start, 64), (i - 1) * 128 : i * 128] = part[p * 64 : (p + 1) * 64]
                chunks[k, 512:, cut] = valid[...]
                if i > 0:
                    pairs[k, 512:, (i - 1) * 128 : i * 128] = valid[...]


def project_two(info, pooled, pieces, weights, valid):
    return pl.pallas_call(
        project_kernel,
        out_shape=(
            jax.ShapeDtypeStruct((4, 512 + EXT, 384), BF16),
            jax.ShapeDtypeStruct((4, 512 + EXT, 256), BF16),
            jax.ShapeDtypeStruct((512, 512), BF16),
        ),
        grid_spec=pltpu.PrefetchScalarGridSpec(
            num_scalar_prefetch=1,
            grid=(8,),
            in_specs=[
                pl.BlockSpec((512, D1), lambda s, info: (0, 0)),
                *[pl.BlockSpec((192, 512), lambda s, info: (s, 0)) for _ in range(8)],
                pl.BlockSpec((3, 512, 512), lambda s, info: (0, info[s], 0)),
                pl.BlockSpec((EXT, 128), lambda s, info: (0, 0)),
            ],
            out_specs=(
                pl.BlockSpec((4, 512 + EXT, 384), lambda s, info: (0, 0, 0)),
                pl.BlockSpec((4, 512 + EXT, 256), lambda s, info: (0, 0, 0)),
                pl.BlockSpec((512, 512), lambda s, info: (0, 0)),
            ),
            scratch_shapes=[pltpu.VMEM((512, 1536), F32), pltpu.VMEM((512, 128), F32)],
        ),
        compiler_params=pltpu.CompilerParams(vmem_limit_bytes=40 * 2**20),
        cost_estimate=pl.CostEstimate(
            flops=4 * 512 * 4096 * 1536, bytes_accessed=28 * 2**20, transcendentals=512
        ),
        name="project_two",
    )(info, pooled, *pieces, weights, valid)


def causal_kernel(own_part, info, queries, kv_pair, start, start_stats, out, out_stats, keys, values, even, odd):
    half, core, y = info[0], info[1], info[2]
    slot = pl.program_id(0)
    own_pair = (y + slot) & 3

    @pl.when(slot == 0)
    def _():
        def prepare(block, _):
            row = lax.broadcasted_iota(jnp.int32, (512, 128), 0).astype(F32)
            lane = lax.broadcasted_iota(jnp.int32, (512, 128), 1)
            for which, kv in enumerate(kv_pair):
                count = jnp.sum(kv[block, 512 : 512 + EXT, :128].astype(F32))
                invalid = (lane == 0) & (row >= count)
                keys[which * 4 + block, :, :128] = kv[block, :512, :128]
                keys[which * 4 + block, :, 128:] = jnp.where(invalid, MASKED, 0.0).astype(BF16)
                values[which * 4 + block] = kv[block, :512, 128:].T
            return 0

        lax.fori_loop(0, 4, prepare, 0)

    lane = lax.broadcasted_iota(jnp.int32, (512, 128), 1)
    query = jnp.concatenate([queries[0], jnp.where(lane == 0, 1.0, 0.0).astype(BF16)], axis=1)

    def block_of(pair, which):
        return (which ^ core) * 4 + ((pair - y) & 3)

    def scores_of(pair, which):
        return lax.dot_general(
            keys[block_of(pair, which)], query, (((1,), (1,)), ((), ())), preferred_element_type=F32
        )

    def absorb(scores, pair, which, carry, edge):
        largest, total, sums = carry
        if edge:
            key = lax.broadcasted_iota(jnp.int32, scores.shape, 0) + which * 512
            own = lax.broadcasted_iota(jnp.int32, scores.shape, 1) + core * 512
            scores = jnp.where(key <= own, scores, MASKED)
        new_largest = jnp.maximum(largest, jnp.max(scores, axis=0, keepdims=True))
        decay = jnp.exp2(largest - new_largest)
        weights = jnp.exp2(scores - new_largest)
        total = total * decay + jnp.sum(weights, axis=0, keepdims=True)
        sums = sums * decay + dot(values[block_of(pair, which)], weights.astype(BF16))
        return new_largest, total, sums

    even[...] = scores_of(0, 0)

    def both(pair, carry, edge=False):
        odd[...] = scores_of(pair, 1)
        carry = absorb(even[...], pair, 0, carry, edge)
        if not edge:
            even[...] = scores_of((pair + 1) & 3, 0)
        return absorb(odd[...], pair, 1, carry, edge)

    if own_part:
        carry = (
            jnp.full((1, 512), MASKED, F32), jnp.zeros((1, 512), F32), jnp.zeros((128, 512), F32)
        )
        carry = lax.fori_loop(0, own_pair, both, carry)
        largest, total, sums = both(own_pair, carry, True)
        out[0] = sums
        out_stats[0] = jnp.concatenate([largest, total, jnp.zeros((6, 512), F32)], axis=0)
    else:
        carry = (start_stats[0, 0:1], start_stats[0, 1:2], start[0])
        _, total, sums = lax.fori_loop(0, half * 4, both, carry)
        out[0] = (sums / total).T.astype(BF16)


def causal_attend(own_part, info, queries, kv_pair, start=None):
    def by_slot(*shape):
        return pl.BlockSpec((1, *shape), lambda s, info: (s, 0, 0))

    sums_shape = jax.ShapeDtypeStruct((4, 128, 512), F32)
    stats_shape = jax.ShapeDtypeStruct((4, 8, 512), F32)
    whole = pl.BlockSpec((4, 512 + EXT, 256), lambda s, info: (0, 0, 0))
    in_specs = [by_slot(512, 128), whole, whole]
    operands = [queries, *kv_pair]
    if own_part:
        def kernel(info, queries, kv, other, out, out_stats, *scratch):
            causal_kernel(True, info, queries, (kv, other), None, None, out, out_stats, *scratch)

        out_shape = (sums_shape, stats_shape)
        out_specs = (by_slot(128, 512), by_slot(8, 512))
        tiles = 18
    else:
        def kernel(info, queries, kv, other, start, start_stats, out, *scratch):
            causal_kernel(False, info, queries, (kv, other), start, start_stats, out, None, *scratch)

        out_shape = jax.ShapeDtypeStruct((4, 512, 128), BF16)
        out_specs = by_slot(512, 128)
        in_specs += [by_slot(128, 512), by_slot(8, 512)]
        operands += list(start)
        tiles = 32
    return pl.pallas_call(
        kernel,
        out_shape=out_shape,
        grid_spec=pltpu.PrefetchScalarGridSpec(
            num_scalar_prefetch=1,
            grid=(4,),
            in_specs=in_specs,
            out_specs=out_specs,
            scratch_shapes=[
                pltpu.VMEM((8, 512, 256), BF16),
                pltpu.VMEM((8, 128, 512), BF16),
                pltpu.VMEM((512, 512), F32),
                pltpu.VMEM((512, 512), F32),
            ],
        ),
        compiler_params=pltpu.CompilerParams(vmem_limit_bytes=40 * 2**20),
        cost_estimate=pl.CostEstimate(
            flops=tiles * 512 * 512 * 512, bytes_accessed=4 * 2**20, transcendentals=tiles * 2**18
        ),
        name="causal_own" if own_part else "causal_first_half",
    )(info, *operands)


def turn_y(value, steps, first=0):
    return lax.ppermute(
        value, "seq", [(i, (i & 9) | ((i + 2 * steps) & 6)) for i in range(first, 16)]
    )


def flip_seq(value, bit):
    return lax.ppermute(value, "seq", [(i, i ^ bit) for i in range(16)])


def per_device(
    tokens, boundary, heads_in, heads_out, gate_up, down_weight, widen, heads_in_two, heads_out_two
):
    seq_position = lax.axis_index("seq")
    me = lax.axis_index("blk")
    rows = tokens.shape[0]
    capacity = 512
    width = D1 // 8
    block_of = jnp.stack([((me ^ (4 * x)) & 4) | ((me + z) & 3) for x, z in PLACES])
    numbers = jnp.arange(8, dtype=jnp.int32)
    place_of = jnp.sum(
        jnp.where(block_of[None, :] == numbers[:, None], numbers[None, :], 0), axis=1
    )

    def later(number, value):
        return number + (value[0, 0].astype(F32) * 0.0).astype(number.dtype)

    heads_in_flat = heads_in.transpose(1, 2, 0).reshape(3 * width, D1)
    gate_flat, up_flat = lax.optimization_barrier((gate_up[:, 0, :], gate_up[:, 1, :]))
    core, y, half = seq_position & 1, (seq_position >> 1) & 3, seq_position >> 3
    piece = lax.dynamic_slice(widen, (seq_position * 96, 0), (96, 512))

    near, far = gather_blk(prepare(tokens, boundary[None, :]))
    piece = later(jnp.concatenate([piece, flip_seq(piece, 8)], axis=0), near)
    piece = jnp.concatenate([*gather_blk(piece), jnp.zeros((EXT, 512), BF16)], axis=0)
    pieces = [piece, turn_y(piece, 3), turn_y(piece, 2), turn_y(piece, 1)]
    marks = jnp.concatenate(
        [part.reshape(4, SENT, D1)[:, rows, :rows] for part in (near, far)], axis=0
    )
    info = later(jnp.concatenate([place_of, seq_position[None]]).astype(jnp.int32), gate_flat)
    qkv, edge = project_one(far, heads_in_flat, info, project_one(near, heads_in_flat))
    halo = lax.ppermute(edge, "seq", [(i, i + 1) for i in range(15)])
    attended = window_attend(info, qkv, halo, window_attend(info, qkv))
    attn_near = dot(attended[: 4 * rows], heads_out).astype(BF16)
    attn_far = dot(attended[4 * rows :], heads_out).astype(BF16)
    mid_stream = (tokens.astype(F32) + reduce_blk(attn_near, attn_far)).astype(BF16)

    normed_mid = normalize(mid_stream).astype(BF16)

    near, far = gather_blk(normed_mid)
    mlp_near = mlp(near, gate_flat, up_flat, down_weight)
    mlp_far = mlp(far, gate_flat, up_flat, down_weight)
    marks = marks.astype(F32)
    counts = jnp.sum(marks, axis=1)
    before = jnp.sum(
        jnp.where(block_of[None, :] < block_of[:, None], counts[None, :], 0.0), axis=1
    )
    steps = jnp.arange(rows)
    running = dot(marks.astype(BF16), (steps[:, None] <= steps[None, :]).astype(BF16))
    slots = jnp.where(marks > 0.5, before[:, None] + running - 1.0, -1.0).astype(jnp.int32)
    span_count = jnp.sum(counts).astype(jnp.int32)
    targets = (block_of[:, None] * 64 + jnp.arange(64)[None, :]).reshape(capacity, 1)
    selector = (slots.reshape(1, 8 * rows) == targets).astype(BF16)
    placed = (
        dot(selector[:, : 4 * rows], mlp_near)
        + dot(selector[:, 4 * rows :], mlp_far)
        + dot(selector[:, :rows], mid_stream)
    ).astype(BF16)
    pooled_own = reduce_blk(placed[:256], placed[256:]).astype(BF16)
    for k, value in ((1, mlp_near), (2, pooled_own), (3, mlp_near)):
        unread = later(jnp.zeros((EXT, 512), BF16), value)
        pieces[k] = lax.dynamic_update_slice(pieces[k], unread, (1536, 0))
    pieces = [part for own in pieces for part in (own, flip_seq(own, 1))]
    pooled_own = jnp.concatenate(
        [
            lax.dynamic_slice(
                pooled_own, (0, 96 * ((half ^ h) * 8 + ((y + k) & 3) * 2 + (core ^ c))), (64, 96)
            )
            for k in range(4)
            for c in range(2)
            for h in range(2)
        ],
        axis=1,
    )
    pooled = jnp.concatenate(gather_blk(pooled_own), axis=0)

    far = later(mlp_far, pooled)
    opposite, diagonal = reduce_first(far)
    level_one = mid_stream.astype(F32) + reduce_second(mlp_near, opposite, diagonal)

    validity = (jnp.arange(capacity, dtype=jnp.int32) < span_count).astype(F32)
    valid_rows = jnp.pad(
        validity.reshape(4, 128).astype(BF16), ((0, EXT - 4), (0, 0))
    )
    info_one = jnp.concatenate([block_of, y[None]]).astype(jnp.int32)
    chunks, pairs, wide_cols = project_two(
        info_one, pooled, pieces, heads_in_two.transpose(1, 0, 2), valid_rows
    )
    from_behind = turn_y(chunks[1], 1)
    from_ahead = turn_y(chunks[3], 3)
    from_opposite = turn_y(chunks[2], 2)
    first = lax.ppermute(pairs, "seq", [(i, i + 8) for i in range(8)])
    mine = jnp.stack([chunks[0], from_ahead, from_opposite, from_behind])
    queries, own_kv = mine[:, :capacity, :128], mine[:, :, 128:]
    info_two = jnp.stack([half, core, y]).astype(jnp.int32)
    running = causal_attend(True, later(info_two, first[0]), queries, (own_kv, flip_seq(own_kv, 1)))
    first_kv = jnp.stack(
        [first[0], turn_y(first[3], 3, 8), turn_y(first[2], 2, 8), turn_y(first[1], 1, 8)]
    )
    first_kv = first_kv + running[1][0, 2, 0].astype(BF16)
    mixed = causal_attend(False, info_two, queries, (first_kv, flip_seq(first_kv, 1)), running)
    back = [mixed[0], turn_y(mixed[3], 3), turn_y(mixed[2], 2), turn_y(mixed[1], 1)]
    heads = jnp.concatenate([back[0], back[1], back[2], back[3]] * 2, axis=1)
    attended_two = lax.dynamic_slice(heads, (0, ((4 - y) & 3) * 128), (capacity, 512))

    level_one = later(level_one, mixed[0]).astype(BF16)
    column_of = later(block_of, level_one)

    def columns(place):
        part = lax.dynamic_slice(heads_out_two, (0, column_of[place] * 512), (512, 512))
        return dot(attended_two, part).astype(BF16)

    out_far = jnp.concatenate([columns(place) for place in range(4, 8)], axis=0)
    out_near = jnp.concatenate([columns(place) for place in range(4)], axis=0)
    out_near = lax.optimization_barrier(out_near)
    level_two = (
        (wide_cols.astype(F32) + reduce_blk(out_near, out_far)) * validity[:, None]
    ).astype(BF16)
    return (level_one, level_two)


def solution(mesh):
    placed = (
        P(("seq", "blk"), None),
        P(("seq", "blk")),
        P(None, None, "blk"),
        P("blk", None),
        P(None, None, "blk"),
        P("blk", None),
        P(None, "blk"),
        P(None, None, "blk"),
        P("blk", None),
    )
    return jax.shard_map(
        per_device,
        mesh=mesh,
        in_specs=placed,
        out_specs=(P(("seq", "blk"), None), P("seq", "blk")),
        check_vma=False,
    )
```

```python
import jax
import jax.numpy as jnp
from jax import lax
from jax.experimental import pallas as pl
from jax.experimental.pallas import tpu as pltpu
from jax.sharding import PartitionSpec as P

D1 = 1536
H1 = 24
D2 = 4096
H2 = 32
WIN = 512
EXT = 16
SENT = 128 + EXT
BF16 = jnp.bfloat16
F32 = jnp.float32
MASKED = -1e30
SCORE_FACTOR = 128 ** (-0.5) * 1.4426950408889634

PLACES = ((0, 0), (1, 0), (0, 1), (0, 3), (0, 2), (1, 2), (1, 1), (1, 3))


def flip_x(value):
    return lax.ppermute(value, "blk", [(i, i ^ 4) for i in range(8)])


def turn_z(value, steps):
    return lax.ppermute(value, "blk", [(i, (i & 4) | ((i + steps) & 3)) for i in range(8)])


def later(array, value):
    return array + (value[0, 0].astype(F32) * 0.0).astype(array.dtype)


def gather_blk(own, between=None):
    across = flip_x(own)
    behind = turn_z(own, 1)
    ahead = turn_z(own, 3)
    first = jnp.concatenate([own, across], axis=0)
    second = jnp.concatenate([ahead, behind], axis=0)
    if between is not None:
        first, second = later(first, between), later(second, between)
    opposite = turn_z(first, 2)
    diagonal = flip_x(second)
    near = jnp.concatenate([first, second], axis=0)
    far = jnp.concatenate([opposite, diagonal], axis=0)
    return near, far


def reduce_first(far):
    count = far.shape[0] // 4
    return turn_z(far[: 2 * count], 2), flip_x(far[2 * count :])


def reduce_second(near, opposite, diagonal):
    count = near.shape[0] // 4

    def plus(block, other):
        return near[block * count : (block + 1) * count].astype(F32) + other.astype(F32)

    across = flip_x(plus(1, opposite[count:]).astype(BF16))
    behind = turn_z(plus(2, diagonal[:count]).astype(BF16), 1)
    ahead = turn_z(plus(3, diagonal[count:]).astype(BF16), 3)
    return (
        plus(0, opposite[:count])
        + across.astype(F32)
        + behind.astype(F32)
        + ahead.astype(F32)
    )


def reduce_blk(near, far):
    return reduce_second(near, *reduce_first(far))


def normalize(values):
    floats = values.astype(F32)
    return floats * lax.rsqrt(jnp.mean(floats * floats, axis=-1, keepdims=True) + 1e-06)


def dot(left, right):
    return jnp.dot(left, right, preferred_element_type=F32)


def dot_t(left, right):
    return lax.dot_general(left, right, (((1,), (1,)), ((), ())), preferred_element_type=F32)


def window_kernel(blocks, info, qkv, halo, before, out):
    rows, width, size, stride = 128, D1 // 8, D1 // H1, SENT
    key_count = WIN + rows
    i = lax.broadcasted_iota(jnp.int32, (rows, key_count), 0)
    j = lax.broadcasted_iota(jnp.int32, (rows, key_count), 1)
    band = (j > i) & (j <= i + WIN)
    seq_position = info[8]
    if before is not None:
        out[...] = before[...]
    for n in blocks:
        place = info[n]
        keys, values = [], []
        for k in range(n - 4, n + 1):
            if k >= 0:
                start = pl.multiple_of(info[k] * stride, 16)
                block = qkv[pl.ds(start, rows), :]
                keys.append(block[:, :width])
                values.append(block[:, width : 2 * width])
            else:
                block = halo[(k + 4) * rows : (k + 5) * rows, :]
                keys.append(block[:, :width])
                values.append(block[:, width:])
        keys = jnp.concatenate(keys, axis=0)
        values = jnp.concatenate(values, axis=0)
        queries = qkv[pl.ds(pl.multiple_of(place * stride, 16), rows), 2 * width :]
        allowed = band
        if n < 4:
            allowed = band & (j + ((n - 4) * rows + seq_position * 1024) >= 0)
        parts = []
        for h in range(width // size):
            cut = slice(h * size, (h + 1) * size)
            scores = lax.dot_general(
                queries[:, cut], keys[:, cut], (((1,), (1,)), ((), ())),
                preferred_element_type=F32,
            ) * size ** (-0.5)
            scores = jnp.where(allowed, scores, MASKED)
            largest = jnp.max(scores, axis=-1, keepdims=True)
            weights = jnp.exp(scores - largest)
            total = jnp.sum(weights, axis=-1, keepdims=True)
            parts.append(dot(weights.astype(BF16), values[:, cut]) / total)
        out[pl.ds(pl.multiple_of(place * rows, 16), rows), :] = jnp.concatenate(
            parts, axis=1
        ).astype(BF16)


def window_attend(info, qkv, halo=None, before=None):
    if halo is None:
        def kernel(info, qkv, out):
            window_kernel(range(4, 8), info, qkv, None, None, out)

        operands = (info, qkv)
    else:
        def kernel(info, qkv, halo, before, out):
            window_kernel(range(4), info, qkv, halo, before, out)

        operands = (info, qkv, halo, before)
    vmem = pl.BlockSpec(memory_space=pltpu.VMEM)
    return pl.pallas_call(
        kernel,
        out_shape=jax.ShapeDtypeStruct((1024, D1 // 8), BF16),
        in_specs=[pl.BlockSpec(memory_space=pltpu.SMEM)] + [vmem] * (len(operands) - 1),
        out_specs=vmem,
        compiler_params=pltpu.CompilerParams(vmem_limit_bytes=32 * 2**20),
        cost_estimate=pl.CostEstimate(
            flops=12 * 128 * 640 * 256, bytes_accessed=2 * 2**20, transcendentals=12 * 128 * 640
        ),
        name="window_late" if halo is None else "window_early",
    )(*operands)


def prepare_kernel(tokens, marks, out):
    floats = tokens[...].astype(F32)
    scale = lax.rsqrt(jnp.mean(floats * floats, axis=-1, keepdims=True) + 1e-06)
    out[:128, :] = (floats * scale).astype(BF16)
    out[128:, :] = jnp.zeros((EXT, D1), BF16)
    out[128:, :128] = jnp.broadcast_to(marks[...].astype(F32), (EXT, 128)).astype(BF16)


def prepare(tokens, marks):
    return pl.pallas_call(
        prepare_kernel,
        out_shape=jax.ShapeDtypeStruct((SENT, D1), BF16),
        in_specs=[pl.BlockSpec(memory_space=pltpu.VMEM)] * 2,
        out_specs=pl.BlockSpec(memory_space=pltpu.VMEM),
        name="prepare",
    )(tokens, marks)


def near_kernel(rows, weights, out):
    out[:, :384] = dot_t(rows[...], weights[192:, :]).astype(BF16)
    out[:, 384:] = dot_t(rows[...], weights[:192, :]).astype(BF16)


def far_kernel(info, near, rows, weights, out, edge):
    half = 4 * SENT
    out[:half, :] = near[...]
    out[half:, :384] = dot_t(rows[...], weights[192:, :]).astype(BF16)
    for k in range(4):
        start = pl.multiple_of(info[4 + k] * SENT, 16)
        edge[k * 128 : (k + 1) * 128, :] = out[pl.ds(start, 128), :384]
    out[half:, 384:] = dot_t(rows[...], weights[:192, :]).astype(BF16)


def project_one(rows, weights, info=None, near=None):
    vmem = pl.BlockSpec(memory_space=pltpu.VMEM)
    cost = pl.CostEstimate(flops=2 * 576 * 576 * D1, bytes_accessed=5 * 2**20, transcendentals=0)
    params = pltpu.CompilerParams(vmem_limit_bytes=24 * 2**20)
    if near is None:
        return pl.pallas_call(
            near_kernel,
            out_shape=jax.ShapeDtypeStruct((4 * SENT, 576), BF16),
            in_specs=[vmem] * 2,
            out_specs=vmem,
            compiler_params=params,
            cost_estimate=cost,
            name="project_near",
        )(rows, weights)
    return pl.pallas_call(
        far_kernel,
        out_shape=(
            jax.ShapeDtypeStruct((8 * SENT, 576), BF16), jax.ShapeDtypeStruct((WIN, 384), BF16)
        ),
        in_specs=[pl.BlockSpec(memory_space=pltpu.SMEM)] + [vmem] * 3,
        out_specs=(vmem, vmem),
        compiler_params=params,
        cost_estimate=cost,
        name="project_far",
    )(info, near, rows, weights)


def mlp_kernel(rows, gate, up, down, out):
    def some(step, _):
        cut = pl.ds(pl.multiple_of(step * 256, 256), 256)
        block = rows[cut, :]
        gated = dot(block, gate[...])
        hidden = gated / (1.0 + jnp.exp(-gated)) * dot(block, up[...])
        out[cut, :] = dot(hidden.astype(BF16), down[...]).astype(BF16)
        return 0

    lax.fori_loop(0, rows.shape[0] // 256, some, 0)


def mlp(rows, gate, up, down):
    return pl.pallas_call(
        mlp_kernel,
        out_shape=jax.ShapeDtypeStruct(rows.shape, BF16),
        in_specs=[pl.BlockSpec(memory_space=pltpu.VMEM)] * 4,
        out_specs=pl.BlockSpec(memory_space=pltpu.VMEM),
        compiler_params=pltpu.CompilerParams(vmem_limit_bytes=32 * 2**20),
        cost_estimate=pl.CostEstimate(
            flops=2 * 512 * 1536 * 1536, bytes_accessed=8 * 2**20, transcendentals=512 * 512
        ),
        name="mlp",
    )(rows, gate, up, down)


def project_kernel(info, pooled, pieces, weights, valid, chunks, wide_own, total, squares):
    step = pl.program_id(0)
    y = info[8]

    @pl.when(step == 0)
    def _():
        total[...] = jnp.zeros_like(total)
        squares[...] = jnp.zeros_like(squares)

    wide = dot(pooled[...], pieces[...].reshape(D1, 512)).astype(BF16)
    floats = wide.astype(F32)
    squares[...] += jnp.broadcast_to(
        jnp.sum(floats * floats, axis=-1, keepdims=True), squares.shape
    )
    for i in range(3):
        total[:, i * 512 : (i + 1) * 512] += dot(wide, weights[i])

    @pl.when(step == 0)
    def _():
        for p in range(8):
            start = pl.multiple_of(info[p] * 64, 64)
            wide_own[pl.ds(start, 64), :] = wide[p * 64 : (p + 1) * 64]

    @pl.when(step == 7)
    def _():
        scale = lax.rsqrt(squares[...] / D2 + 1e-06)
        for k in range(4):
            head = (y + k) & 3
            for i in range(3):
                cut = slice(i * 128, (i + 1) * 128)
                lanes = pl.ds(pl.multiple_of(i * 512 + head * 128, 128), 128)
                part = total[:, lanes] * (scale * SCORE_FACTOR if i == 0 else scale)
                part = part.astype(BF16)
                for p in range(8):
                    start = pl.multiple_of(info[p] * 64, 64)
                    chunks[k, pl.ds(start, 64), cut] = part[p * 64 : (p + 1) * 64]
                chunks[k, 512:, cut] = valid[...]


def project_two(info, pooled, pieces, weights, valid):
    return pl.pallas_call(
        project_kernel,
        out_shape=(
            jax.ShapeDtypeStruct((4, 512 + EXT, 384), BF16),
            jax.ShapeDtypeStruct((512, 512), BF16),
        ),
        grid_spec=pltpu.PrefetchScalarGridSpec(
            num_scalar_prefetch=1,
            grid=(8,),
            in_specs=[
                pl.BlockSpec((512, D1), lambda s, info: (0, 0)),
                pl.BlockSpec((8, 1, 192, 512), lambda s, info: (0, s, 0, 0)),
                pl.BlockSpec((3, 512, 512), lambda s, info: (0, info[s], 0)),
                pl.BlockSpec((EXT, 128), lambda s, info: (0, 0)),
            ],
            out_specs=(
                pl.BlockSpec((4, 512 + EXT, 384), lambda s, info: (0, 0, 0)),
                pl.BlockSpec((512, 512), lambda s, info: (0, 0)),
            ),
            scratch_shapes=[pltpu.VMEM((512, 1536), F32), pltpu.VMEM((512, 128), F32)],
        ),
        compiler_params=pltpu.CompilerParams(vmem_limit_bytes=40 * 2**20),
        cost_estimate=pl.CostEstimate(
            flops=4 * 512 * 4096 * 1536, bytes_accessed=28 * 2**20, transcendentals=512
        ),
        name="project_two",
    )(info, pooled, pieces, weights, valid)


def causal_kernel(own_part, info, queries, kv_pair, start, start_stats, out, out_stats, keys, values, even, odd):
    half, core, y = info[0], info[1], info[2]
    slot = pl.program_id(0)
    own_pair = (y + slot) & 3

    @pl.when(slot == 0)
    def _():
        def prepare(block, _):
            row = lax.broadcasted_iota(jnp.int32, (512, 128), 0).astype(F32)
            lane = lax.broadcasted_iota(jnp.int32, (512, 128), 1)
            for which, kv in enumerate(kv_pair):
                count = jnp.sum(kv[block, 512 : 512 + EXT, :128].astype(F32))
                invalid = (lane == 0) & (row >= count)
                keys[which * 4 + block, :, :128] = kv[block, :512, :128]
                keys[which * 4 + block, :, 128:] = jnp.where(invalid, MASKED, 0.0).astype(BF16)
                values[which * 4 + block] = kv[block, :512, 128:].T
            return 0

        lax.fori_loop(0, 4, prepare, 0)

    lane = lax.broadcasted_iota(jnp.int32, (512, 128), 1)
    query = jnp.concatenate([queries[0], jnp.where(lane == 0, 1.0, 0.0).astype(BF16)], axis=1)

    def block_of(pair, which):
        return (which ^ core) * 4 + ((pair - y) & 3)

    def scores_of(pair, which):
        return lax.dot_general(
            keys[block_of(pair, which)], query, (((1,), (1,)), ((), ())), preferred_element_type=F32
        )

    def absorb(scores, pair, which, carry, edge):
        largest, total, sums = carry
        if edge:
            key = lax.broadcasted_iota(jnp.int32, scores.shape, 0) + which * 512
            own = lax.broadcasted_iota(jnp.int32, scores.shape, 1) + core * 512
            scores = jnp.where(key <= own, scores, MASKED)
        new_largest = jnp.maximum(largest, jnp.max(scores, axis=0, keepdims=True))
        decay = jnp.exp2(largest - new_largest)
        weights = jnp.exp2(scores - new_largest)
        total = total * decay + jnp.sum(weights, axis=0, keepdims=True)
        sums = sums * decay + dot(values[block_of(pair, which)], weights.astype(BF16))
        return new_largest, total, sums

    even[...] = scores_of(0, 0)

    def both(pair, carry, edge=False):
        odd[...] = scores_of(pair, 1)
        carry = absorb(even[...], pair, 0, carry, edge)
        if not edge:
            even[...] = scores_of((pair + 1) & 3, 0)
        return absorb(odd[...], pair, 1, carry, edge)

    if own_part:
        carry = (
            jnp.full((1, 512), MASKED, F32), jnp.zeros((1, 512), F32), jnp.zeros((128, 512), F32)
        )
        carry = lax.fori_loop(0, own_pair, both, carry)
        largest, total, sums = both(own_pair, carry, True)
        out[0] = sums
        out_stats[0] = jnp.concatenate([largest, total, jnp.zeros((6, 512), F32)], axis=0)
    else:
        carry = (start_stats[0, 0:1], start_stats[0, 1:2], start[0])
        _, total, sums = lax.fori_loop(0, half * 4, both, carry)
        out[0] = (sums / total).T.astype(BF16)


def causal_attend(own_part, info, queries, kv_pair, start=None):
    def by_slot(*shape):
        return pl.BlockSpec((1, *shape), lambda s, info: (s, 0, 0))

    sums_shape = jax.ShapeDtypeStruct((4, 128, 512), F32)
    stats_shape = jax.ShapeDtypeStruct((4, 8, 512), F32)
    whole = pl.BlockSpec((4, 512 + EXT, 256), lambda s, info: (0, 0, 0))
    in_specs = [by_slot(512, 128), whole, whole]
    operands = [queries, *kv_pair]
    if own_part:
        def kernel(info, queries, kv, other, out, out_stats, *scratch):
            causal_kernel(True, info, queries, (kv, other), None, None, out, out_stats, *scratch)

        out_shape = (sums_shape, stats_shape)
        out_specs = (by_slot(128, 512), by_slot(8, 512))
        tiles = 18
    else:
        def kernel(info, queries, kv, other, start, start_stats, out, *scratch):
            causal_kernel(False, info, queries, (kv, other), start, start_stats, out, None, *scratch)

        out_shape = jax.ShapeDtypeStruct((4, 512, 128), BF16)
        out_specs = by_slot(512, 128)
        in_specs += [by_slot(128, 512), by_slot(8, 512)]
        operands += list(start)
        tiles = 32
    return pl.pallas_call(
        kernel,
        out_shape=out_shape,
        grid_spec=pltpu.PrefetchScalarGridSpec(
            num_scalar_prefetch=1,
            grid=(4,),
            in_specs=in_specs,
            out_specs=out_specs,
            scratch_shapes=[
                pltpu.VMEM((8, 512, 256), BF16),
                pltpu.VMEM((8, 128, 512), BF16),
                pltpu.VMEM((512, 512), F32),
                pltpu.VMEM((512, 512), F32),
            ],
        ),
        compiler_params=pltpu.CompilerParams(vmem_limit_bytes=40 * 2**20),
        cost_estimate=pl.CostEstimate(
            flops=tiles * 512 * 512 * 512, bytes_accessed=4 * 2**20, transcendentals=tiles * 2**18
        ),
        name="causal_own" if own_part else "causal_first_half",
    )(info, *operands)


def turn_y(value, steps, first=0):
    return lax.ppermute(
        value, "seq", [(i, (i & 9) | ((i + 2 * steps) & 6)) for i in range(first, 16)]
    )


def flip_seq(value, bit):
    return lax.ppermute(value, "seq", [(i, i ^ bit) for i in range(16)])


def per_device(
    tokens, boundary, heads_in, heads_out, gate_up, down_weight, widen, heads_in_two, heads_out_two
):
    seq_position = lax.axis_index("seq")
    me = lax.axis_index("blk")
    rows = tokens.shape[0]
    capacity = 512
    width = D1 // 8
    block_of = jnp.stack([((me ^ (4 * x)) & 4) | ((me + z) & 3) for x, z in PLACES])
    numbers = jnp.arange(8, dtype=jnp.int32)
    place_of = jnp.sum(
        jnp.where(block_of[None, :] == numbers[:, None], numbers[None, :], 0), axis=1
    )

    heads_in_flat = heads_in.transpose(1, 2, 0).reshape(3 * width, D1)
    core, y, half = seq_position & 1, (seq_position >> 1) & 3, seq_position >> 3
    piece = lax.dynamic_slice(widen, (seq_position * 96, 0), (96, 512))

    near, far = gather_blk(prepare(tokens, boundary[None, :]))
    arrived = near[2 * SENT :]
    gates = later(gate_up, arrived)
    gate_flat, up_flat = lax.optimization_barrier((gates[:, 0, :], gates[:, 1, :]))
    marks = jnp.concatenate(
        [part.reshape(4, SENT, D1)[:, rows, :rows] for part in (near, far)], axis=0
    )
    info = later(jnp.concatenate([place_of, seq_position[None]]).astype(jnp.int32), gate_flat)
    piece_across = flip_seq(piece, 8)
    info = later(info, piece_across)
    qkv_near = project_one(near, heads_in_flat)
    qkv, edge = project_one(far, heads_in_flat, info, qkv_near)
    halo = lax.ppermute(edge, "seq", [(i, i + 1) for i in range(15)])
    attended = window_attend(info, qkv, halo, window_attend(info, qkv))
    attn_near = dot(attended[: 4 * rows], heads_out).astype(BF16)
    attn_far = dot(attended[4 * rows :], heads_out).astype(BF16)
    opposite, diagonal = reduce_first(attn_far)

    piece = later(jnp.concatenate([piece, piece_across], axis=0), qkv_near)
    pieces = jnp.concatenate(gather_blk(piece, attended), axis=0)
    pieces = later(later(pieces, opposite), diagonal)
    pieces = lax.all_gather(
        pieces, "seq", axis=0, axis_index_groups=[[h * 8 + k for k in range(8)] for h in range(2)]
    ).reshape(8, 8, 192, 512)
    mid_stream = (
        tokens.astype(F32) + reduce_second(attn_near, opposite, diagonal)
    ).astype(BF16)

    normed_mid = normalize(mid_stream).astype(BF16)

    near, far = gather_blk(normed_mid)
    mlp_near = mlp(near, gate_flat, up_flat, down_weight)
    mlp_far = mlp(far, gate_flat, up_flat, down_weight)
    marks = marks.astype(F32)
    counts = jnp.sum(marks, axis=1)
    before = jnp.sum(
        jnp.where(block_of[None, :] < block_of[:, None], counts[None, :], 0.0), axis=1
    )
    steps = jnp.arange(rows)
    running = dot(marks.astype(BF16), (steps[:, None] <= steps[None, :]).astype(BF16))
    slots = jnp.where(marks > 0.5, before[:, None] + running - 1.0, -1.0).astype(jnp.int32)
    span_count = jnp.sum(counts).astype(jnp.int32)
    targets = (block_of[:, None] * 64 + jnp.arange(64)[None, :]).reshape(capacity, 1)
    selector = (slots.reshape(1, 8 * rows) == targets).astype(BF16)
    placed = (
        dot(selector[:, : 4 * rows], mlp_near)
        + dot(selector[:, 4 * rows :], mlp_far)
        + dot(selector[:, :rows], mid_stream)
    ).astype(BF16)
    pooled_own = reduce_blk(placed[:256], placed[256:]).astype(BF16)
    pooled_own = jnp.concatenate(
        [
            lax.dynamic_slice(
                pooled_own, (0, 96 * ((half ^ h) * 8 + k)), (64, 96)
            )
            for k in range(8)
            for h in range(2)
        ],
        axis=1,
    )
    pooled = jnp.concatenate(gather_blk(pooled_own), axis=0)

    validity = (jnp.arange(capacity, dtype=jnp.int32) < span_count).astype(F32)
    valid_rows = jnp.pad(
        validity.reshape(4, 128).astype(BF16), ((0, EXT - 4), (0, 0))
    )
    info_one = jnp.concatenate([block_of, y[None]]).astype(jnp.int32)
    chunks, wide_cols = project_two(
        info_one, pooled, pieces, heads_in_two.transpose(1, 0, 2), valid_rows
    )
    from_behind = turn_y(chunks[1], 1)
    from_ahead = turn_y(chunks[3], 3)
    from_opposite = turn_y(chunks[2], 2)
    across = [(i, i + 8) for i in range(8)]
    first_own = lax.ppermute(chunks[:1, :, 128:], "seq", across)
    mine = jnp.stack([chunks[0], from_ahead, from_opposite, from_behind])
    queries, own_kv = mine[:, :capacity, :128], mine[:, :, 128:]
    first_rest = lax.ppermute(own_kv[1:], "seq", across)
    info_two = jnp.stack([half, core, y]).astype(jnp.int32)
    running = causal_attend(
        True, later(info_two, first_own[0]), queries, (own_kv, flip_seq(own_kv, 1))
    )
    first_kv = jnp.concatenate([first_own, first_rest], axis=0)
    first_kv = first_kv + running[1][0, 2, 0].astype(BF16)
    opposite, diagonal = reduce_first(later(mlp_far, running[1][0, 2:3]))
    level_one = mid_stream.astype(F32) + reduce_second(mlp_near, opposite, diagonal)
    mixed = causal_attend(False, info_two, queries, (first_kv, flip_seq(first_kv, 1)), running)
    back = [mixed[0], turn_y(mixed[3], 3), turn_y(mixed[2], 2), turn_y(mixed[1], 1)]
    heads = jnp.concatenate([back[0], back[1], back[2], back[3]] * 2, axis=1)
    attended_two = lax.dynamic_slice(heads, (0, ((4 - y) & 3) * 128), (capacity, 512))

    level_one = later(level_one, mixed[0]).astype(BF16)
    column_of = later(block_of, level_one)

    def columns(place):
        part = lax.dynamic_slice(heads_out_two, (0, column_of[place] * 512), (512, 512))
        return dot(attended_two, part).astype(BF16)

    out_far = jnp.concatenate([columns(place) for place in range(4, 8)], axis=0)
    out_near = jnp.concatenate([columns(place) for place in range(4)], axis=0)
    out_near = lax.optimization_barrier(out_near)
    level_two = (
        (wide_cols.astype(F32) + reduce_blk(out_near, out_far)) * validity[:, None]
    ).astype(BF16)
    return (level_one, level_two)


def solution(mesh):
    placed = (
        P(("seq", "blk"), None),
        P(("seq", "blk")),
        P(None, None, "blk"),
        P("blk", None),
        P(None, None, "blk"),
        P("blk", None),
        P(None, "blk"),
        P(None, None, "blk"),
        P("blk", None),
    )
    return jax.shard_map(
        per_device,
        mesh=mesh,
        in_specs=placed,
        out_specs=(P(("seq", "blk"), None), P("seq", "blk")),
        check_vma=False,
    )
```

```python
import jax
import jax.numpy as jnp
from jax import lax
from jax.experimental import pallas as pl
from jax.experimental.pallas import tpu as pltpu
from jax.sharding import PartitionSpec as P

D1 = 1536
H1 = 24
D2 = 4096
H2 = 32
WIN = 512
EXT = 16
SENT = 128 + EXT
BF16 = jnp.bfloat16
F32 = jnp.float32
MASKED = -1e30
SCORE_FACTOR = 128 ** (-0.5) * 1.4426950408889634

PLACES = ((0, 0), (1, 0), (0, 1), (0, 3), (0, 2), (1, 2), (1, 1), (1, 3))


def flip_x(value):
    return lax.ppermute(value, "blk", [(i, i ^ 4) for i in range(8)])


def turn_z(value, steps):
    return lax.ppermute(value, "blk", [(i, (i & 4) | ((i + steps) & 3)) for i in range(8)])


def later(array, value):
    return array + (value[0, 0].astype(F32) * 0.0).astype(array.dtype)


def gather_blk(own, between=None):
    across = flip_x(own)
    behind = turn_z(own, 1)
    ahead = turn_z(own, 3)
    first = jnp.concatenate([own, across], axis=0)
    second = jnp.concatenate([ahead, behind], axis=0)
    if between is not None:
        first, second = later(first, between), later(second, between)
    opposite = turn_z(first, 2)
    diagonal = flip_x(second)
    near = jnp.concatenate([first, second], axis=0)
    far = jnp.concatenate([opposite, diagonal], axis=0)
    return near, far


def reduce_first(far):
    count = far.shape[0] // 4
    return turn_z(far[: 2 * count], 2), flip_x(far[2 * count :])


def reduce_second(near, opposite, diagonal):
    count = near.shape[0] // 4

    def plus(block, other):
        return near[block * count : (block + 1) * count].astype(F32) + other.astype(F32)

    across = flip_x(plus(1, opposite[count:]).astype(BF16))
    behind = turn_z(plus(2, diagonal[:count]).astype(BF16), 1)
    ahead = turn_z(plus(3, diagonal[count:]).astype(BF16), 3)
    return (
        plus(0, opposite[:count])
        + across.astype(F32)
        + behind.astype(F32)
        + ahead.astype(F32)
    )


def reduce_blk(near, far):
    return reduce_second(near, *reduce_first(far))


def normalize(values):
    floats = values.astype(F32)
    return floats * lax.rsqrt(jnp.mean(floats * floats, axis=-1, keepdims=True) + 1e-06)


def dot(left, right):
    return jnp.dot(left, right, preferred_element_type=F32)


def dot_t(left, right):
    return lax.dot_general(left, right, (((1,), (1,)), ((), ())), preferred_element_type=F32)


def window_kernel(blocks, info, qkv, halo, before, out):
    rows, width, size, stride = 128, D1 // 8, D1 // H1, SENT
    key_count = WIN + rows
    i = lax.broadcasted_iota(jnp.int32, (rows, key_count), 0)
    j = lax.broadcasted_iota(jnp.int32, (rows, key_count), 1)
    band = (j > i) & (j <= i + WIN)
    seq_position = info[8]
    if before is not None:
        out[...] = before[...]
    for n in blocks:
        place = info[n]
        keys, values = [], []
        for k in range(n - 4, n + 1):
            if k >= 0:
                start = pl.multiple_of(info[k] * stride, 16)
                block = qkv[pl.ds(start, rows), :]
                keys.append(block[:, :width])
                values.append(block[:, width : 2 * width])
            else:
                block = halo[(k + 4) * rows : (k + 5) * rows, :]
                keys.append(block[:, :width])
                values.append(block[:, width:])
        keys = jnp.concatenate(keys, axis=0)
        values = jnp.concatenate(values, axis=0)
        queries = qkv[pl.ds(pl.multiple_of(place * stride, 16), rows), 2 * width :]
        allowed = band
        if n < 4:
            allowed = band & (j + ((n - 4) * rows + seq_position * 1024) >= 0)
        parts = []
        for h in range(width // size):
            cut = slice(h * size, (h + 1) * size)
            scores = lax.dot_general(
                queries[:, cut], keys[:, cut], (((1,), (1,)), ((), ())),
                preferred_element_type=F32,
            ) * size ** (-0.5)
            scores = jnp.where(allowed, scores, MASKED)
            largest = jnp.max(scores, axis=-1, keepdims=True)
            weights = jnp.exp(scores - largest)
            total = jnp.sum(weights, axis=-1, keepdims=True)
            parts.append(dot(weights.astype(BF16), values[:, cut]) / total)
        out[pl.ds(pl.multiple_of(place * rows, 16), rows), :] = jnp.concatenate(
            parts, axis=1
        ).astype(BF16)


def window_attend(info, qkv, halo=None, before=None):
    if halo is None:
        def kernel(info, qkv, out):
            window_kernel(range(4, 8), info, qkv, None, None, out)

        operands = (info, qkv)
    else:
        def kernel(info, qkv, halo, before, out):
            window_kernel(range(4), info, qkv, halo, before, out)

        operands = (info, qkv, halo, before)
    vmem = pl.BlockSpec(memory_space=pltpu.VMEM)
    return pl.pallas_call(
        kernel,
        out_shape=jax.ShapeDtypeStruct((1024, D1 // 8), BF16),
        in_specs=[pl.BlockSpec(memory_space=pltpu.SMEM)] + [vmem] * (len(operands) - 1),
        out_specs=vmem,
        compiler_params=pltpu.CompilerParams(vmem_limit_bytes=32 * 2**20),
        cost_estimate=pl.CostEstimate(
            flops=12 * 128 * 640 * 256, bytes_accessed=2 * 2**20, transcendentals=12 * 128 * 640
        ),
        name="window_late" if halo is None else "window_early",
    )(*operands)


def prepare_kernel(tokens, marks, out):
    floats = tokens[...].astype(F32)
    scale = lax.rsqrt(jnp.mean(floats * floats, axis=-1, keepdims=True) + 1e-06)
    out[:128, :] = (floats * scale).astype(BF16)
    out[128:, :] = jnp.zeros((EXT, D1), BF16)
    out[128:, :128] = jnp.broadcast_to(marks[...].astype(F32), (EXT, 128)).astype(BF16)


def prepare(tokens, marks):
    return pl.pallas_call(
        prepare_kernel,
        out_shape=jax.ShapeDtypeStruct((SENT, D1), BF16),
        in_specs=[pl.BlockSpec(memory_space=pltpu.VMEM)] * 2,
        out_specs=pl.BlockSpec(memory_space=pltpu.VMEM),
        name="prepare",
    )(tokens, marks)


def near_kernel(rows, weights, out):
    out[:, :384] = dot_t(rows[...], weights[192:, :]).astype(BF16)
    out[:, 384:] = dot_t(rows[...], weights[:192, :]).astype(BF16)


def far_kernel(info, near, rows, weights, out, edge):
    half = 4 * SENT
    out[:half, :] = near[...]
    out[half:, :384] = dot_t(rows[...], weights[192:, :]).astype(BF16)
    for k in range(4):
        start = pl.multiple_of(info[4 + k] * SENT, 16)
        edge[k * 128 : (k + 1) * 128, :] = out[pl.ds(start, 128), :384]
    out[half:, 384:] = dot_t(rows[...], weights[:192, :]).astype(BF16)


def project_one(rows, weights, info=None, near=None):
    vmem = pl.BlockSpec(memory_space=pltpu.VMEM)
    cost = pl.CostEstimate(flops=2 * 576 * 576 * D1, bytes_accessed=5 * 2**20, transcendentals=0)
    params = pltpu.CompilerParams(vmem_limit_bytes=24 * 2**20)
    if near is None:
        return pl.pallas_call(
            near_kernel,
            out_shape=jax.ShapeDtypeStruct((4 * SENT, 576), BF16),
            in_specs=[vmem] * 2,
            out_specs=vmem,
            compiler_params=params,
            cost_estimate=cost,
            name="project_near",
        )(rows, weights)
    return pl.pallas_call(
        far_kernel,
        out_shape=(
            jax.ShapeDtypeStruct((8 * SENT, 576), BF16), jax.ShapeDtypeStruct((WIN, 384), BF16)
        ),
        in_specs=[pl.BlockSpec(memory_space=pltpu.SMEM)] + [vmem] * 3,
        out_specs=(vmem, vmem),
        compiler_params=params,
        cost_estimate=cost,
        name="project_far",
    )(info, near, rows, weights)


def mlp_kernel(rows, gate, up, down, out):
    def some(step, _):
        cut = pl.ds(pl.multiple_of(step * 256, 256), 256)
        block = rows[cut, :]
        gated = dot(block, gate[...])
        hidden = gated / (1.0 + jnp.exp(-gated)) * dot(block, up[...])
        out[cut, :] = dot(hidden.astype(BF16), down[...]).astype(BF16)
        return 0

    lax.fori_loop(0, rows.shape[0] // 256, some, 0)


def mlp(rows, gate, up, down):
    return pl.pallas_call(
        mlp_kernel,
        out_shape=jax.ShapeDtypeStruct(rows.shape, BF16),
        in_specs=[pl.BlockSpec(memory_space=pltpu.VMEM)] * 4,
        out_specs=pl.BlockSpec(memory_space=pltpu.VMEM),
        compiler_params=pltpu.CompilerParams(vmem_limit_bytes=32 * 2**20),
        cost_estimate=pl.CostEstimate(
            flops=2 * 512 * 1536 * 1536, bytes_accessed=8 * 2**20, transcendentals=512 * 512
        ),
        name="mlp",
    )(rows, gate, up, down)


def project_kernel(info, pooled, pieces, weights, valid, chunks, wide_own, total, squares):
    step = pl.program_id(0)
    y = info[8]

    @pl.when(step == 0)
    def _():
        total[...] = jnp.zeros_like(total)
        squares[...] = jnp.zeros_like(squares)

    wide = dot(pooled[...], pieces[...].reshape(D1, 512)).astype(BF16)
    floats = wide.astype(F32)
    squares[...] += jnp.broadcast_to(
        jnp.sum(floats * floats, axis=-1, keepdims=True), squares.shape
    )
    for i in range(3):
        total[:, i * 512 : (i + 1) * 512] += dot(wide, weights[i])

    @pl.when(step == 0)
    def _():
        for p in range(8):
            start = pl.multiple_of(info[p] * 64, 64)
            wide_own[pl.ds(start, 64), :] = wide[p * 64 : (p + 1) * 64]

    @pl.when(step == 7)
    def _():
        scale = lax.rsqrt(squares[...] / D2 + 1e-06)
        for k in range(4):
            head = (y + k) & 3
            for i in range(3):
                cut = slice(i * 128, (i + 1) * 128)
                lanes = pl.ds(pl.multiple_of(i * 512 + head * 128, 128), 128)
                part = total[:, lanes] * (scale * SCORE_FACTOR if i == 0 else scale)
                part = part.astype(BF16)
                for p in range(8):
                    start = pl.multiple_of(info[p] * 64, 64)
                    chunks[k, pl.ds(start, 64), cut] = part[p * 64 : (p + 1) * 64]
                chunks[k, 512:, cut] = valid[...]


def project_two(info, pooled, pieces, weights, valid):
    return pl.pallas_call(
        project_kernel,
        out_shape=(
            jax.ShapeDtypeStruct((4, 512 + EXT, 384), BF16),
            jax.ShapeDtypeStruct((512, 512), BF16),
        ),
        grid_spec=pltpu.PrefetchScalarGridSpec(
            num_scalar_prefetch=1,
            grid=(8,),
            in_specs=[
                pl.BlockSpec((512, D1), lambda s, info: (0, 0)),
                pl.BlockSpec((8, 1, 192, 512), lambda s, info: (0, s, 0, 0)),
                pl.BlockSpec((3, 512, 512), lambda s, info: (0, info[s], 0)),
                pl.BlockSpec((EXT, 128), lambda s, info: (0, 0)),
            ],
            out_specs=(
                pl.BlockSpec((4, 512 + EXT, 384), lambda s, info: (0, 0, 0)),
                pl.BlockSpec((512, 512), lambda s, info: (0, 0)),
            ),
            scratch_shapes=[pltpu.VMEM((512, 1536), F32), pltpu.VMEM((512, 128), F32)],
        ),
        compiler_params=pltpu.CompilerParams(vmem_limit_bytes=40 * 2**20),
        cost_estimate=pl.CostEstimate(
            flops=4 * 512 * 4096 * 1536, bytes_accessed=28 * 2**20, transcendentals=512
        ),
        name="project_two",
    )(info, pooled, pieces, weights, valid)


def causal_kernel(own_part, info, queries, kv_pair, start, start_stats, out, out_stats, keys, values, even, odd):
    half, core, y = info[0], info[1], info[2]
    slot = pl.program_id(0)
    own_pair = (y + slot) & 3

    @pl.when(slot == 0)
    def _():
        def prepare(block, _):
            row = lax.broadcasted_iota(jnp.int32, (512, 128), 0).astype(F32)
            lane = lax.broadcasted_iota(jnp.int32, (512, 128), 1)
            for which, kv in enumerate(kv_pair):
                count = jnp.sum(kv[block, 512 : 512 + EXT, :128].astype(F32))
                invalid = (lane == 0) & (row >= count)
                keys[which * 4 + block, :, :128] = kv[block, :512, :128]
                keys[which * 4 + block, :, 128:] = jnp.where(invalid, MASKED, 0.0).astype(BF16)
                values[which * 4 + block] = kv[block, :512, 128:].T
            return 0

        lax.fori_loop(0, 4, prepare, 0)

    lane = lax.broadcasted_iota(jnp.int32, (512, 128), 1)
    query = jnp.concatenate([queries[0], jnp.where(lane == 0, 1.0, 0.0).astype(BF16)], axis=1)

    def block_of(pair, which):
        return (which ^ core) * 4 + ((pair - y) & 3)

    def scores_of(pair, which):
        return lax.dot_general(
            keys[block_of(pair, which)], query, (((1,), (1,)), ((), ())), preferred_element_type=F32
        )

    def absorb(scores, pair, which, carry, edge):
        largest, total, sums = carry
        if edge:
            key = lax.broadcasted_iota(jnp.int32, scores.shape, 0) + which * 512
            own = lax.broadcasted_iota(jnp.int32, scores.shape, 1) + core * 512
            scores = jnp.where(key <= own, scores, MASKED)
        new_largest = jnp.maximum(largest, jnp.max(scores, axis=0, keepdims=True))
        decay = jnp.exp2(largest - new_largest)
        weights = jnp.exp2(scores - new_largest)
        total = total * decay + jnp.sum(weights, axis=0, keepdims=True)
        sums = sums * decay + dot(values[block_of(pair, which)], weights.astype(BF16))
        return new_largest, total, sums

    even[...] = scores_of(0, 0)

    def both(pair, carry, edge=False):
        odd[...] = scores_of(pair, 1)
        carry = absorb(even[...], pair, 0, carry, edge)
        if not edge:
            even[...] = scores_of((pair + 1) & 3, 0)
        return absorb(odd[...], pair, 1, carry, edge)

    if own_part:
        carry = (
            jnp.full((1, 512), MASKED, F32), jnp.zeros((1, 512), F32), jnp.zeros((128, 512), F32)
        )
        carry = lax.fori_loop(0, own_pair, both, carry)
        largest, total, sums = both(own_pair, carry, True)
        out[0] = sums
        out_stats[0] = jnp.concatenate([largest, total, jnp.zeros((6, 512), F32)], axis=0)
    else:
        carry = (start_stats[0, 0:1], start_stats[0, 1:2], start[0])
        _, total, sums = lax.fori_loop(0, half * 4, both, carry)
        out[0] = (sums / total).T.astype(BF16)


def causal_attend(own_part, info, queries, kv_pair, start=None):
    def by_slot(*shape):
        return pl.BlockSpec((1, *shape), lambda s, info: (s, 0, 0))

    sums_shape = jax.ShapeDtypeStruct((4, 128, 512), F32)
    stats_shape = jax.ShapeDtypeStruct((4, 8, 512), F32)
    whole = pl.BlockSpec((4, 512 + EXT, 256), lambda s, info: (0, 0, 0))
    in_specs = [by_slot(512, 128), whole, whole]
    operands = [queries, *kv_pair]
    if own_part:
        def kernel(info, queries, kv, other, out, out_stats, *scratch):
            causal_kernel(True, info, queries, (kv, other), None, None, out, out_stats, *scratch)

        out_shape = (sums_shape, stats_shape)
        out_specs = (by_slot(128, 512), by_slot(8, 512))
        tiles = 18
    else:
        def kernel(info, queries, kv, other, start, start_stats, out, *scratch):
            causal_kernel(False, info, queries, (kv, other), start, start_stats, out, None, *scratch)

        out_shape = jax.ShapeDtypeStruct((4, 512, 128), BF16)
        out_specs = by_slot(512, 128)
        in_specs += [by_slot(128, 512), by_slot(8, 512)]
        operands += list(start)
        tiles = 32
    return pl.pallas_call(
        kernel,
        out_shape=out_shape,
        grid_spec=pltpu.PrefetchScalarGridSpec(
            num_scalar_prefetch=1,
            grid=(4,),
            in_specs=in_specs,
            out_specs=out_specs,
            scratch_shapes=[
                pltpu.VMEM((8, 512, 256), BF16),
                pltpu.VMEM((8, 128, 512), BF16),
                pltpu.VMEM((512, 512), F32),
                pltpu.VMEM((512, 512), F32),
            ],
        ),
        compiler_params=pltpu.CompilerParams(vmem_limit_bytes=40 * 2**20),
        cost_estimate=pl.CostEstimate(
            flops=tiles * 512 * 512 * 512, bytes_accessed=4 * 2**20, transcendentals=tiles * 2**18
        ),
        name="causal_own" if own_part else "causal_first_half",
    )(info, *operands)


def turn_y(value, steps, first=0):
    return lax.ppermute(
        value, "seq", [(i, (i & 9) | ((i + 2 * steps) & 6)) for i in range(first, 16)]
    )


def flip_seq(value, bit):
    return lax.ppermute(value, "seq", [(i, i ^ bit) for i in range(16)])


def per_device(
    tokens, boundary, heads_in, heads_out, gate_up, down_weight, widen, heads_in_two, heads_out_two
):
    seq_position = lax.axis_index("seq")
    me = lax.axis_index("blk")
    rows = tokens.shape[0]
    capacity = 512
    width = D1 // 8
    block_of = jnp.stack([((me ^ (4 * x)) & 4) | ((me + z) & 3) for x, z in PLACES])
    numbers = jnp.arange(8, dtype=jnp.int32)
    place_of = jnp.sum(
        jnp.where(block_of[None, :] == numbers[:, None], numbers[None, :], 0), axis=1
    )

    heads_in_flat = heads_in.transpose(1, 2, 0).reshape(3 * width, D1)
    core, y, half = seq_position & 1, (seq_position >> 1) & 3, seq_position >> 3
    piece = lax.dynamic_slice(widen, (seq_position * 96, 0), (96, 512))

    near, far = gather_blk(prepare(tokens, boundary[None, :]))
    arrived = near[2 * SENT :]
    piece_across = flip_seq(piece, 8)
    gates = later(gate_up, arrived)
    gate_flat, up_flat = lax.optimization_barrier((gates[:, 0, :], gates[:, 1, :]))
    marks = jnp.concatenate(
        [part.reshape(4, SENT, D1)[:, rows, :rows] for part in (near, far)], axis=0
    )
    info = later(jnp.concatenate([place_of, seq_position[None]]).astype(jnp.int32), gate_flat)
    qkv_near = project_one(near, heads_in_flat)
    qkv, edge = project_one(far, heads_in_flat, info, qkv_near)
    halo = lax.ppermute(edge, "seq", [(i, i + 1) for i in range(15)])
    attended = window_attend(info, qkv, halo, window_attend(info, qkv))
    attn_near = dot(attended[: 4 * rows], heads_out).astype(BF16)
    attn_far = dot(attended[4 * rows :], heads_out).astype(BF16)
    opposite, diagonal = reduce_first(attn_far)

    piece = later(jnp.concatenate([piece, piece_across], axis=0), qkv)
    pieces = jnp.concatenate(gather_blk(piece, halo), axis=0)
    pieces = later(later(pieces, opposite), diagonal)
    pieces = lax.all_gather(
        pieces, "seq", axis=0, axis_index_groups=[[h * 8 + k for k in range(8)] for h in range(2)]
    ).reshape(8, 8, 192, 512)
    mid_stream = (
        tokens.astype(F32) + reduce_second(attn_near, opposite, diagonal)
    ).astype(BF16)

    normed_mid = normalize(mid_stream).astype(BF16)

    near, far = gather_blk(normed_mid)
    mlp_near = mlp(near, gate_flat, up_flat, down_weight)
    mlp_far = mlp(far, gate_flat, up_flat, down_weight)
    marks = marks.astype(F32)
    counts = jnp.sum(marks, axis=1)
    before = jnp.sum(
        jnp.where(block_of[None, :] < block_of[:, None], counts[None, :], 0.0), axis=1
    )
    steps = jnp.arange(rows)
    running = dot(marks.astype(BF16), (steps[:, None] <= steps[None, :]).astype(BF16))
    slots = jnp.where(marks > 0.5, before[:, None] + running - 1.0, -1.0).astype(jnp.int32)
    span_count = jnp.sum(counts).astype(jnp.int32)
    targets = (block_of[:, None] * 64 + jnp.arange(64)[None, :]).reshape(capacity, 1)
    selector = (slots.reshape(1, 8 * rows) == targets).astype(BF16)
    placed = (
        dot(selector[:, : 4 * rows], mlp_near)
        + dot(selector[:, 4 * rows :], mlp_far)
        + dot(selector[:, :rows], mid_stream)
    ).astype(BF16)
    pooled_own = reduce_blk(placed[:256], placed[256:]).astype(BF16)
    pooled_own = jnp.concatenate(
        [
            lax.dynamic_slice(
                pooled_own, (0, 96 * ((half ^ h) * 8 + k)), (64, 96)
            )
            for k in range(8)
            for h in range(2)
        ],
        axis=1,
    )
    pooled = jnp.concatenate(gather_blk(pooled_own), axis=0)

    validity = (jnp.arange(capacity, dtype=jnp.int32) < span_count).astype(F32)
    valid_rows = jnp.pad(
        validity.reshape(4, 128).astype(BF16), ((0, EXT - 4), (0, 0))
    )
    info_one = jnp.concatenate([block_of, y[None]]).astype(jnp.int32)
    chunks, wide_cols = project_two(
        info_one, pooled, pieces, heads_in_two.transpose(1, 0, 2), valid_rows
    )
    opposite, diagonal = reduce_first(later(mlp_far, chunks[0]))
    from_behind = turn_y(chunks[1], 1)
    from_ahead = turn_y(chunks[3], 3)
    from_opposite = turn_y(chunks[2], 2)
    mine = jnp.stack([chunks[0], from_ahead, from_opposite, from_behind])
    queries, own_kv = mine[:, :capacity, :128], mine[:, :, 128:]
    first_kv = lax.ppermute(own_kv, "seq", [(i, i + 8) for i in range(8)])
    info_two = jnp.stack([half, core, y]).astype(jnp.int32)
    running = causal_attend(True, info_two, queries, (own_kv, flip_seq(own_kv, 1)))
    first_kv = first_kv + running[1][0, 2, 0].astype(BF16)
    level_one = mid_stream.astype(F32) + reduce_second(
        later(mlp_near, running[1][0, 2:3]), opposite, diagonal
    )
    mixed = causal_attend(False, info_two, queries, (first_kv, flip_seq(first_kv, 1)), running)
    back = [mixed[0], turn_y(mixed[3], 3), turn_y(mixed[2], 2), turn_y(mixed[1], 1)]
    heads = jnp.concatenate([back[0], back[1], back[2], back[3]] * 2, axis=1)
    attended_two = lax.dynamic_slice(heads, (0, ((4 - y) & 3) * 128), (capacity, 512))


    level_one = later(level_one, mixed[0]).astype(BF16)
    column_of = later(block_of, level_one)

    def columns(place):
        part = lax.dynamic_slice(heads_out_two, (0, column_of[place] * 512), (512, 512))
        return dot(attended_two, part).astype(BF16)

    out_far = jnp.concatenate([columns(place) for place in range(4, 8)], axis=0)
    out_near = jnp.concatenate([columns(place) for place in range(4)], axis=0)
    out_near = lax.optimization_barrier(out_near)
    level_two = (
        (wide_cols.astype(F32) + reduce_blk(out_near, out_far)) * validity[:, None]
    ).astype(BF16)
    return (level_one, level_two)


def solution(mesh):
    placed = (
        P(("seq", "blk"), None),
        P(("seq", "blk")),
        P(None, None, "blk"),
        P("blk", None),
        P(None, None, "blk"),
        P("blk", None),
        P(None, "blk"),
        P(None, None, "blk"),
        P("blk", None),
    )
    return jax.shard_map(
        per_device,
        mesh=mesh,
        in_specs=placed,
        out_specs=(P(("seq", "blk"), None), P("seq", "blk")),
        check_vma=False,
    )
```

```python
import jax
import jax.numpy as jnp
from jax import lax
from jax.experimental import pallas as pl
from jax.experimental.pallas import tpu as pltpu
from jax.sharding import PartitionSpec as P

D1 = 1536
H1 = 24
D2 = 4096
H2 = 32
WIN = 512
EXT = 16
SENT = 128 + EXT
BF16 = jnp.bfloat16
F32 = jnp.float32
MASKED = -1e30
SCORE_FACTOR = 128 ** (-0.5) * 1.4426950408889634

PLACES = ((0, 0), (1, 0), (0, 1), (0, 3), (0, 2), (1, 2), (1, 1), (1, 3))


def flip_x(value):
    return lax.ppermute(value, "blk", [(i, i ^ 4) for i in range(8)])


def turn_z(value, steps):
    return lax.ppermute(value, "blk", [(i, (i & 4) | ((i + steps) & 3)) for i in range(8)])


def later(array, value):
    return array + (value[0, 0].astype(F32) * 0.0).astype(array.dtype)


def gather_blk(own, between=None):
    across = flip_x(own)
    behind = turn_z(own, 1)
    ahead = turn_z(own, 3)
    first = jnp.concatenate([own, across], axis=0)
    second = jnp.concatenate([ahead, behind], axis=0)
    if between is not None:
        first, second = later(first, between), later(second, between)
    opposite = turn_z(first, 2)
    diagonal = flip_x(second)
    near = jnp.concatenate([first, second], axis=0)
    far = jnp.concatenate([opposite, diagonal], axis=0)
    return near, far


def reduce_first(far):
    count = far.shape[0] // 4
    return turn_z(far[: 2 * count], 2), flip_x(far[2 * count :])


def reduce_second(near, opposite, diagonal):
    count = near.shape[0] // 4

    def plus(block, other):
        return near[block * count : (block + 1) * count].astype(F32) + other.astype(F32)

    across = flip_x(plus(1, opposite[count:]).astype(BF16))
    behind = turn_z(plus(2, diagonal[:count]).astype(BF16), 1)
    ahead = turn_z(plus(3, diagonal[count:]).astype(BF16), 3)
    return (
        plus(0, opposite[:count])
        + across.astype(F32)
        + behind.astype(F32)
        + ahead.astype(F32)
    )


def reduce_blk(near, far):
    return reduce_second(near, *reduce_first(far))


def normalize(values):
    floats = values.astype(F32)
    return floats * lax.rsqrt(jnp.mean(floats * floats, axis=-1, keepdims=True) + 1e-06)


def dot(left, right):
    return jnp.dot(left, right, preferred_element_type=F32)


def dot_t(left, right):
    return lax.dot_general(left, right, (((1,), (1,)), ((), ())), preferred_element_type=F32)


def window_kernel(blocks, info, qkv, halo, before, out):
    rows, width, size, stride = 128, D1 // 8, D1 // H1, SENT
    key_count = WIN + rows
    i = lax.broadcasted_iota(jnp.int32, (rows, key_count), 0)
    j = lax.broadcasted_iota(jnp.int32, (rows, key_count), 1)
    band = (j > i) & (j <= i + WIN)
    seq_position = info[8]
    if before is not None:
        out[...] = before[...]
    for n in blocks:
        place = info[n]
        keys, values = [], []
        for k in range(n - 4, n + 1):
            if k >= 0:
                start = pl.multiple_of(info[k] * stride, 16)
                block = qkv[pl.ds(start, rows), :]
                keys.append(block[:, :width])
                values.append(block[:, width : 2 * width])
            else:
                block = halo[(k + 4) * rows : (k + 5) * rows, :]
                keys.append(block[:, :width])
                values.append(block[:, width:])
        keys = jnp.concatenate(keys, axis=0)
        values = jnp.concatenate(values, axis=0)
        queries = qkv[pl.ds(pl.multiple_of(place * stride, 16), rows), 2 * width :]
        allowed = band
        if n < 4:
            allowed = band & (j + ((n - 4) * rows + seq_position * 1024) >= 0)
        parts = []
        for h in range(width // size):
            cut = slice(h * size, (h + 1) * size)
            scores = lax.dot_general(
                queries[:, cut], keys[:, cut], (((1,), (1,)), ((), ())),
                preferred_element_type=F32,
            ) * size ** (-0.5)
            scores = jnp.where(allowed, scores, MASKED)
            largest = jnp.max(scores, axis=-1, keepdims=True)
            weights = jnp.exp(scores - largest)
            total = jnp.sum(weights, axis=-1, keepdims=True)
            parts.append(dot(weights.astype(BF16), values[:, cut]) / total)
        out[pl.ds(pl.multiple_of(place * rows, 16), rows), :] = jnp.concatenate(
            parts, axis=1
        ).astype(BF16)


def window_attend(info, qkv, halo=None, before=None):
    if halo is None:
        def kernel(info, qkv, out):
            window_kernel(range(4, 8), info, qkv, None, None, out)

        operands = (info, qkv)
    else:
        def kernel(info, qkv, halo, before, out):
            window_kernel(range(4), info, qkv, halo, before, out)

        operands = (info, qkv, halo, before)
    vmem = pl.BlockSpec(memory_space=pltpu.VMEM)
    return pl.pallas_call(
        kernel,
        out_shape=jax.ShapeDtypeStruct((1024, D1 // 8), BF16),
        in_specs=[pl.BlockSpec(memory_space=pltpu.SMEM)] + [vmem] * (len(operands) - 1),
        out_specs=vmem,
        compiler_params=pltpu.CompilerParams(vmem_limit_bytes=32 * 2**20),
        cost_estimate=pl.CostEstimate(
            flops=12 * 128 * 640 * 256, bytes_accessed=2 * 2**20, transcendentals=12 * 128 * 640
        ),
        name="window_late" if halo is None else "window_early",
    )(*operands)


def prepare_kernel(tokens, marks, out):
    floats = tokens[...].astype(F32)
    scale = lax.rsqrt(jnp.mean(floats * floats, axis=-1, keepdims=True) + 1e-06)
    out[:128, :] = (floats * scale).astype(BF16)
    out[128:, :] = jnp.zeros((EXT, D1), BF16)
    out[128:, :128] = jnp.broadcast_to(marks[...].astype(F32), (EXT, 128)).astype(BF16)


def prepare(tokens, marks):
    return pl.pallas_call(
        prepare_kernel,
        out_shape=jax.ShapeDtypeStruct((SENT, D1), BF16),
        in_specs=[pl.BlockSpec(memory_space=pltpu.VMEM)] * 2,
        out_specs=pl.BlockSpec(memory_space=pltpu.VMEM),
        name="prepare",
    )(tokens, marks)


def near_kernel(rows, weights, out):
    out[:, :384] = dot_t(rows[...], weights[192:, :]).astype(BF16)
    out[:, 384:] = dot_t(rows[...], weights[:192, :]).astype(BF16)


def far_kernel(info, near, rows, weights, out, edge):
    half = 4 * SENT
    out[:half, :] = near[...]
    out[half:, :384] = dot_t(rows[...], weights[192:, :]).astype(BF16)
    for k in range(4):
        start = pl.multiple_of(info[4 + k] * SENT, 16)
        edge[k * 128 : (k + 1) * 128, :] = out[pl.ds(start, 128), :384]
    out[half:, 384:] = dot_t(rows[...], weights[:192, :]).astype(BF16)


def project_one(rows, weights, info=None, near=None):
    vmem = pl.BlockSpec(memory_space=pltpu.VMEM)
    cost = pl.CostEstimate(flops=2 * 576 * 576 * D1, bytes_accessed=5 * 2**20, transcendentals=0)
    params = pltpu.CompilerParams(vmem_limit_bytes=24 * 2**20)
    if near is None:
        return pl.pallas_call(
            near_kernel,
            out_shape=jax.ShapeDtypeStruct((4 * SENT, 576), BF16),
            in_specs=[vmem] * 2,
            out_specs=vmem,
            compiler_params=params,
            cost_estimate=cost,
            name="project_near",
        )(rows, weights)
    return pl.pallas_call(
        far_kernel,
        out_shape=(
            jax.ShapeDtypeStruct((8 * SENT, 576), BF16), jax.ShapeDtypeStruct((WIN, 384), BF16)
        ),
        in_specs=[pl.BlockSpec(memory_space=pltpu.SMEM)] + [vmem] * 3,
        out_specs=(vmem, vmem),
        compiler_params=params,
        cost_estimate=cost,
        name="project_far",
    )(info, near, rows, weights)


def mlp_kernel(rows, gate, up, down, out):
    def some(step, _):
        cut = pl.ds(pl.multiple_of(step * 256, 256), 256)
        block = rows[cut, :]
        gated = dot(block, gate[...])
        hidden = gated / (1.0 + jnp.exp(-gated)) * dot(block, up[...])
        out[cut, :] = dot(hidden.astype(BF16), down[...]).astype(BF16)
        return 0

    lax.fori_loop(0, rows.shape[0] // 256, some, 0)


def mlp(rows, gate, up, down):
    return pl.pallas_call(
        mlp_kernel,
        out_shape=jax.ShapeDtypeStruct(rows.shape, BF16),
        in_specs=[pl.BlockSpec(memory_space=pltpu.VMEM)] * 4,
        out_specs=pl.BlockSpec(memory_space=pltpu.VMEM),
        compiler_params=pltpu.CompilerParams(vmem_limit_bytes=32 * 2**20),
        cost_estimate=pl.CostEstimate(
            flops=2 * 512 * 1536 * 1536, bytes_accessed=8 * 2**20, transcendentals=512 * 512
        ),
        name="mlp",
    )(rows, gate, up, down)


def project_kernel(info, pooled, pieces, weights, valid, chunks, wide_own, total, squares):
    step = pl.program_id(0)
    y = info[8]

    @pl.when(step == 0)
    def _():
        total[...] = jnp.zeros_like(total)
        squares[...] = jnp.zeros_like(squares)

    wide = dot(pooled[...], pieces[...].reshape(D1, 512)).astype(BF16)
    floats = wide.astype(F32)
    squares[...] += jnp.broadcast_to(
        jnp.sum(floats * floats, axis=-1, keepdims=True), squares.shape
    )
    for i in range(3):
        total[:, i * 512 : (i + 1) * 512] += dot(wide, weights[i])

    @pl.when(step == 0)
    def _():
        for p in range(8):
            start = pl.multiple_of(info[p] * 64, 64)
            wide_own[pl.ds(start, 64), :] = wide[p * 64 : (p + 1) * 64]

    @pl.when(step == 7)
    def _():
        scale = lax.rsqrt(squares[...] / D2 + 1e-06)
        for k in range(4):
            head = (y + k) & 3
            for i in range(3):
                cut = slice(i * 128, (i + 1) * 128)
                lanes = pl.ds(pl.multiple_of(i * 512 + head * 128, 128), 128)
                part = total[:, lanes] * (scale * SCORE_FACTOR if i == 0 else scale)
                part = part.astype(BF16)
                for p in range(8):
                    start = pl.multiple_of(info[p] * 64, 64)
                    chunks[k, pl.ds(start, 64), cut] = part[p * 64 : (p + 1) * 64]
                chunks[k, 512:, cut] = valid[...]


def project_two(info, pooled, pieces, weights, valid):
    return pl.pallas_call(
        project_kernel,
        out_shape=(
            jax.ShapeDtypeStruct((4, 512 + EXT, 384), BF16),
            jax.ShapeDtypeStruct((512, 512), BF16),
        ),
        grid_spec=pltpu.PrefetchScalarGridSpec(
            num_scalar_prefetch=1,
            grid=(8,),
            in_specs=[
                pl.BlockSpec((512, D1), lambda s, info: (0, 0)),
                pl.BlockSpec((8, 1, 192, 512), lambda s, info: (0, s, 0, 0)),
                pl.BlockSpec((3, 512, 512), lambda s, info: (0, info[s], 0)),
                pl.BlockSpec((EXT, 128), lambda s, info: (0, 0)),
            ],
            out_specs=(
                pl.BlockSpec((4, 512 + EXT, 384), lambda s, info: (0, 0, 0)),
                pl.BlockSpec((512, 512), lambda s, info: (0, 0)),
            ),
            scratch_shapes=[pltpu.VMEM((512, 1536), F32), pltpu.VMEM((512, 128), F32)],
        ),
        compiler_params=pltpu.CompilerParams(vmem_limit_bytes=40 * 2**20),
        cost_estimate=pl.CostEstimate(
            flops=4 * 512 * 4096 * 1536, bytes_accessed=28 * 2**20, transcendentals=512
        ),
        name="project_two",
    )(info, pooled, pieces, weights, valid)


def causal_kernel(own_part, info, queries, kv_pair, start, start_stats, out, out_stats, keys, values, even, odd):
    half, core, y = info[0], info[1], info[2]
    slot = pl.program_id(0)
    own_pair = (y + slot) & 3

    @pl.when(slot == 0)
    def _():
        def prepare(block, _):
            row = lax.broadcasted_iota(jnp.int32, (512, 128), 0).astype(F32)
            lane = lax.broadcasted_iota(jnp.int32, (512, 128), 1)
            for which, kv in enumerate(kv_pair):
                count = jnp.sum(kv[block, 512 : 512 + EXT, :128].astype(F32))
                invalid = (lane == 0) & (row >= count)
                keys[which * 4 + block, :, :128] = kv[block, :512, :128]
                keys[which * 4 + block, :, 128:] = jnp.where(invalid, MASKED, 0.0).astype(BF16)
                values[which * 4 + block] = kv[block, :512, 128:].T
            return 0

        lax.fori_loop(0, 4, prepare, 0)

    lane = lax.broadcasted_iota(jnp.int32, (512, 128), 1)
    query = jnp.concatenate([queries[0], jnp.where(lane == 0, 1.0, 0.0).astype(BF16)], axis=1)

    def block_of(pair, which):
        return (which ^ core) * 4 + ((pair - y) & 3)

    def scores_of(pair, which):
        return lax.dot_general(
            keys[block_of(pair, which)], query, (((1,), (1,)), ((), ())), preferred_element_type=F32
        )

    def absorb(scores, pair, which, carry, edge):
        largest, total, sums = carry
        if edge:
            key = lax.broadcasted_iota(jnp.int32, scores.shape, 0) + which * 512
            own = lax.broadcasted_iota(jnp.int32, scores.shape, 1) + core * 512
            scores = jnp.where(key <= own, scores, MASKED)
        new_largest = jnp.maximum(largest, jnp.max(scores, axis=0, keepdims=True))
        decay = jnp.exp2(largest - new_largest)
        weights = jnp.exp2(scores - new_largest)
        total = total * decay + jnp.sum(weights, axis=0, keepdims=True)
        sums = sums * decay + dot(values[block_of(pair, which)], weights.astype(BF16))
        return new_largest, total, sums

    even[...] = scores_of(0, 0)

    def both(pair, carry, edge=False):
        odd[...] = scores_of(pair, 1)
        carry = absorb(even[...], pair, 0, carry, edge)
        if not edge:
            even[...] = scores_of((pair + 1) & 3, 0)
        return absorb(odd[...], pair, 1, carry, edge)

    if own_part:
        carry = (
            jnp.full((1, 512), MASKED, F32), jnp.zeros((1, 512), F32), jnp.zeros((128, 512), F32)
        )
        carry = lax.fori_loop(0, own_pair, both, carry)
        largest, total, sums = both(own_pair, carry, True)
        out[0] = sums
        out_stats[0] = jnp.concatenate([largest, total, jnp.zeros((6, 512), F32)], axis=0)
    else:
        carry = (start_stats[0, 0:1], start_stats[0, 1:2], start[0])
        _, total, sums = lax.fori_loop(0, half * 4, both, carry)
        out[0] = (sums / total).T.astype(BF16)


def causal_attend(own_part, info, queries, kv_pair, start=None):
    def by_slot(*shape):
        return pl.BlockSpec((1, *shape), lambda s, info: (s, 0, 0))

    sums_shape = jax.ShapeDtypeStruct((4, 128, 512), F32)
    stats_shape = jax.ShapeDtypeStruct((4, 8, 512), F32)
    whole = pl.BlockSpec((4, 512 + EXT, 256), lambda s, info: (0, 0, 0))
    in_specs = [by_slot(512, 128), whole, whole]
    operands = [queries, *kv_pair]
    if own_part:
        def kernel(info, queries, kv, other, out, out_stats, *scratch):
            causal_kernel(True, info, queries, (kv, other), None, None, out, out_stats, *scratch)

        out_shape = (sums_shape, stats_shape)
        out_specs = (by_slot(128, 512), by_slot(8, 512))
        tiles = 18
    else:
        def kernel(info, queries, kv, other, start, start_stats, out, *scratch):
            causal_kernel(False, info, queries, (kv, other), start, start_stats, out, None, *scratch)

        out_shape = jax.ShapeDtypeStruct((4, 512, 128), BF16)
        out_specs = by_slot(512, 128)
        in_specs += [by_slot(128, 512), by_slot(8, 512)]
        operands += list(start)
        tiles = 32
    return pl.pallas_call(
        kernel,
        out_shape=out_shape,
        grid_spec=pltpu.PrefetchScalarGridSpec(
            num_scalar_prefetch=1,
            grid=(4,),
            in_specs=in_specs,
            out_specs=out_specs,
            scratch_shapes=[
                pltpu.VMEM((8, 512, 256), BF16),
                pltpu.VMEM((8, 128, 512), BF16),
                pltpu.VMEM((512, 512), F32),
                pltpu.VMEM((512, 512), F32),
            ],
        ),
        compiler_params=pltpu.CompilerParams(vmem_limit_bytes=40 * 2**20),
        cost_estimate=pl.CostEstimate(
            flops=tiles * 512 * 512 * 512, bytes_accessed=4 * 2**20, transcendentals=tiles * 2**18
        ),
        name="causal_own" if own_part else "causal_first_half",
    )(info, *operands)


def turn_y(value, steps, first=0):
    return lax.ppermute(
        value, "seq", [(i, (i & 9) | ((i + 2 * steps) & 6)) for i in range(first, 16)]
    )


def flip_seq(value, bit):
    return lax.ppermute(value, "seq", [(i, i ^ bit) for i in range(16)])


def per_device(
    tokens, boundary, heads_in, heads_out, gate_up, down_weight, widen, heads_in_two, heads_out_two
):
    seq_position = lax.axis_index("seq")
    me = lax.axis_index("blk")
    rows = tokens.shape[0]
    capacity = 512
    width = D1 // 8
    block_of = jnp.stack([((me ^ (4 * x)) & 4) | ((me + z) & 3) for x, z in PLACES])
    numbers = jnp.arange(8, dtype=jnp.int32)
    place_of = jnp.sum(
        jnp.where(block_of[None, :] == numbers[:, None], numbers[None, :], 0), axis=1
    )

    heads_in_flat = heads_in.transpose(1, 2, 0).reshape(3 * width, D1)
    core, y, half = seq_position & 1, (seq_position >> 1) & 3, seq_position >> 3
    piece = lax.dynamic_slice(widen, ((seq_position & 7) * 192, 0), (192, 512))

    near, far = gather_blk(prepare(tokens, boundary[None, :]))
    arrived = near[2 * SENT :]
    gates = later(gate_up, arrived)
    gate_flat, up_flat = lax.optimization_barrier((gates[:, 0, :], gates[:, 1, :]))
    marks = jnp.concatenate(
        [part.reshape(4, SENT, D1)[:, rows, :rows] for part in (near, far)], axis=0
    )
    info = later(jnp.concatenate([place_of, seq_position[None]]).astype(jnp.int32), gate_flat)
    qkv_near = project_one(near, heads_in_flat)
    qkv, edge = project_one(far, heads_in_flat, info, qkv_near)
    halo = lax.ppermute(edge, "seq", [(i, i + 1) for i in range(15)])
    attended = window_attend(info, qkv, halo, window_attend(info, qkv))
    attn_near = dot(attended[: 4 * rows], heads_out).astype(BF16)
    attn_far = dot(attended[4 * rows :], heads_out).astype(BF16)
    opposite, diagonal = reduce_first(attn_far)

    pieces = jnp.concatenate(gather_blk(piece, qkv), axis=0)
    pieces = later(pieces, attended)
    pieces = lax.all_gather(
        pieces, "seq", axis=0, axis_index_groups=[[h * 8 + k for k in range(8)] for h in range(2)]
    ).reshape(8, 8, 192, 512)
    mid_stream = (
        tokens.astype(F32) + reduce_second(attn_near, opposite, diagonal)
    ).astype(BF16)

    normed_mid = normalize(mid_stream).astype(BF16)

    near, far = gather_blk(normed_mid)
    mlp_near = mlp(near, gate_flat, up_flat, down_weight)
    mlp_far = mlp(far, gate_flat, up_flat, down_weight)
    marks = marks.astype(F32)
    counts = jnp.sum(marks, axis=1)
    before = jnp.sum(
        jnp.where(block_of[None, :] < block_of[:, None], counts[None, :], 0.0), axis=1
    )
    steps = jnp.arange(rows)
    running = dot(marks.astype(BF16), (steps[:, None] <= steps[None, :]).astype(BF16))
    slots = jnp.where(marks > 0.5, before[:, None] + running - 1.0, -1.0).astype(jnp.int32)
    span_count = jnp.sum(counts).astype(jnp.int32)
    targets = (block_of[:, None] * 64 + jnp.arange(64)[None, :]).reshape(capacity, 1)
    selector = (slots.reshape(1, 8 * rows) == targets).astype(BF16)
    placed = (
        dot(selector[:, : 4 * rows], mlp_near)
        + dot(selector[:, 4 * rows :], mlp_far)
        + dot(selector[:, :rows], mid_stream)
    ).astype(BF16)
    pooled_own = reduce_blk(placed[:256], placed[256:]).astype(BF16)
    pooled = jnp.concatenate(gather_blk(pooled_own), axis=0)

    validity = (jnp.arange(capacity, dtype=jnp.int32) < span_count).astype(F32)
    valid_rows = jnp.pad(
        validity.reshape(4, 128).astype(BF16), ((0, EXT - 4), (0, 0))
    )
    info_one = jnp.concatenate([block_of, y[None]]).astype(jnp.int32)
    chunks, wide_cols = project_two(
        info_one, pooled, pieces, heads_in_two.transpose(1, 0, 2), valid_rows
    )
    opposite, diagonal = reduce_first(later(mlp_far, chunks[0]))
    from_behind = turn_y(chunks[1], 1)
    from_ahead = turn_y(chunks[3], 3)
    from_opposite = turn_y(chunks[2], 2)
    mine = jnp.stack([chunks[0], from_ahead, from_opposite, from_behind])
    queries, own_kv = mine[:, :capacity, :128], mine[:, :, 128:]
    first_kv = lax.ppermute(own_kv, "seq", [(i, i + 8) for i in range(8)])
    info_two = jnp.stack([half, core, y]).astype(jnp.int32)
    running = causal_attend(True, info_two, queries, (own_kv, flip_seq(own_kv, 1)))
    first_kv = first_kv + running[1][0, 2, 0].astype(BF16)
    mixed = causal_attend(False, info_two, queries, (first_kv, flip_seq(first_kv, 1)), running)
    back = [mixed[0], turn_y(mixed[3], 3), turn_y(mixed[2], 2), turn_y(mixed[1], 1)]
    heads = jnp.concatenate([back[0], back[1], back[2], back[3]] * 2, axis=1)
    attended_two = lax.dynamic_slice(heads, (0, ((4 - y) & 3) * 128), (capacity, 512))


    level_one = (
        mid_stream.astype(F32)
        + reduce_second(later(mlp_near, mixed[0]), opposite, diagonal)
    ).astype(BF16)
    column_of = later(block_of, level_one)

    def columns(place):
        part = lax.dynamic_slice(heads_out_two, (0, column_of[place] * 512), (512, 512))
        return dot(attended_two, part).astype(BF16)

    out_far = jnp.concatenate([columns(place) for place in range(4, 8)], axis=0)
    out_near = jnp.concatenate([columns(place) for place in range(4)], axis=0)
    out_near = lax.optimization_barrier(out_near)
    level_two = (
        (wide_cols.astype(F32) + reduce_blk(out_near, out_far)) * validity[:, None]
    ).astype(BF16)
    return (level_one, level_two)


def solution(mesh):
    placed = (
        P(("seq", "blk"), None),
        P(("seq", "blk")),
        P(None, None, "blk"),
        P("blk", None),
        P(None, None, "blk"),
        P("blk", None),
        P(None, "blk"),
        P(None, None, "blk"),
        P("blk", None),
    )
    return jax.shard_map(
        per_device,
        mesh=mesh,
        in_specs=placed,
        out_specs=(P(("seq", "blk"), None), P("seq", "blk")),
        check_vma=False,
    )
```

```python
import jax
import jax.numpy as jnp
from jax import lax
from jax.experimental import pallas as pl
from jax.experimental.pallas import tpu as pltpu
from jax.sharding import PartitionSpec as P

D1 = 1536
H1 = 24
D2 = 4096
H2 = 32
WIN = 512
EXT = 16
SENT = 128
BF16 = jnp.bfloat16
F32 = jnp.float32
MASKED = -1e30
SCORE_FACTOR = 128 ** (-0.5) * 1.4426950408889634

PLACES = ((0, 0), (1, 0), (0, 1), (0, 3), (0, 2), (1, 2), (1, 1), (1, 3))


def flip_x(value):
    return lax.ppermute(value, "blk", [(i, i ^ 4) for i in range(8)])


def turn_z(value, steps):
    return lax.ppermute(value, "blk", [(i, (i & 4) | ((i + steps) & 3)) for i in range(8)])


def later(array, value):
    return array + (value[0, 0].astype(F32) * 0.0).astype(array.dtype)


def gather_blk(own, between=None):
    across = flip_x(own)
    behind = turn_z(own, 1)
    ahead = turn_z(own, 3)
    first = jnp.concatenate([own, across], axis=0)
    second = jnp.concatenate([ahead, behind], axis=0)
    if between is not None:
        first, second = later(first, between), later(second, between)
    opposite = turn_z(first, 2)
    diagonal = flip_x(second)
    near = jnp.concatenate([first, second], axis=0)
    far = jnp.concatenate([opposite, diagonal], axis=0)
    return near, far


def reduce_first(far):
    count = far.shape[0] // 4
    return turn_z(far[: 2 * count], 2), flip_x(far[2 * count :])


def reduce_second(near, opposite, diagonal):
    count = near.shape[0] // 4

    def plus(block, other):
        return near[block * count : (block + 1) * count].astype(F32) + other.astype(F32)

    across = flip_x(plus(1, opposite[count:]).astype(BF16))
    behind = turn_z(plus(2, diagonal[:count]).astype(BF16), 1)
    ahead = turn_z(plus(3, diagonal[count:]).astype(BF16), 3)
    return (
        plus(0, opposite[:count])
        + across.astype(F32)
        + behind.astype(F32)
        + ahead.astype(F32)
    )


def reduce_blk(near, far):
    return reduce_second(near, *reduce_first(far))


def normalize(values):
    floats = values.astype(F32)
    return floats * lax.rsqrt(jnp.mean(floats * floats, axis=-1, keepdims=True) + 1e-06)


def dot(left, right):
    return jnp.dot(left, right, preferred_element_type=F32)


def dot_t(left, right):
    return lax.dot_general(left, right, (((1,), (1,)), ((), ())), preferred_element_type=F32)


def window_kernel(blocks, info, qkv, halo, before, out):
    rows, width, size, stride = 128, D1 // 8, D1 // H1, SENT
    key_count = WIN + rows
    i = lax.broadcasted_iota(jnp.int32, (rows, key_count), 0)
    j = lax.broadcasted_iota(jnp.int32, (rows, key_count), 1)
    band = (j > i) & (j <= i + WIN)
    seq_position = info[8]
    if before is not None:
        out[...] = before[...]
    for n in blocks:
        place = info[n]
        keys, values = [], []
        for k in range(n - 4, n + 1):
            if k >= 0:
                start = pl.multiple_of(info[k] * stride, 16)
                block = qkv[pl.ds(start, rows), :]
                keys.append(block[:, :width])
                values.append(block[:, width : 2 * width])
            else:
                block = halo[(k + 4) * rows : (k + 5) * rows, :]
                keys.append(block[:, :width])
                values.append(block[:, width:])
        keys = jnp.concatenate(keys, axis=0)
        values = jnp.concatenate(values, axis=0)
        queries = qkv[pl.ds(pl.multiple_of(place * stride, 16), rows), 2 * width :]
        allowed = band
        if n < 4:
            allowed = band & (j + ((n - 4) * rows + seq_position * 1024) >= 0)
        parts = []
        for h in range(width // size):
            cut = slice(h * size, (h + 1) * size)
            scores = lax.dot_general(
                queries[:, cut], keys[:, cut], (((1,), (1,)), ((), ())),
                preferred_element_type=F32,
            ) * size ** (-0.5)
            scores = jnp.where(allowed, scores, MASKED)
            largest = jnp.max(scores, axis=-1, keepdims=True)
            weights = jnp.exp(scores - largest)
            total = jnp.sum(weights, axis=-1, keepdims=True)
            parts.append(dot(weights.astype(BF16), values[:, cut]) / total)
        out[pl.ds(pl.multiple_of(place * rows, 16), rows), :] = jnp.concatenate(
            parts, axis=1
        ).astype(BF16)


def window_attend(info, qkv, halo=None, before=None):
    if halo is None:
        def kernel(info, qkv, out):
            window_kernel(range(4, 8), info, qkv, None, None, out)

        operands = (info, qkv)
    else:
        def kernel(info, qkv, halo, before, out):
            window_kernel(range(4), info, qkv, halo, before, out)

        operands = (info, qkv, halo, before)
    vmem = pl.BlockSpec(memory_space=pltpu.VMEM)
    return pl.pallas_call(
        kernel,
        out_shape=jax.ShapeDtypeStruct((1024, D1 // 8), BF16),
        in_specs=[pl.BlockSpec(memory_space=pltpu.SMEM)] + [vmem] * (len(operands) - 1),
        out_specs=vmem,
        compiler_params=pltpu.CompilerParams(vmem_limit_bytes=32 * 2**20),
        cost_estimate=pl.CostEstimate(
            flops=12 * 128 * 640 * 256, bytes_accessed=2 * 2**20, transcendentals=12 * 128 * 640
        ),
        name="window_late" if halo is None else "window_early",
    )(*operands)


def prepare_kernel(tokens, out):
    floats = tokens[...].astype(F32)
    scale = lax.rsqrt(jnp.mean(floats * floats, axis=-1, keepdims=True) + 1e-06)
    out[...] = (floats * scale).astype(BF16)


def prepare(tokens):
    return pl.pallas_call(
        prepare_kernel,
        out_shape=jax.ShapeDtypeStruct(tokens.shape, BF16),
        in_specs=[pl.BlockSpec(memory_space=pltpu.VMEM)],
        out_specs=pl.BlockSpec(memory_space=pltpu.VMEM),
        name="prepare",
    )(tokens)


def near_kernel(rows, weights, out):
    out[:, :384] = dot_t(rows[...], weights[192:, :]).astype(BF16)
    out[:, 384:] = dot_t(rows[...], weights[:192, :]).astype(BF16)


def far_kernel(info, near, rows, weights, out, edge):
    half = 4 * SENT
    out[:half, :] = near[...]
    out[half:, :384] = dot_t(rows[...], weights[192:, :]).astype(BF16)
    for k in range(4):
        start = pl.multiple_of(info[4 + k] * SENT, 16)
        edge[k * 128 : (k + 1) * 128, :] = out[pl.ds(start, 128), :384]
    out[half:, 384:] = dot_t(rows[...], weights[:192, :]).astype(BF16)


def project_one(rows, weights, info=None, near=None):
    vmem = pl.BlockSpec(memory_space=pltpu.VMEM)
    cost = pl.CostEstimate(flops=2 * 576 * 576 * D1, bytes_accessed=5 * 2**20, transcendentals=0)
    params = pltpu.CompilerParams(vmem_limit_bytes=24 * 2**20)
    if near is None:
        return pl.pallas_call(
            near_kernel,
            out_shape=jax.ShapeDtypeStruct((4 * SENT, 576), BF16),
            in_specs=[vmem] * 2,
            out_specs=vmem,
            compiler_params=params,
            cost_estimate=cost,
            name="project_near",
        )(rows, weights)
    return pl.pallas_call(
        far_kernel,
        out_shape=(
            jax.ShapeDtypeStruct((8 * SENT, 576), BF16), jax.ShapeDtypeStruct((WIN, 384), BF16)
        ),
        in_specs=[pl.BlockSpec(memory_space=pltpu.SMEM)] + [vmem] * 3,
        out_specs=(vmem, vmem),
        compiler_params=params,
        cost_estimate=cost,
        name="project_far",
    )(info, near, rows, weights)


def mlp_kernel(rows, gate, up, down, out):
    def some(step, _):
        cut = pl.ds(pl.multiple_of(step * 256, 256), 256)
        block = rows[cut, :]
        gated = dot(block, gate[...])
        hidden = gated / (1.0 + jnp.exp(-gated)) * dot(block, up[...])
        out[cut, :] = dot(hidden.astype(BF16), down[...]).astype(BF16)
        return 0

    lax.fori_loop(0, rows.shape[0] // 256, some, 0)


def mlp(rows, gate, up, down):
    return pl.pallas_call(
        mlp_kernel,
        out_shape=jax.ShapeDtypeStruct(rows.shape, BF16),
        in_specs=[pl.BlockSpec(memory_space=pltpu.VMEM)] * 4,
        out_specs=pl.BlockSpec(memory_space=pltpu.VMEM),
        compiler_params=pltpu.CompilerParams(vmem_limit_bytes=32 * 2**20),
        cost_estimate=pl.CostEstimate(
            flops=2 * 512 * 1536 * 1536, bytes_accessed=8 * 2**20, transcendentals=512 * 512
        ),
        name="mlp",
    )(rows, gate, up, down)


def project_kernel(info, pooled, pieces, weights, valid, chunks, wide_own, total, squares):
    step = pl.program_id(0)
    y = info[8]

    @pl.when(step == 0)
    def _():
        total[...] = jnp.zeros_like(total)
        squares[...] = jnp.zeros_like(squares)

    wide = dot(pooled[...], pieces[...].reshape(D1, 512)).astype(BF16)
    floats = wide.astype(F32)
    squares[...] += jnp.broadcast_to(
        jnp.sum(floats * floats, axis=-1, keepdims=True), squares.shape
    )
    for i in range(3):
        total[:, i * 512 : (i + 1) * 512] += dot(wide, weights[i])

    @pl.when(step == 0)
    def _():
        for p in range(8):
            start = pl.multiple_of(info[p] * 64, 64)
            wide_own[pl.ds(start, 64), :] = wide[p * 64 : (p + 1) * 64]

    @pl.when(step == 7)
    def _():
        scale = lax.rsqrt(squares[...] / D2 + 1e-06)
        for k in range(4):
            head = (y + k) & 3
            for i in range(3):
                cut = slice(i * 128, (i + 1) * 128)
                lanes = pl.ds(pl.multiple_of(i * 512 + head * 128, 128), 128)
                part = total[:, lanes] * (scale * SCORE_FACTOR if i == 0 else scale)
                part = part.astype(BF16)
                for p in range(8):
                    start = pl.multiple_of(info[p] * 64, 64)
                    chunks[k, pl.ds(start, 64), cut] = part[p * 64 : (p + 1) * 64]
                chunks[k, 512:, cut] = valid[...]


def project_two(info, pooled, pieces, weights, valid):
    return pl.pallas_call(
        project_kernel,
        out_shape=(
            jax.ShapeDtypeStruct((4, 512 + EXT, 384), BF16),
            jax.ShapeDtypeStruct((512, 512), BF16),
        ),
        grid_spec=pltpu.PrefetchScalarGridSpec(
            num_scalar_prefetch=1,
            grid=(8,),
            in_specs=[
                pl.BlockSpec((512, D1), lambda s, info: (0, 0)),
                pl.BlockSpec((8, 1, 192, 512), lambda s, info: (0, s, 0, 0)),
                pl.BlockSpec((3, 512, 512), lambda s, info: (0, info[s], 0)),
                pl.BlockSpec((EXT, 128), lambda s, info: (0, 0)),
            ],
            out_specs=(
                pl.BlockSpec((4, 512 + EXT, 384), lambda s, info: (0, 0, 0)),
                pl.BlockSpec((512, 512), lambda s, info: (0, 0)),
            ),
            scratch_shapes=[pltpu.VMEM((512, 1536), F32), pltpu.VMEM((512, 128), F32)],
        ),
        compiler_params=pltpu.CompilerParams(vmem_limit_bytes=40 * 2**20),
        cost_estimate=pl.CostEstimate(
            flops=4 * 512 * 4096 * 1536, bytes_accessed=28 * 2**20, transcendentals=512
        ),
        name="project_two",
    )(info, pooled, pieces, weights, valid)


def causal_kernel(own_part, info, queries, kv_pair, start, start_stats, out, out_stats, keys, values, even, odd):
    half, core, y = info[0], info[1], info[2]
    slot = pl.program_id(0)
    own_pair = (y + slot) & 3

    @pl.when(slot == 0)
    def _():
        def prepare(block, _):
            row = lax.broadcasted_iota(jnp.int32, (512, 128), 0).astype(F32)
            lane = lax.broadcasted_iota(jnp.int32, (512, 128), 1)
            for which, kv in enumerate(kv_pair):
                count = jnp.sum(kv[block, 512 : 512 + EXT, :128].astype(F32))
                invalid = (lane == 0) & (row >= count)
                keys[which * 4 + block, :, :128] = kv[block, :512, :128]
                keys[which * 4 + block, :, 128:] = jnp.where(invalid, MASKED, 0.0).astype(BF16)
                values[which * 4 + block] = kv[block, :512, 128:].T
            return 0

        lax.fori_loop(0, 4, prepare, 0)

    lane = lax.broadcasted_iota(jnp.int32, (512, 128), 1)
    query = jnp.concatenate([queries[0], jnp.where(lane == 0, 1.0, 0.0).astype(BF16)], axis=1)

    def block_of(pair, which):
        return (which ^ core) * 4 + ((pair - y) & 3)

    def scores_of(pair, which):
        return lax.dot_general(
            keys[block_of(pair, which)], query, (((1,), (1,)), ((), ())), preferred_element_type=F32
        )

    def absorb(scores, pair, which, carry, edge):
        largest, total, sums = carry
        if edge:
            key = lax.broadcasted_iota(jnp.int32, scores.shape, 0) + which * 512
            own = lax.broadcasted_iota(jnp.int32, scores.shape, 1) + core * 512
            scores = jnp.where(key <= own, scores, MASKED)
        new_largest = jnp.maximum(largest, jnp.max(scores, axis=0, keepdims=True))
        decay = jnp.exp2(largest - new_largest)
        weights = jnp.exp2(scores - new_largest)
        total = total * decay + jnp.sum(weights, axis=0, keepdims=True)
        sums = sums * decay + dot(values[block_of(pair, which)], weights.astype(BF16))
        return new_largest, total, sums

    even[...] = scores_of(0, 0)

    def both(pair, carry, edge=False):
        odd[...] = scores_of(pair, 1)
        carry = absorb(even[...], pair, 0, carry, edge)
        if not edge:
            even[...] = scores_of((pair + 1) & 3, 0)
        return absorb(odd[...], pair, 1, carry, edge)

    if own_part:
        carry = (
            jnp.full((1, 512), MASKED, F32), jnp.zeros((1, 512), F32), jnp.zeros((128, 512), F32)
        )
        carry = lax.fori_loop(0, own_pair, both, carry)
        largest, total, sums = both(own_pair, carry, True)
        out[0] = sums
        out_stats[0] = jnp.concatenate([largest, total, jnp.zeros((6, 512), F32)], axis=0)
    else:
        carry = (start_stats[0, 0:1], start_stats[0, 1:2], start[0])
        _, total, sums = lax.fori_loop(0, half * 4, both, carry)
        out[0] = (sums / total).T.astype(BF16)


def causal_attend(own_part, info, queries, kv_pair, start=None):
    def by_slot(*shape):
        return pl.BlockSpec((1, *shape), lambda s, info: (s, 0, 0))

    sums_shape = jax.ShapeDtypeStruct((4, 128, 512), F32)
    stats_shape = jax.ShapeDtypeStruct((4, 8, 512), F32)
    whole = pl.BlockSpec((4, 512 + EXT, 256), lambda s, info: (0, 0, 0))
    in_specs = [by_slot(512, 128), whole, whole]
    operands = [queries, *kv_pair]
    if own_part:
        def kernel(info, queries, kv, other, out, out_stats, *scratch):
            causal_kernel(True, info, queries, (kv, other), None, None, out, out_stats, *scratch)

        out_shape = (sums_shape, stats_shape)
        out_specs = (by_slot(128, 512), by_slot(8, 512))
        tiles = 18
    else:
        def kernel(info, queries, kv, other, start, start_stats, out, *scratch):
            causal_kernel(False, info, queries, (kv, other), start, start_stats, out, None, *scratch)

        out_shape = jax.ShapeDtypeStruct((4, 512, 128), BF16)
        out_specs = by_slot(512, 128)
        in_specs += [by_slot(128, 512), by_slot(8, 512)]
        operands += list(start)
        tiles = 32
    return pl.pallas_call(
        kernel,
        out_shape=out_shape,
        grid_spec=pltpu.PrefetchScalarGridSpec(
            num_scalar_prefetch=1,
            grid=(4,),
            in_specs=in_specs,
            out_specs=out_specs,
            scratch_shapes=[
                pltpu.VMEM((8, 512, 256), BF16),
                pltpu.VMEM((8, 128, 512), BF16),
                pltpu.VMEM((512, 512), F32),
                pltpu.VMEM((512, 512), F32),
            ],
        ),
        compiler_params=pltpu.CompilerParams(vmem_limit_bytes=40 * 2**20),
        cost_estimate=pl.CostEstimate(
            flops=tiles * 512 * 512 * 512, bytes_accessed=4 * 2**20, transcendentals=tiles * 2**18
        ),
        name="causal_own" if own_part else "causal_first_half",
    )(info, *operands)


def turn_y(value, steps, first=0):
    return lax.ppermute(
        value, "seq", [(i, (i & 9) | ((i + 2 * steps) & 6)) for i in range(first, 16)]
    )


def output_kernel(count, info, own, ahead, opposite, behind, weights, out, mixed):
    @pl.when(pl.program_id(0) == 0)
    def _():
        for k, part in enumerate((own, ahead, opposite, behind)):
            head = (info[count] + k) & 3
            mixed[:, pl.ds(pl.multiple_of(head * 128, 128), 128)] = part[...]

    out[...] = dot(mixed[...], weights[...]).astype(BF16)


def output_columns(blocks, y, parts, weights):
    count = blocks.shape[0]

    def kernel(*refs):
        output_kernel(count, *refs)

    return pl.pallas_call(
        kernel,
        out_shape=jax.ShapeDtypeStruct((count * 512, 512), BF16),
        grid_spec=pltpu.PrefetchScalarGridSpec(
            num_scalar_prefetch=1,
            grid=(count,),
            in_specs=[pl.BlockSpec((512, 128), lambda s, info: (0, 0))] * 4
            + [pl.BlockSpec((512, 512), lambda s, info: (0, info[s]))],
            out_specs=pl.BlockSpec((512, 512), lambda s, info: (s, 0)),
            scratch_shapes=[pltpu.VMEM((512, 512), BF16)],
        ),
        compiler_params=pltpu.CompilerParams(vmem_limit_bytes=24 * 2**20),
        cost_estimate=pl.CostEstimate(
            flops=2 * 512**3 * count, bytes_accessed=count * 2**20, transcendentals=0
        ),
        name="output_columns",
    )(jnp.concatenate([blocks, y[None]]).astype(jnp.int32), *parts, weights)


def flip_seq(value, bit):
    return lax.ppermute(value, "seq", [(i, i ^ bit) for i in range(16)])


def per_device(
    tokens, boundary, heads_in, heads_out, gate_up, down_weight, widen, heads_in_two, heads_out_two
):
    seq_position = lax.axis_index("seq")
    me = lax.axis_index("blk")
    rows = tokens.shape[0]
    capacity = 512
    width = D1 // 8
    block_of = jnp.stack([((me ^ (4 * x)) & 4) | ((me + z) & 3) for x, z in PLACES])
    numbers = jnp.arange(8, dtype=jnp.int32)
    place_of = jnp.sum(
        jnp.where(block_of[None, :] == numbers[:, None], numbers[None, :], 0), axis=1
    )

    heads_in_flat = heads_in.transpose(1, 2, 0).reshape(3 * width, D1)
    core, y, half = seq_position & 1, (seq_position >> 1) & 3, seq_position >> 3
    piece = lax.dynamic_slice(widen, ((seq_position & 7) * 192, 0), (192, 512))

    near, far = gather_blk(prepare(tokens))
    arrived = near[2 * SENT :]
    gates = later(gate_up, arrived)
    gate_flat, up_flat = lax.optimization_barrier((gates[:, 0, :], gates[:, 1, :]))
    info = later(jnp.concatenate([place_of, seq_position[None]]).astype(jnp.int32), gate_flat)
    qkv_near = project_one(near, heads_in_flat)
    qkv, edge = project_one(far, heads_in_flat, info, qkv_near)
    halo = lax.ppermute(edge, "seq", [(i, i + 1) for i in range(15)])
    attended = window_attend(info, qkv, halo, window_attend(info, qkv))
    attn_near = dot(attended[: 4 * rows], heads_out).astype(BF16)
    attn_far = dot(attended[4 * rows :], heads_out).astype(BF16)
    opposite, diagonal = reduce_first(attn_far)

    marks_rows = jnp.pad(boundary.astype(BF16)[None, :], ((0, EXT - 1), (0, 512 - rows)))
    pieces = gather_blk(jnp.concatenate([piece, marks_rows], axis=0), qkv)
    starts = [(part, k * (192 + EXT)) for part in pieces for k in range(4)]
    marks = jnp.concatenate([part[k + 192 : k + 193, :rows] for part, k in starts], axis=0)
    pieces = later(jnp.concatenate([part[k : k + 192] for part, k in starts], axis=0), attended)
    pieces = lax.all_gather(
        pieces, "seq", axis=0, axis_index_groups=[[h * 8 + k for k in range(8)] for h in range(2)]
    ).reshape(8, 8, 192, 512)
    mid_stream = (
        tokens.astype(F32) + reduce_second(attn_near, opposite, diagonal)
    ).astype(BF16)

    normed_mid = normalize(mid_stream).astype(BF16)

    near, far = gather_blk(normed_mid)
    mlp_near = mlp(near, gate_flat, up_flat, down_weight)
    mlp_far = mlp(far, gate_flat, up_flat, down_weight)
    marks = marks.astype(F32)
    counts = jnp.sum(marks, axis=1)
    before = jnp.sum(
        jnp.where(block_of[None, :] < block_of[:, None], counts[None, :], 0.0), axis=1
    )
    steps = jnp.arange(rows)
    running = dot(marks.astype(BF16), (steps[:, None] <= steps[None, :]).astype(BF16))
    slots = jnp.where(marks > 0.5, before[:, None] + running - 1.0, -1.0).astype(jnp.int32)
    span_count = jnp.sum(counts).astype(jnp.int32)
    targets = (block_of[:, None] * 64 + jnp.arange(64)[None, :]).reshape(capacity, 1)
    selector = (slots.reshape(1, 8 * rows) == targets).astype(BF16)
    placed = (
        dot(selector[:, : 4 * rows], mlp_near)
        + dot(selector[:, 4 * rows :], mlp_far)
        + dot(selector[:, :rows], mid_stream)
    ).astype(BF16)
    pooled_own = reduce_blk(placed[:256], placed[256:]).astype(BF16)
    pooled = jnp.concatenate(gather_blk(pooled_own), axis=0)

    validity = (jnp.arange(capacity, dtype=jnp.int32) < span_count).astype(F32)
    valid_rows = jnp.pad(
        validity.reshape(4, 128).astype(BF16), ((0, EXT - 4), (0, 0))
    )
    info_one = jnp.concatenate([block_of, y[None]]).astype(jnp.int32)
    chunks, wide_cols = project_two(
        info_one, pooled, pieces, heads_in_two.transpose(1, 0, 2), valid_rows
    )
    opposite, diagonal = reduce_first(later(mlp_far, chunks[0]))
    from_behind = turn_y(chunks[1], 1)
    from_ahead = turn_y(chunks[3], 3)
    from_opposite = turn_y(chunks[2], 2)
    mine = jnp.stack([chunks[0], from_ahead, from_opposite, from_behind])
    queries, own_kv = mine[:, :capacity, :128], mine[:, :, 128:]
    first_kv = lax.ppermute(own_kv, "seq", [(i, i + 8) for i in range(8)])
    info_two = jnp.stack([half, core, y]).astype(jnp.int32)
    running = causal_attend(True, info_two, queries, (own_kv, flip_seq(own_kv, 1)))
    first_kv = first_kv + running[1][0, 2, 0].astype(BF16)
    mixed = causal_attend(False, info_two, queries, (first_kv, flip_seq(first_kv, 1)), running)
    back = [mixed[0], turn_y(mixed[3], 3), turn_y(mixed[2], 2), turn_y(mixed[1], 1)]
    out_opposite = turn_z(output_columns(block_of[4:6], y, back, heads_out_two), 2)
    out_diagonal = flip_x(output_columns(block_of[6:], y, back, heads_out_two))
    level_one = (
        mid_stream.astype(F32)
        + reduce_second(later(mlp_near, mixed[0]), opposite, diagonal)
    ).astype(BF16)
    out_near = output_columns(later(block_of[:4], level_one), y, back, heads_out_two)
    level_two = (
        (wide_cols.astype(F32) + reduce_second(out_near, out_opposite, out_diagonal)) * validity[:, None]
    ).astype(BF16)
    return (level_one, level_two)


def solution(mesh):
    placed = (
        P(("seq", "blk"), None),
        P(("seq", "blk")),
        P(None, None, "blk"),
        P("blk", None),
        P(None, None, "blk"),
        P("blk", None),
        P(None, "blk"),
        P(None, None, "blk"),
        P("blk", None),
    )
    return jax.shard_map(
        per_device,
        mesh=mesh,
        in_specs=placed,
        out_specs=(P(("seq", "blk"), None), P("seq", "blk")),
        check_vma=False,
    )
```

```python
import jax
import jax.numpy as jnp
from jax import lax
from jax.experimental import pallas as pl
from jax.experimental.pallas import tpu as pltpu
from jax.sharding import PartitionSpec as P

D1 = 1536
H1 = 24
D2 = 4096
H2 = 32
WIN = 512
EXT = 16
SENT = 128
BF16 = jnp.bfloat16
F32 = jnp.float32
MASKED = -1e30
SCORE_FACTOR = 128 ** (-0.5) * 1.4426950408889634

PLACES = ((0, 0), (1, 0), (0, 1), (0, 3), (0, 2), (1, 2), (1, 1), (1, 3))


def flip_x(value):
    return lax.ppermute(value, "blk", [(i, i ^ 4) for i in range(8)])


def turn_z(value, steps):
    return lax.ppermute(value, "blk", [(i, (i & 4) | ((i + steps) & 3)) for i in range(8)])


def later(array, value):
    return array + (value[0, 0].astype(F32) * 0.0).astype(array.dtype)


def gather_blk(own, between=None):
    across = flip_x(own)
    behind = turn_z(own, 1)
    ahead = turn_z(own, 3)
    first = jnp.concatenate([own, across], axis=0)
    second = jnp.concatenate([ahead, behind], axis=0)
    if between is not None:
        first, second = later(first, between), later(second, between)
    opposite = turn_z(first, 2)
    diagonal = flip_x(second)
    near = jnp.concatenate([first, second], axis=0)
    return near, opposite, diagonal


def reduce_first(far):
    count = far.shape[0] // 4
    return turn_z(far[: 2 * count], 2), flip_x(far[2 * count :])


def reduce_second(near, opposite, diagonal):
    count = near.shape[0] // 4

    def plus(block, other):
        return near[block * count : (block + 1) * count].astype(F32) + other.astype(F32)

    across = flip_x(plus(1, opposite[count:]).astype(BF16))
    behind = turn_z(plus(2, diagonal[:count]).astype(BF16), 1)
    ahead = turn_z(plus(3, diagonal[count:]).astype(BF16), 3)
    return (
        plus(0, opposite[:count])
        + across.astype(F32)
        + behind.astype(F32)
        + ahead.astype(F32)
    )


def reduce_blk(near, far):
    return reduce_second(near, *reduce_first(far))


def normalize(values):
    floats = values.astype(F32)
    return floats * lax.rsqrt(jnp.mean(floats * floats, axis=-1, keepdims=True) + 1e-06)


def dot(left, right):
    return jnp.dot(left, right, preferred_element_type=F32)


def dot_t(left, right):
    return lax.dot_general(left, right, (((1,), (1,)), ((), ())), preferred_element_type=F32)


def window_kernel(blocks, info, qkv, halo, before, out):
    rows, width, size, stride = 128, D1 // 8, D1 // H1, SENT
    key_count = WIN + rows
    i = lax.broadcasted_iota(jnp.int32, (key_count, rows), 1)
    j = lax.broadcasted_iota(jnp.int32, (key_count, rows), 0)
    band = (j > i) & (j <= i + WIN)
    seq_position = info[8]
    if before is not None:
        out[...] = before[...]
    for n in blocks:
        place = info[n]
        keys, values = [], []
        for k in range(n - 4, n + 1):
            if k >= 0:
                start = pl.multiple_of(info[k] * stride, 16)
                block = qkv[pl.ds(start, rows), :]
                keys.append(block[:, :width])
                values.append(block[:, width : 2 * width])
            else:
                block = halo[(k + 4) * rows : (k + 5) * rows, :]
                keys.append(block[:, :width])
                values.append(block[:, width:])
        keys = jnp.concatenate(keys, axis=0)
        values = jnp.concatenate(values, axis=0)
        queries = qkv[pl.ds(pl.multiple_of(place * stride, 16), rows), 2 * width :]
        allowed = band
        if n < 4:
            allowed = band & (j + ((n - 4) * rows + seq_position * 1024) >= 0)
        values = values.T
        parts = []
        for h in range(width // size):
            cut = slice(h * size, (h + 1) * size)
            scores = dot_t(keys[:, cut], queries[:, cut]) * size ** (-0.5)
            scores = jnp.where(allowed, scores, MASKED)
            largest = jnp.max(scores, axis=0, keepdims=True)
            weights = jnp.exp(scores - largest)
            total = jnp.sum(weights, axis=0, keepdims=True)
            parts.append(dot(values[cut, :], weights.astype(BF16)) / total)
        out[pl.ds(pl.multiple_of(place * rows, 16), rows), :] = jnp.concatenate(
            parts, axis=0
        ).T.astype(BF16)


def window_attend(info, qkv, halo=None, before=None):
    if halo is None:
        def kernel(info, qkv, out):
            window_kernel(range(4, 8), info, qkv, None, None, out)

        operands = (info, qkv)
    else:
        def kernel(info, qkv, halo, before, out):
            window_kernel(range(4), info, qkv, halo, before, out)

        operands = (info, qkv, halo, before)
    vmem = pl.BlockSpec(memory_space=pltpu.VMEM)
    return pl.pallas_call(
        kernel,
        out_shape=jax.ShapeDtypeStruct((1024, D1 // 8), BF16),
        in_specs=[pl.BlockSpec(memory_space=pltpu.SMEM)] + [vmem] * (len(operands) - 1),
        out_specs=vmem,
        compiler_params=pltpu.CompilerParams(vmem_limit_bytes=32 * 2**20),
        cost_estimate=pl.CostEstimate(
            flops=12 * 128 * 640 * 256, bytes_accessed=2 * 2**20, transcendentals=12 * 128 * 640
        ),
        name="window_late" if halo is None else "window_early",
    )(*operands)


def prepare_kernel(tokens, out):
    floats = tokens[...].astype(F32)
    scale = lax.rsqrt(jnp.mean(floats * floats, axis=-1, keepdims=True) + 1e-06)
    out[...] = (floats * scale).astype(BF16)


def prepare(tokens):
    return pl.pallas_call(
        prepare_kernel,
        out_shape=jax.ShapeDtypeStruct(tokens.shape, BF16),
        in_specs=[pl.BlockSpec(memory_space=pltpu.VMEM)],
        out_specs=pl.BlockSpec(memory_space=pltpu.VMEM),
        name="prepare",
    )(tokens)


def near_kernel(rows, weights, out):
    out[:, :384] = dot_t(rows[...], weights[192:, :]).astype(BF16)
    out[:, 384:] = dot_t(rows[...], weights[:192, :]).astype(BF16)


def far_kernel(info, near, opposite, diagonal, weights, out, edge):
    half = 4 * SENT
    out[:half, :] = near[...]
    cuts = ((slice(half, half + 2 * SENT), opposite), (slice(half + 2 * SENT, 2 * half), diagonal))
    for cut, rows in cuts:
        out[cut, :384] = dot_t(rows[...], weights[192:, :]).astype(BF16)
    for k in range(4):
        start = pl.multiple_of(info[4 + k] * SENT, 16)
        edge[k * 128 : (k + 1) * 128, :] = out[pl.ds(start, 128), :384]
    for cut, rows in cuts:
        out[cut, 384:] = dot_t(rows[...], weights[:192, :]).astype(BF16)


def project_one(weights, near, info=None, opposite=None, diagonal=None):
    vmem = pl.BlockSpec(memory_space=pltpu.VMEM)
    cost = pl.CostEstimate(flops=2 * 576 * 576 * D1, bytes_accessed=5 * 2**20, transcendentals=0)
    params = pltpu.CompilerParams(vmem_limit_bytes=24 * 2**20)
    if info is None:
        return pl.pallas_call(
            near_kernel,
            out_shape=jax.ShapeDtypeStruct((4 * SENT, 576), BF16),
            in_specs=[vmem] * 2,
            out_specs=vmem,
            compiler_params=params,
            cost_estimate=cost,
            name="project_near",
        )(near, weights)
    return pl.pallas_call(
        far_kernel,
        out_shape=(
            jax.ShapeDtypeStruct((8 * SENT, 576), BF16), jax.ShapeDtypeStruct((WIN, 384), BF16)
        ),
        in_specs=[pl.BlockSpec(memory_space=pltpu.SMEM)] + [vmem] * 4,
        out_specs=(vmem, vmem),
        compiler_params=params,
        cost_estimate=cost,
        name="project_far",
    )(info, near, opposite, diagonal, weights)


def pieces_kernel(near, opposite, diagonal, _, out, marks):
    blocks = [(part, k * 208) for part, n in ((near, 4), (opposite, 2), (diagonal, 2)) for k in range(n)]
    rows = []
    for k, (part, start) in enumerate(blocks):
        out[k * 192 : (k + 1) * 192, :] = part[start : start + 192, :]
        rows.append(part[start + 192 : start + 208, :128].astype(F32)[:1])
    marks[...] = jnp.concatenate(rows, axis=0)


def collect_pieces(near, opposite, diagonal, before):
    vmem = pl.BlockSpec(memory_space=pltpu.VMEM)
    return pl.pallas_call(
        pieces_kernel,
        out_shape=(
            jax.ShapeDtypeStruct((1536, 512), BF16), jax.ShapeDtypeStruct((8, 128), F32)
        ),
        in_specs=[vmem] * 3 + [pl.BlockSpec(memory_space=pl.ANY)],
        out_specs=(vmem, vmem),
        compiler_params=pltpu.CompilerParams(vmem_limit_bytes=16 * 2**20),
        name="collect_pieces",
    )(near, opposite, diagonal, before)


def mlp_kernel(gate, up, down, *refs):
    out, first = refs[-1], 0
    for rows in refs[:-1]:
        def some(step, _, rows=rows, first=first):
            start = pl.multiple_of(step * 256, 256)
            block = rows[pl.ds(start, 256), :]
            gated = dot(block, gate[...])
            hidden = gated / (1.0 + jnp.exp(-gated)) * dot(block, up[...])
            out[pl.ds(first + start, 256), :] = dot(hidden.astype(BF16), down[...]).astype(BF16)
            return 0

        lax.fori_loop(0, rows.shape[0] // 256, some, 0)
        first += rows.shape[0]


def mlp(gate, up, down, *rows):
    return pl.pallas_call(
        mlp_kernel,
        out_shape=jax.ShapeDtypeStruct((512, D1), BF16),
        in_specs=[pl.BlockSpec(memory_space=pltpu.VMEM)] * (3 + len(rows)),
        out_specs=pl.BlockSpec(memory_space=pltpu.VMEM),
        compiler_params=pltpu.CompilerParams(vmem_limit_bytes=32 * 2**20),
        cost_estimate=pl.CostEstimate(
            flops=2 * 512 * 1536 * 1536, bytes_accessed=8 * 2**20, transcendentals=512 * 512
        ),
        name="mlp",
    )(gate, up, down, *rows)


def project_kernel(
    info, near, opposite, diagonal, pieces, weights, valid, chunks, wide_own, pooled, total, squares
):
    step = pl.program_id(0)
    y = info[8]

    @pl.when(step == 0)
    def _():
        pooled[:256, :] = near[...]
        pooled[256:384, :] = opposite[...]
        pooled[384:, :] = diagonal[...]
        total[...] = jnp.zeros_like(total)
        squares[...] = jnp.zeros_like(squares)

    wide = dot(pooled[...], pieces[...].reshape(D1, 512)).astype(BF16)
    floats = wide.astype(F32)
    squares[...] += jnp.broadcast_to(
        jnp.sum(floats * floats, axis=-1, keepdims=True), squares.shape
    )
    for i in range(3):
        total[:, i * 512 : (i + 1) * 512] += dot(wide, weights[i])

    @pl.when(step == 0)
    def _():
        for p in range(8):
            start = pl.multiple_of(info[p] * 64, 64)
            wide_own[pl.ds(start, 64), :] = wide[p * 64 : (p + 1) * 64]

    @pl.when(step == 7)
    def _():
        scale = lax.rsqrt(squares[...] / D2 + 1e-06)
        for k in range(4):
            head = (y + k) & 3
            for i in range(3):
                cut = slice(i * 128, (i + 1) * 128)
                lanes = pl.ds(pl.multiple_of(i * 512 + head * 128, 128), 128)
                part = total[:, lanes] * (scale * SCORE_FACTOR if i == 0 else scale)
                part = part.astype(BF16)
                for p in range(8):
                    start = pl.multiple_of(info[p] * 64, 64)
                    chunks[k, pl.ds(start, 64), cut] = part[p * 64 : (p + 1) * 64]
                chunks[k, 512:, cut] = valid[...]


def project_two(info, pooled, pieces, weights, valid):
    return pl.pallas_call(
        project_kernel,
        out_shape=(
            jax.ShapeDtypeStruct((4, 512 + EXT, 384), BF16),
            jax.ShapeDtypeStruct((512, 512), BF16),
        ),
        grid_spec=pltpu.PrefetchScalarGridSpec(
            num_scalar_prefetch=1,
            grid=(8,),
            in_specs=[
                *[pl.BlockSpec((k, D1), lambda s, info: (0, 0)) for k in (256, 128, 128)],
                pl.BlockSpec((8, 1, 192, 512), lambda s, info: (0, s, 0, 0)),
                pl.BlockSpec((3, 512, 512), lambda s, info: (0, info[s], 0)),
                pl.BlockSpec((EXT, 128), lambda s, info: (0, 0)),
            ],
            out_specs=(
                pl.BlockSpec((4, 512 + EXT, 384), lambda s, info: (0, 0, 0)),
                pl.BlockSpec((512, 512), lambda s, info: (0, 0)),
            ),
            scratch_shapes=[
                pltpu.VMEM((512, D1), BF16),
                pltpu.VMEM((512, 1536), F32),
                pltpu.VMEM((512, 128), F32),
            ],
        ),
        compiler_params=pltpu.CompilerParams(vmem_limit_bytes=40 * 2**20),
        cost_estimate=pl.CostEstimate(
            flops=4 * 512 * 4096 * 1536, bytes_accessed=28 * 2**20, transcendentals=512
        ),
        name="project_two",
    )(info, *pooled, pieces, weights, valid)


def causal_kernel(own_part, info, queries, kv_pair, start, start_stats, out, out_stats, keys, values, even, odd):
    half, core, y = info[0], info[1], info[2]
    slot = pl.program_id(0)
    own_pair = (y + slot) & 3

    @pl.when(slot == 0)
    def _():
        def prepare(block, _):
            row = lax.broadcasted_iota(jnp.int32, (512, 128), 0).astype(F32)
            lane = lax.broadcasted_iota(jnp.int32, (512, 128), 1)
            for which, kv in enumerate(kv_pair):
                count = jnp.sum(kv[block, 512 : 512 + EXT, :128].astype(F32))
                invalid = (lane == 0) & (row >= count)
                keys[which * 4 + block, :, :128] = kv[block, :512, :128]
                keys[which * 4 + block, :, 128:] = jnp.where(invalid, MASKED, 0.0).astype(BF16)
                values[which * 4 + block] = kv[block, :512, 128:].T
            return 0

        lax.fori_loop(0, 4, prepare, 0)

    lane = lax.broadcasted_iota(jnp.int32, (512, 128), 1)
    query = jnp.concatenate([queries[0], jnp.where(lane == 0, 1.0, 0.0).astype(BF16)], axis=1)

    def block_of(pair, which):
        return (which ^ core) * 4 + ((pair - y) & 3)

    def scores_of(pair, which):
        return lax.dot_general(
            keys[block_of(pair, which)], query, (((1,), (1,)), ((), ())), preferred_element_type=F32
        )

    def absorb(scores, pair, which, carry, edge):
        largest, total, sums = carry
        if edge:
            key = lax.broadcasted_iota(jnp.int32, scores.shape, 0) + which * 512
            own = lax.broadcasted_iota(jnp.int32, scores.shape, 1) + core * 512
            scores = jnp.where(key <= own, scores, MASKED)
        new_largest = jnp.maximum(largest, jnp.max(scores, axis=0, keepdims=True))
        decay = jnp.exp2(largest - new_largest)
        weights = jnp.exp2(scores - new_largest)
        total = total * decay + jnp.sum(weights, axis=0, keepdims=True)
        sums = sums * decay + dot(values[block_of(pair, which)], weights.astype(BF16))
        return new_largest, total, sums

    even[...] = scores_of(0, 0)

    def both(pair, carry, edge=False):
        odd[...] = scores_of(pair, 1)
        carry = absorb(even[...], pair, 0, carry, edge)
        if not edge:
            even[...] = scores_of((pair + 1) & 3, 0)
        return absorb(odd[...], pair, 1, carry, edge)

    if own_part:
        carry = (
            jnp.full((1, 512), MASKED, F32), jnp.zeros((1, 512), F32), jnp.zeros((128, 512), F32)
        )
        carry = lax.fori_loop(0, own_pair, both, carry)
        largest, total, sums = both(own_pair, carry, True)
        out[0] = sums
        out_stats[0] = jnp.concatenate([largest, total, jnp.zeros((6, 512), F32)], axis=0)
    else:
        carry = (start_stats[0, 0:1], start_stats[0, 1:2], start[0])
        _, total, sums = lax.fori_loop(0, half * 4, both, carry)
        out[0] = (sums / total).T.astype(BF16)


def causal_attend(own_part, info, queries, kv_pair, start=None):
    def by_slot(*shape):
        return pl.BlockSpec((1, *shape), lambda s, info: (s, 0, 0))

    sums_shape = jax.ShapeDtypeStruct((4, 128, 512), F32)
    stats_shape = jax.ShapeDtypeStruct((4, 8, 512), F32)
    whole = pl.BlockSpec((4, 512 + EXT, 256), lambda s, info: (0, 0, 0))
    in_specs = [by_slot(512, 128), whole, whole]
    operands = [queries, *kv_pair]
    if own_part:
        def kernel(info, queries, kv, other, out, out_stats, *scratch):
            causal_kernel(True, info, queries, (kv, other), None, None, out, out_stats, *scratch)

        out_shape = (sums_shape, stats_shape)
        out_specs = (by_slot(128, 512), by_slot(8, 512))
        tiles = 18
    else:
        def kernel(info, queries, kv, other, start, start_stats, out, *scratch):
            causal_kernel(False, info, queries, (kv, other), start, start_stats, out, None, *scratch)

        out_shape = jax.ShapeDtypeStruct((4, 512, 128), BF16)
        out_specs = by_slot(512, 128)
        in_specs += [by_slot(128, 512), by_slot(8, 512)]
        operands += list(start)
        tiles = 32
    return pl.pallas_call(
        kernel,
        out_shape=out_shape,
        grid_spec=pltpu.PrefetchScalarGridSpec(
            num_scalar_prefetch=1,
            grid=(4,),
            in_specs=in_specs,
            out_specs=out_specs,
            scratch_shapes=[
                pltpu.VMEM((8, 512, 256), BF16),
                pltpu.VMEM((8, 128, 512), BF16),
                pltpu.VMEM((512, 512), F32),
                pltpu.VMEM((512, 512), F32),
            ],
        ),
        compiler_params=pltpu.CompilerParams(vmem_limit_bytes=40 * 2**20),
        cost_estimate=pl.CostEstimate(
            flops=tiles * 512 * 512 * 512, bytes_accessed=4 * 2**20, transcendentals=tiles * 2**18
        ),
        name="causal_own" if own_part else "causal_first_half",
    )(info, *operands)


def turn_y(value, steps, first=0):
    return lax.ppermute(
        value, "seq", [(i, (i & 9) | ((i + 2 * steps) & 6)) for i in range(first, 16)]
    )


def output_kernel(count, info, own, ahead, opposite, behind, weights, out, mixed):
    @pl.when(pl.program_id(0) == 0)
    def _():
        for k, part in enumerate((own, ahead, opposite, behind)):
            head = (info[count] + k) & 3
            mixed[:, pl.ds(pl.multiple_of(head * 128, 128), 128)] = part[...]

    out[...] = dot(mixed[...], weights[...]).astype(BF16)


def output_columns(blocks, y, parts, weights):
    count = blocks.shape[0]

    def kernel(*refs):
        output_kernel(count, *refs)

    return pl.pallas_call(
        kernel,
        out_shape=jax.ShapeDtypeStruct((count * 512, 512), BF16),
        grid_spec=pltpu.PrefetchScalarGridSpec(
            num_scalar_prefetch=1,
            grid=(count,),
            in_specs=[pl.BlockSpec((512, 128), lambda s, info: (0, 0))] * 4
            + [pl.BlockSpec((512, 512), lambda s, info: (0, info[s]))],
            out_specs=pl.BlockSpec((512, 512), lambda s, info: (s, 0)),
            scratch_shapes=[pltpu.VMEM((512, 512), BF16)],
        ),
        compiler_params=pltpu.CompilerParams(vmem_limit_bytes=24 * 2**20),
        cost_estimate=pl.CostEstimate(
            flops=2 * 512**3 * count, bytes_accessed=count * 2**20, transcendentals=0
        ),
        name="output_columns",
    )(jnp.concatenate([blocks, y[None]]).astype(jnp.int32), *parts, weights)


def flip_seq(value, bit):
    return lax.ppermute(value, "seq", [(i, i ^ bit) for i in range(16)])


def per_device(
    tokens, boundary, heads_in, heads_out, gate_up, down_weight, widen, heads_in_two, heads_out_two
):
    seq_position = lax.axis_index("seq")
    me = lax.axis_index("blk")
    rows = tokens.shape[0]
    capacity = 512
    width = D1 // 8
    block_of = jnp.stack([((me ^ (4 * x)) & 4) | ((me + z) & 3) for x, z in PLACES])
    numbers = jnp.arange(8, dtype=jnp.int32)
    place_of = jnp.sum(
        jnp.where(block_of[None, :] == numbers[:, None], numbers[None, :], 0), axis=1
    )

    heads_in_flat = heads_in.transpose(1, 2, 0).reshape(3 * width, D1)
    core, y, half = seq_position & 1, (seq_position >> 1) & 3, seq_position >> 3
    piece = lax.dynamic_slice(widen, ((seq_position & 7) * 192, 0), (192, 512))

    near, opposite, diagonal = gather_blk(prepare(tokens))
    arrived = near[2 * SENT :]
    gates = later(gate_up, arrived)
    gate_flat, up_flat = lax.optimization_barrier((gates[:, 0, :], gates[:, 1, :]))
    info = later(jnp.concatenate([place_of, seq_position[None]]).astype(jnp.int32), gate_flat)
    qkv_near = project_one(heads_in_flat, near)
    qkv, edge = project_one(heads_in_flat, qkv_near, info, opposite, diagonal)
    halo = lax.ppermute(edge, "seq", [(i, i + 1) for i in range(15)])
    attended = window_attend(info, qkv, halo, window_attend(info, qkv))
    attn_near = dot(attended[: 4 * rows], heads_out).astype(BF16)
    attn_far = dot(attended[4 * rows :], heads_out).astype(BF16)
    opposite, diagonal = reduce_first(attn_far)

    marks_rows = jnp.pad(boundary.astype(BF16)[None, :], ((0, EXT - 1), (0, 512 - rows)))
    pieces = gather_blk(jnp.concatenate([piece, marks_rows], axis=0), qkv)
    pieces, marks = collect_pieces(*pieces, attended)
    pieces = lax.all_gather(
        pieces, "seq", axis=0, axis_index_groups=[[h * 8 + k for k in range(8)] for h in range(2)]
    ).reshape(8, 8, 192, 512)
    mid_stream = (
        tokens.astype(F32) + reduce_second(attn_near, opposite, diagonal)
    ).astype(BF16)

    normed_mid = normalize(mid_stream).astype(BF16)

    parts = gather_blk(normed_mid)
    mlp_near = mlp(gate_flat, up_flat, down_weight, parts[0])
    mlp_far = mlp(gate_flat, up_flat, down_weight, *parts[1:])
    counts = jnp.sum(marks, axis=1)
    before = jnp.sum(
        jnp.where(block_of[None, :] < block_of[:, None], counts[None, :], 0.0), axis=1
    )
    steps = jnp.arange(rows)
    running = dot(marks.astype(BF16), (steps[:, None] <= steps[None, :]).astype(BF16))
    slots = jnp.where(marks > 0.5, before[:, None] + running - 1.0, -1.0).astype(jnp.int32)
    span_count = jnp.sum(counts).astype(jnp.int32)
    targets = (block_of[:, None] * 64 + jnp.arange(64)[None, :]).reshape(capacity, 1)
    selector = (slots.reshape(1, 8 * rows) == targets).astype(BF16)
    placed = (
        dot(selector[:, : 4 * rows], mlp_near)
        + dot(selector[:, 4 * rows :], mlp_far)
        + dot(selector[:, :rows], mid_stream)
    ).astype(BF16)
    pooled_own = reduce_blk(placed[:256], placed[256:]).astype(BF16)
    pooled = gather_blk(pooled_own)

    validity = (jnp.arange(capacity, dtype=jnp.int32) < span_count).astype(F32)
    valid_rows = jnp.pad(
        validity.reshape(4, 128).astype(BF16), ((0, EXT - 4), (0, 0))
    )
    info_one = jnp.concatenate([block_of, y[None]]).astype(jnp.int32)
    chunks, wide_cols = project_two(
        info_one, pooled, pieces, heads_in_two.transpose(1, 0, 2), valid_rows
    )
    opposite, diagonal = reduce_first(later(mlp_far, chunks[0]))
    from_behind = turn_y(chunks[1], 1)
    from_ahead = turn_y(chunks[3], 3)
    from_opposite = turn_y(chunks[2], 2)
    mine = jnp.stack([chunks[0], from_ahead, from_opposite, from_behind])
    queries, own_kv = mine[:, :capacity, :128], mine[:, :, 128:]
    first_kv = lax.ppermute(own_kv, "seq", [(i, i + 8) for i in range(8)])
    info_two = jnp.stack([half, core, y]).astype(jnp.int32)
    running = causal_attend(True, info_two, queries, (own_kv, flip_seq(own_kv, 1)))
    first_kv = first_kv + running[1][0, 2, 0].astype(BF16)
    mixed = causal_attend(False, info_two, queries, (first_kv, flip_seq(first_kv, 1)), running)
    back = [mixed[0], turn_y(mixed[3], 3), turn_y(mixed[2], 2), turn_y(mixed[1], 1)]
    out_opposite = turn_z(output_columns(block_of[4:6], y, back, heads_out_two), 2)
    out_diagonal = flip_x(output_columns(block_of[6:], y, back, heads_out_two))
    level_one = (
        mid_stream.astype(F32)
        + reduce_second(later(mlp_near, mixed[0]), opposite, diagonal)
    ).astype(BF16)
    out_near = output_columns(later(block_of[:4], level_one), y, back, heads_out_two)
    level_two = (
        (wide_cols.astype(F32) + reduce_second(out_near, out_opposite, out_diagonal)) * validity[:, None]
    ).astype(BF16)
    return (level_one, level_two)


def solution(mesh):
    placed = (
        P(("seq", "blk"), None),
        P(("seq", "blk")),
        P(None, None, "blk"),
        P("blk", None),
        P(None, None, "blk"),
        P("blk", None),
        P(None, "blk"),
        P(None, None, "blk"),
        P("blk", None),
    )
    return jax.shard_map(
        per_device,
        mesh=mesh,
        in_specs=placed,
        out_specs=(P(("seq", "blk"), None), P("seq", "blk")),
        check_vma=False,
    )
```

```python
import jax
import jax.numpy as jnp
from jax import lax
from jax.experimental import pallas as pl
from jax.experimental.pallas import tpu as pltpu
from jax.sharding import PartitionSpec as P

D1 = 1536
H1 = 24
D2 = 4096
H2 = 32
WIN = 512
EXT = 16
SENT = 128
BF16 = jnp.bfloat16
F32 = jnp.float32
MASKED = -1e30
SCORE_FACTOR = 128 ** (-0.5) * 1.4426950408889634

PLACES = ((0, 0), (1, 0), (0, 1), (0, 3), (0, 2), (1, 2), (1, 1), (1, 3))


def flip_x(value):
    return lax.ppermute(value, "blk", [(i, i ^ 4) for i in range(8)])


def turn_z(value, steps):
    return lax.ppermute(value, "blk", [(i, (i & 4) | ((i + steps) & 3)) for i in range(8)])


def later(array, value):
    return array + (value[0, 0].astype(F32) * 0.0).astype(array.dtype)


def gather_blk(own, between=None):
    across = flip_x(own)
    behind = turn_z(own, 1)
    ahead = turn_z(own, 3)
    first = jnp.concatenate([own, across], axis=0)
    second = jnp.concatenate([ahead, behind], axis=0)
    if between is not None:
        first, second = later(first, between), later(second, between)
    opposite = turn_z(first, 2)
    diagonal = flip_x(second)
    near = jnp.concatenate([first, second], axis=0)
    return near, opposite, diagonal


def reduce_first(far):
    count = far.shape[0] // 4
    return turn_z(far[: 2 * count], 2), flip_x(far[2 * count :])


def reduce_second(near, opposite, diagonal):
    count = near.shape[0] // 4

    def plus(block, other):
        return near[block * count : (block + 1) * count].astype(F32) + other.astype(F32)

    across = flip_x(plus(1, opposite[count:]).astype(BF16))
    behind = turn_z(plus(2, diagonal[:count]).astype(BF16), 1)
    ahead = turn_z(plus(3, diagonal[count:]).astype(BF16), 3)
    return (
        plus(0, opposite[:count])
        + across.astype(F32)
        + behind.astype(F32)
        + ahead.astype(F32)
    )


def reduce_blk(near, far):
    return reduce_second(near, *reduce_first(far))


def normalize(values):
    floats = values.astype(F32)
    return floats * lax.rsqrt(jnp.mean(floats * floats, axis=-1, keepdims=True) + 1e-06)


def dot(left, right):
    return jnp.dot(left, right, preferred_element_type=F32)


def dot_t(left, right):
    return lax.dot_general(left, right, (((1,), (1,)), ((), ())), preferred_element_type=F32)


def window_kernel(blocks, info, qkv, halo, before, out):
    rows, width, size, stride = 128, D1 // 8, D1 // H1, SENT
    key_count = WIN + rows
    i = lax.broadcasted_iota(jnp.int32, (key_count, rows), 1)
    j = lax.broadcasted_iota(jnp.int32, (key_count, rows), 0)
    band = (j > i) & (j <= i + WIN)
    seq_position = info[8]
    if before is not None:
        out[...] = before[...]
    for n in blocks:
        place = info[n]
        keys, values = [], []
        for k in range(n - 4, n + 1):
            if k >= 0:
                start = pl.multiple_of(info[k] * stride, 16)
                block = qkv[pl.ds(start, rows), :]
                keys.append(block[:, :width])
                values.append(block[:, width : 2 * width])
            else:
                block = halo[(k + 4) * rows : (k + 5) * rows, :]
                keys.append(block[:, :width])
                values.append(block[:, width:])
        keys = jnp.concatenate(keys, axis=0)
        values = jnp.concatenate(values, axis=0)
        queries = qkv[pl.ds(pl.multiple_of(place * stride, 16), rows), 2 * width :]
        allowed = band
        if n < 4:
            allowed = band & (j + ((n - 4) * rows + seq_position * 1024) >= 0)
        values = values.T
        parts = []
        for h in range(width // size):
            cut = slice(h * size, (h + 1) * size)
            scores = dot_t(keys[:, cut], queries[:, cut]) * size ** (-0.5)
            scores = jnp.where(allowed, scores, MASKED)
            largest = jnp.max(scores, axis=0, keepdims=True)
            weights = jnp.exp(scores - largest)
            total = jnp.sum(weights, axis=0, keepdims=True)
            parts.append(dot(values[cut, :], weights.astype(BF16)) / total)
        out[pl.ds(pl.multiple_of(place * rows, 16), rows), :] = jnp.concatenate(
            parts, axis=0
        ).T.astype(BF16)


def window_attend(info, qkv, halo=None, before=None):
    if halo is None:
        def kernel(info, qkv, out):
            window_kernel(range(4, 8), info, qkv, None, None, out)

        operands = (info, qkv)
    else:
        def kernel(info, qkv, halo, before, out):
            window_kernel(range(4), info, qkv, halo, before, out)

        operands = (info, qkv, halo, before)
    vmem = pl.BlockSpec(memory_space=pltpu.VMEM)
    return pl.pallas_call(
        kernel,
        out_shape=jax.ShapeDtypeStruct((1024, D1 // 8), BF16),
        in_specs=[pl.BlockSpec(memory_space=pltpu.SMEM)] + [vmem] * (len(operands) - 1),
        out_specs=vmem,
        compiler_params=pltpu.CompilerParams(vmem_limit_bytes=32 * 2**20),
        cost_estimate=pl.CostEstimate(
            flops=12 * 128 * 640 * 256, bytes_accessed=2 * 2**20, transcendentals=12 * 128 * 640
        ),
        name="window_late" if halo is None else "window_early",
    )(*operands)


def prepare_kernel(tokens, out):
    floats = tokens[...].astype(F32)
    scale = lax.rsqrt(jnp.mean(floats * floats, axis=-1, keepdims=True) + 1e-06)
    out[...] = (floats * scale).astype(BF16)


def prepare(tokens):
    return pl.pallas_call(
        prepare_kernel,
        out_shape=jax.ShapeDtypeStruct(tokens.shape, BF16),
        in_specs=[pl.BlockSpec(memory_space=pltpu.VMEM)],
        out_specs=pl.BlockSpec(memory_space=pltpu.VMEM),
        name="prepare",
    )(tokens)


def near_kernel(rows, weights, out):
    out[:, :384] = dot_t(rows[...], weights[192:, :]).astype(BF16)
    out[:, 384:] = dot_t(rows[...], weights[:192, :]).astype(BF16)


def far_kernel(info, near, opposite, diagonal, weights, out, edge):
    half = 4 * SENT
    out[:half, :] = near[...]
    cuts = ((slice(half, half + 2 * SENT), opposite), (slice(half + 2 * SENT, 2 * half), diagonal))
    for cut, rows in cuts:
        out[cut, :384] = dot_t(rows[...], weights[192:, :]).astype(BF16)
    for k in range(4):
        start = pl.multiple_of(info[4 + k] * SENT, 16)
        edge[k * 128 : (k + 1) * 128, :] = out[pl.ds(start, 128), :384]
    for cut, rows in cuts:
        out[cut, 384:] = dot_t(rows[...], weights[:192, :]).astype(BF16)


def project_one(weights, near, info=None, opposite=None, diagonal=None):
    vmem = pl.BlockSpec(memory_space=pltpu.VMEM)
    cost = pl.CostEstimate(flops=2 * 576 * 576 * D1, bytes_accessed=5 * 2**20, transcendentals=0)
    params = pltpu.CompilerParams(vmem_limit_bytes=24 * 2**20)
    if info is None:
        return pl.pallas_call(
            near_kernel,
            out_shape=jax.ShapeDtypeStruct((4 * SENT, 576), BF16),
            in_specs=[vmem] * 2,
            out_specs=vmem,
            compiler_params=params,
            cost_estimate=cost,
            name="project_near",
        )(near, weights)
    return pl.pallas_call(
        far_kernel,
        out_shape=(
            jax.ShapeDtypeStruct((8 * SENT, 576), BF16), jax.ShapeDtypeStruct((WIN, 384), BF16)
        ),
        in_specs=[pl.BlockSpec(memory_space=pltpu.SMEM)] + [vmem] * 4,
        out_specs=(vmem, vmem),
        compiler_params=params,
        cost_estimate=cost,
        name="project_far",
    )(info, near, opposite, diagonal, weights)


def pieces_kernel(near, opposite, diagonal, _, out, marks):
    blocks = [(part, k * 208) for part, n in ((near, 4), (opposite, 2), (diagonal, 2)) for k in range(n)]
    rows = []
    for k, (part, start) in enumerate(blocks):
        out[k * 192 : (k + 1) * 192, :] = part[start : start + 192, :]
        rows.append(part[start + 192 : start + 208, :128].astype(F32)[:1])
    marks[...] = jnp.concatenate(rows, axis=0)


def collect_pieces(near, opposite, diagonal, before):
    vmem = pl.BlockSpec(memory_space=pltpu.VMEM)
    return pl.pallas_call(
        pieces_kernel,
        out_shape=(
            jax.ShapeDtypeStruct((1536, 512), BF16), jax.ShapeDtypeStruct((8, 128), F32)
        ),
        in_specs=[vmem] * 3 + [pl.BlockSpec(memory_space=pl.ANY)],
        out_specs=(vmem, vmem),
        compiler_params=pltpu.CompilerParams(vmem_limit_bytes=16 * 2**20),
        name="collect_pieces",
    )(near, opposite, diagonal, before)


def mlp_kernel(gate, up, down, *refs):
    out, first = refs[-1], 0
    for rows in refs[:-1]:
        def some(step, _, rows=rows, first=first):
            start = pl.multiple_of(step * 256, 256)
            block = rows[pl.ds(start, 256), :]
            gated = dot(block, gate[...])
            hidden = gated / (1.0 + jnp.exp(-gated)) * dot(block, up[...])
            out[pl.ds(first + start, 256), :] = dot(hidden.astype(BF16), down[...]).astype(BF16)
            return 0

        lax.fori_loop(0, rows.shape[0] // 256, some, 0)
        first += rows.shape[0]


def mlp(gate, up, down, *rows):
    return pl.pallas_call(
        mlp_kernel,
        out_shape=jax.ShapeDtypeStruct((512, D1), BF16),
        in_specs=[pl.BlockSpec(memory_space=pltpu.VMEM)] * (3 + len(rows)),
        out_specs=pl.BlockSpec(memory_space=pltpu.VMEM),
        compiler_params=pltpu.CompilerParams(vmem_limit_bytes=32 * 2**20),
        cost_estimate=pl.CostEstimate(
            flops=2 * 512 * 1536 * 1536, bytes_accessed=8 * 2**20, transcendentals=512 * 512
        ),
        name="mlp",
    )(gate, up, down, *rows)


def project_kernel(
    info, near, opposite, diagonal, pieces, weights, valid, chunks, wide_own, pooled, total, squares
):
    step = pl.program_id(0)
    y = info[8]

    @pl.when(step == 0)
    def _():
        pooled[:256, :] = near[...]
        pooled[256:384, :] = opposite[...]
        pooled[384:, :] = diagonal[...]
        total[...] = jnp.zeros_like(total)
        squares[...] = jnp.zeros_like(squares)

    wide = dot(pooled[...], pieces[...].reshape(D1, 512)).astype(BF16)
    floats = wide.astype(F32)
    squares[...] += jnp.broadcast_to(
        jnp.sum(floats * floats, axis=-1, keepdims=True), squares.shape
    )
    for i in range(3):
        total[:, i * 512 : (i + 1) * 512] += dot(wide, weights[i])

    @pl.when(step == 0)
    def _():
        for p in range(8):
            start = pl.multiple_of(info[p] * 64, 64)
            wide_own[pl.ds(start, 64), :] = wide[p * 64 : (p + 1) * 64]

    @pl.when(step == 7)
    def _():
        scale = lax.rsqrt(squares[...] / D2 + 1e-06)
        for k in range(4):
            head = (y + k) & 3
            for i in range(3):
                cut = slice(i * 128, (i + 1) * 128)
                lanes = pl.ds(pl.multiple_of(i * 512 + head * 128, 128), 128)
                part = total[:, lanes] * (scale * SCORE_FACTOR if i == 0 else scale)
                part = part.astype(BF16)
                for p in range(8):
                    start = pl.multiple_of(info[p] * 64, 64)
                    chunks[k, pl.ds(start, 64), cut] = part[p * 64 : (p + 1) * 64]
                chunks[k, 512:, cut] = valid[...]


def project_two(info, pooled, pieces, weights, valid):
    return pl.pallas_call(
        project_kernel,
        out_shape=(
            jax.ShapeDtypeStruct((4, 512 + EXT, 384), BF16),
            jax.ShapeDtypeStruct((512, 512), BF16),
        ),
        grid_spec=pltpu.PrefetchScalarGridSpec(
            num_scalar_prefetch=1,
            grid=(8,),
            in_specs=[
                *[pl.BlockSpec((k, D1), lambda s, info: (0, 0)) for k in (256, 128, 128)],
                pl.BlockSpec((8, 1, 192, 512), lambda s, info: (0, s, 0, 0)),
                pl.BlockSpec((3, 512, 512), lambda s, info: (0, info[s], 0)),
                pl.BlockSpec((EXT, 128), lambda s, info: (0, 0)),
            ],
            out_specs=(
                pl.BlockSpec((4, 512 + EXT, 384), lambda s, info: (0, 0, 0)),
                pl.BlockSpec((512, 512), lambda s, info: (0, 0)),
            ),
            scratch_shapes=[
                pltpu.VMEM((512, D1), BF16),
                pltpu.VMEM((512, 1536), F32),
                pltpu.VMEM((512, 128), F32),
            ],
        ),
        compiler_params=pltpu.CompilerParams(vmem_limit_bytes=40 * 2**20),
        cost_estimate=pl.CostEstimate(
            flops=4 * 512 * 4096 * 1536, bytes_accessed=28 * 2**20, transcendentals=512
        ),
        name="project_two",
    )(info, *pooled, pieces, weights, valid)


def causal_kernel(mode, info, queries, kv_parts, start, start_stats, out, out_stats, keys, values, even, odd):
    half, core, y = info[0], info[1], info[2]
    slot = pl.program_id(0)
    own_pair = (y + slot) & 3

    @pl.when(slot == 0)
    def _():
        def prepare(block, _):
            row = lax.broadcasted_iota(jnp.int32, (512, 128), 0).astype(F32)
            lane = lax.broadcasted_iota(jnp.int32, (512, 128), 1)
            for which, kv in enumerate(kv_parts):
                count = jnp.sum(kv[block, 512 : 512 + EXT, :128].astype(F32))
                invalid = (lane == 0) & (row >= count)
                keys[which * 4 + block, :, :128] = kv[block, :512, :128]
                keys[which * 4 + block, :, 128:] = jnp.where(invalid, MASKED, 0.0).astype(BF16)
                values[which * 4 + block] = kv[block, :512, 128:].T
            return 0

        lax.fori_loop(0, 4, prepare, 0)

    lane = lax.broadcasted_iota(jnp.int32, (512, 128), 1)
    query = jnp.concatenate([queries[0], jnp.where(lane == 0, 1.0, 0.0).astype(BF16)], axis=1)

    def block_of(pair, which):
        if mode != "own":
            return pair * 2 + which
        return (which ^ core) * 4 + ((pair - y) & 3)

    def scores_of(pair, which):
        return lax.dot_general(
            keys[block_of(pair, which)], query, (((1,), (1,)), ((), ())), preferred_element_type=F32
        )

    def absorb(scores, pair, which, carry, edge):
        largest, total, sums = carry
        if edge:
            key = lax.broadcasted_iota(jnp.int32, scores.shape, 0) + which * 512
            own = lax.broadcasted_iota(jnp.int32, scores.shape, 1) + core * 512
            scores = jnp.where(key <= own, scores, MASKED)
        new_largest = jnp.maximum(largest, jnp.max(scores, axis=0, keepdims=True))
        decay = jnp.exp2(largest - new_largest)
        weights = jnp.exp2(scores - new_largest)
        total = total * decay + jnp.sum(weights, axis=0, keepdims=True)
        sums = sums * decay + dot(values[block_of(pair, which)], weights.astype(BF16))
        return new_largest, total, sums

    even[...] = scores_of(0, 0)

    def both(pair, carry, edge=False):
        odd[...] = scores_of(pair, 1)
        carry = absorb(even[...], pair, 0, carry, edge)
        if not edge:
            even[...] = scores_of((pair + 1) & (3 if mode == "own" else 1), 0)
        return absorb(odd[...], pair, 1, carry, edge)

    if mode == "own":
        carry = (
            jnp.full((1, 512), MASKED, F32), jnp.zeros((1, 512), F32), jnp.zeros((128, 512), F32)
        )
        carry = lax.fori_loop(0, own_pair, both, carry)
        carry = both(own_pair, carry, True)
    else:
        carry = (start_stats[0, 0:1], start_stats[0, 1:2], start[0])
        carry = lax.fori_loop(0, half * 2, both, carry)
    largest, total, sums = carry
    if mode == "last":
        out[0] = (sums / total).T.astype(BF16)
    else:
        out[0] = sums
        out_stats[0] = jnp.concatenate([largest, total, jnp.zeros((6, 512), F32)], axis=0)


def causal_attend(mode, info, queries, kv_parts, start=()):
    def by_slot(*shape):
        return pl.BlockSpec((1, *shape), lambda s, info: (s, 0, 0))

    sums_shape = jax.ShapeDtypeStruct((4, 128, 512), F32)
    stats_shape = jax.ShapeDtypeStruct((4, 8, 512), F32)
    whole = pl.BlockSpec((4, 512 + EXT, 256), lambda s, info: (0, 0, 0))
    in_specs = [by_slot(512, 128)] + [whole] * len(kv_parts)
    out_shape, out_specs = (sums_shape, stats_shape), (by_slot(128, 512), by_slot(8, 512))
    if mode == "own":
        def kernel(info, queries, kv, other, *rest):
            causal_kernel(mode, info, queries, (kv, other), None, None, *rest)
    elif mode == "more":
        def kernel(info, queries, kv, *rest):
            causal_kernel(mode, info, queries, (kv,), *rest)
    else:
        def kernel(info, queries, kv, start, start_stats, out, *scratch):
            causal_kernel(mode, info, queries, (kv,), start, start_stats, out, None, *scratch)

        out_shape, out_specs = jax.ShapeDtypeStruct((4, 512, 128), BF16), by_slot(512, 128)
    if start:
        in_specs += [by_slot(128, 512), by_slot(8, 512)]
    operands = [queries, *kv_parts, *start]
    tiles = 18 if mode == "own" else 16
    return pl.pallas_call(
        kernel,
        out_shape=out_shape,
        grid_spec=pltpu.PrefetchScalarGridSpec(
            num_scalar_prefetch=1,
            grid=(4,),
            in_specs=in_specs,
            out_specs=out_specs,
            scratch_shapes=[
                pltpu.VMEM((8, 512, 256), BF16),
                pltpu.VMEM((8, 128, 512), BF16),
                pltpu.VMEM((512, 512), F32),
                pltpu.VMEM((512, 512), F32),
            ],
        ),
        compiler_params=pltpu.CompilerParams(vmem_limit_bytes=40 * 2**20),
        cost_estimate=pl.CostEstimate(
            flops=tiles * 512 * 512 * 512, bytes_accessed=4 * 2**20, transcendentals=tiles * 2**18
        ),
        name="causal_" + mode,
    )(info, *operands)


def turn_y(value, steps, first=0):
    return lax.ppermute(
        value, "seq", [(i, (i & 9) | ((i + 2 * steps) & 6)) for i in range(first, 16)]
    )


def output_kernel(count, info, own, ahead, opposite, behind, weights, out, mixed):
    @pl.when(pl.program_id(0) == 0)
    def _():
        for k, part in enumerate((own, ahead, opposite, behind)):
            head = (info[count] + k) & 3
            mixed[:, pl.ds(pl.multiple_of(head * 128, 128), 128)] = part[...]

    out[...] = dot(mixed[...], weights[...]).astype(BF16)


def output_columns(blocks, y, parts, weights):
    count = blocks.shape[0]

    def kernel(*refs):
        output_kernel(count, *refs)

    return pl.pallas_call(
        kernel,
        out_shape=jax.ShapeDtypeStruct((count * 512, 512), BF16),
        grid_spec=pltpu.PrefetchScalarGridSpec(
            num_scalar_prefetch=1,
            grid=(count,),
            in_specs=[pl.BlockSpec((512, 128), lambda s, info: (0, 0))] * 4
            + [pl.BlockSpec((512, 512), lambda s, info: (0, info[s]))],
            out_specs=pl.BlockSpec((512, 512), lambda s, info: (s, 0)),
            scratch_shapes=[pltpu.VMEM((512, 512), BF16)],
        ),
        compiler_params=pltpu.CompilerParams(vmem_limit_bytes=24 * 2**20),
        cost_estimate=pl.CostEstimate(
            flops=2 * 512**3 * count, bytes_accessed=count * 2**20, transcendentals=0
        ),
        name="output_columns",
    )(jnp.concatenate([blocks, y[None]]).astype(jnp.int32), *parts, weights)


def flip_seq(value, bit):
    return lax.ppermute(value, "seq", [(i, i ^ bit) for i in range(16)])


def per_device(
    tokens, boundary, heads_in, heads_out, gate_up, down_weight, widen, heads_in_two, heads_out_two
):
    seq_position = lax.axis_index("seq")
    me = lax.axis_index("blk")
    rows = tokens.shape[0]
    capacity = 512
    width = D1 // 8
    block_of = jnp.stack([((me ^ (4 * x)) & 4) | ((me + z) & 3) for x, z in PLACES])
    numbers = jnp.arange(8, dtype=jnp.int32)
    place_of = jnp.sum(
        jnp.where(block_of[None, :] == numbers[:, None], numbers[None, :], 0), axis=1
    )

    heads_in_flat = heads_in.transpose(1, 2, 0).reshape(3 * width, D1)
    core, y, half = seq_position & 1, (seq_position >> 1) & 3, seq_position >> 3
    piece = lax.dynamic_slice(widen, ((seq_position & 7) * 192, 0), (192, 512))

    near, opposite, diagonal = gather_blk(prepare(tokens))
    arrived = near[2 * SENT :]
    gates = later(gate_up, arrived)
    gate_flat, up_flat = lax.optimization_barrier((gates[:, 0, :], gates[:, 1, :]))
    info = later(jnp.concatenate([place_of, seq_position[None]]).astype(jnp.int32), gate_flat)
    qkv_near = project_one(heads_in_flat, near)
    qkv, edge = project_one(heads_in_flat, qkv_near, info, opposite, diagonal)
    halo = lax.ppermute(edge, "seq", [(i, i + 1) for i in range(15)])
    attended = window_attend(info, qkv, halo, window_attend(info, qkv))
    attn_near = dot(attended[: 4 * rows], heads_out).astype(BF16)
    attn_far = dot(attended[4 * rows :], heads_out).astype(BF16)
    opposite, diagonal = reduce_first(attn_far)

    marks_rows = jnp.pad(boundary.astype(BF16)[None, :], ((0, EXT - 1), (0, 512 - rows)))
    pieces = gather_blk(jnp.concatenate([piece, marks_rows], axis=0), qkv)
    pieces, marks = collect_pieces(*pieces, attended)
    pieces = lax.all_gather(
        pieces, "seq", axis=0, axis_index_groups=[[h * 8 + k for k in range(8)] for h in range(2)]
    ).reshape(8, 8, 192, 512)
    mid_stream = (
        tokens.astype(F32) + reduce_second(attn_near, opposite, diagonal)
    ).astype(BF16)

    normed_mid = normalize(mid_stream).astype(BF16)

    parts = gather_blk(normed_mid)
    mlp_near = mlp(gate_flat, up_flat, down_weight, parts[0])
    mlp_far = mlp(gate_flat, up_flat, down_weight, *parts[1:])
    counts = jnp.sum(marks, axis=1)
    before = jnp.sum(
        jnp.where(block_of[None, :] < block_of[:, None], counts[None, :], 0.0), axis=1
    )
    steps = jnp.arange(rows)
    running = dot(marks.astype(BF16), (steps[:, None] <= steps[None, :]).astype(BF16))
    slots = jnp.where(marks > 0.5, before[:, None] + running - 1.0, -1.0).astype(jnp.int32)
    span_count = jnp.sum(counts).astype(jnp.int32)
    targets = (block_of[:, None] * 64 + jnp.arange(64)[None, :]).reshape(capacity, 1)
    selector = (slots.reshape(1, 8 * rows) == targets).astype(BF16)
    placed = (
        dot(selector[:, : 4 * rows], mlp_near)
        + dot(selector[:, 4 * rows :], mlp_far)
        + dot(selector[:, :rows], mid_stream)
    ).astype(BF16)
    pooled_own = reduce_blk(placed[:256], placed[256:]).astype(BF16)
    pooled = gather_blk(pooled_own)

    validity = (jnp.arange(capacity, dtype=jnp.int32) < span_count).astype(F32)
    valid_rows = jnp.pad(
        validity.reshape(4, 128).astype(BF16), ((0, EXT - 4), (0, 0))
    )
    info_one = jnp.concatenate([block_of, y[None]]).astype(jnp.int32)
    chunks, wide_cols = project_two(
        info_one, pooled, pieces, heads_in_two.transpose(1, 0, 2), valid_rows
    )
    opposite, diagonal = reduce_first(later(mlp_far, chunks[0]))
    from_behind = turn_y(chunks[1], 1)
    from_ahead = turn_y(chunks[3], 3)
    from_opposite = turn_y(chunks[2], 2)
    mine = jnp.stack([chunks[0], from_ahead, from_opposite, from_behind])
    queries, own_kv = mine[:, :capacity, :128], mine[:, :, 128:]
    first_kv = lax.ppermute(own_kv, "seq", [(i, i + 8) for i in range(8)])
    info_two = jnp.stack([half, core, y]).astype(jnp.int32)
    running = causal_attend("own", info_two, queries, (own_kv, flip_seq(own_kv, 1)))
    unread = jnp.broadcast_to(running[1][0:1, 2:3, :128], (1, EXT, 128)).astype(BF16)
    first_kv = lax.dynamic_update_slice(first_kv, unread, (0, capacity, 128))
    first_other = flip_seq(first_kv, 1)
    running = causal_attend("more", info_two, queries, (first_kv,), running)
    mixed = causal_attend("last", info_two, queries, (first_other,), running)
    back = [mixed[0], turn_y(mixed[3], 3), turn_y(mixed[2], 2), turn_y(mixed[1], 1)]
    out_opposite = turn_z(output_columns(block_of[4:6], y, back, heads_out_two), 2)
    out_diagonal = flip_x(output_columns(block_of[6:], y, back, heads_out_two))
    level_one = (
        mid_stream.astype(F32)
        + reduce_second(later(mlp_near, mixed[0]), opposite, diagonal)
    ).astype(BF16)
    out_near = output_columns(later(block_of[:4], level_one), y, back, heads_out_two)
    level_two = (
        (wide_cols.astype(F32) + reduce_second(out_near, out_opposite, out_diagonal)) * validity[:, None]
    ).astype(BF16)
    return (level_one, level_two)


def solution(mesh):
    placed = (
        P(("seq", "blk"), None),
        P(("seq", "blk")),
        P(None, None, "blk"),
        P("blk", None),
        P(None, None, "blk"),
        P("blk", None),
        P(None, "blk"),
        P(None, None, "blk"),
        P("blk", None),
    )
    return jax.shard_map(
        per_device,
        mesh=mesh,
        in_specs=placed,
        out_specs=(P(("seq", "blk"), None), P("seq", "blk")),
        check_vma=False,
    )
```

```python
import jax
import jax.numpy as jnp
from jax import lax
from jax.experimental import pallas as pl
from jax.experimental.pallas import tpu as pltpu
from jax.sharding import PartitionSpec as P

D1 = 1536
H1 = 24
D2 = 4096
H2 = 32
WIN = 512
EXT = 16
SENT = 128
BF16 = jnp.bfloat16
F32 = jnp.float32
MASKED = -1e30
SCORE_FACTOR = 128 ** (-0.5) * 1.4426950408889634

PLACES = ((0, 0), (1, 0), (0, 1), (0, 3), (0, 2), (1, 2), (1, 1), (1, 3))


def flip_x(value):
    return lax.ppermute(value, "blk", [(i, i ^ 4) for i in range(8)])


def turn_z(value, steps):
    return lax.ppermute(value, "blk", [(i, (i & 4) | ((i + steps) & 3)) for i in range(8)])


def later(array, value):
    return array + (value[0, 0].astype(F32) * 0.0).astype(array.dtype)


def gather_blk(own, between=None):
    across = flip_x(own)
    behind = turn_z(own, 1)
    ahead = turn_z(own, 3)
    first = jnp.concatenate([own, across], axis=0)
    second = jnp.concatenate([ahead, behind], axis=0)
    if between is not None:
        first, second = later(first, between), later(second, between)
    opposite = turn_z(first, 2)
    diagonal = flip_x(second)
    near = jnp.concatenate([first, second], axis=0)
    return near, opposite, diagonal


def reduce_first(far):
    count = far.shape[0] // 4
    return turn_z(far[: 2 * count], 2), flip_x(far[2 * count :])


def reduce_second(near, opposite, diagonal):
    count = near.shape[0] // 4

    def plus(block, other):
        return near[block * count : (block + 1) * count].astype(F32) + other.astype(F32)

    across = flip_x(plus(1, opposite[count:]).astype(BF16))
    behind = turn_z(plus(2, diagonal[:count]).astype(BF16), 1)
    ahead = turn_z(plus(3, diagonal[count:]).astype(BF16), 3)
    return (
        plus(0, opposite[:count])
        + across.astype(F32)
        + behind.astype(F32)
        + ahead.astype(F32)
    )


def reduce_blk(near, far):
    return reduce_second(near, *reduce_first(far))


def normalize(values):
    floats = values.astype(F32)
    return floats * lax.rsqrt(jnp.mean(floats * floats, axis=-1, keepdims=True) + 1e-06)


def dot(left, right):
    return jnp.dot(left, right, preferred_element_type=F32)


def dot_t(left, right):
    return lax.dot_general(left, right, (((1,), (1,)), ((), ())), preferred_element_type=F32)


def window_kernel(blocks, info, qkv, halo, before, out):
    rows, width, size, stride = 128, D1 // 8, D1 // H1, SENT
    key_count = WIN + rows
    i = lax.broadcasted_iota(jnp.int32, (key_count, rows), 1)
    j = lax.broadcasted_iota(jnp.int32, (key_count, rows), 0)
    band = (j > i) & (j <= i + WIN)
    seq_position = info[8]
    if before is not None:
        out[...] = before[...]
    for n in blocks:
        place = info[n]
        keys, values = [], []
        for k in range(n - 4, n + 1):
            if k >= 0:
                start = pl.multiple_of(info[k] * stride, 16)
                block = qkv[pl.ds(start, rows), :]
                keys.append(block[:, :width])
                values.append(block[:, width : 2 * width])
            else:
                block = halo[(k + 4) * rows : (k + 5) * rows, :]
                keys.append(block[:, :width])
                values.append(block[:, width:])
        keys = jnp.concatenate(keys, axis=0)
        values = jnp.concatenate(values, axis=0)
        queries = qkv[pl.ds(pl.multiple_of(place * stride, 16), rows), 2 * width :]
        allowed = band
        if n < 4:
            allowed = band & (j + ((n - 4) * rows + seq_position * 1024) >= 0)
        values = values.T
        parts = []
        for h in range(width // size):
            cut = slice(h * size, (h + 1) * size)
            scores = dot_t(keys[:, cut], queries[:, cut]) * size ** (-0.5)
            scores = jnp.where(allowed, scores, MASKED)
            largest = jnp.max(scores, axis=0, keepdims=True)
            weights = jnp.exp(scores - largest)
            total = jnp.sum(weights, axis=0, keepdims=True)
            parts.append(dot(values[cut, :], weights.astype(BF16)) / total)
        out[pl.ds(pl.multiple_of(place * rows, 16), rows), :] = jnp.concatenate(
            parts, axis=0
        ).T.astype(BF16)


def window_attend(info, qkv, halo=None, before=None):
    if halo is None:
        def kernel(info, qkv, out):
            window_kernel(range(4, 8), info, qkv, None, None, out)

        operands = (info, qkv)
    else:
        def kernel(info, qkv, halo, before, out):
            window_kernel(range(4), info, qkv, halo, before, out)

        operands = (info, qkv, halo, before)
    vmem = pl.BlockSpec(memory_space=pltpu.VMEM)
    return pl.pallas_call(
        kernel,
        out_shape=jax.ShapeDtypeStruct((1024, D1 // 8), BF16),
        in_specs=[pl.BlockSpec(memory_space=pltpu.SMEM)] + [vmem] * (len(operands) - 1),
        out_specs=vmem,
        compiler_params=pltpu.CompilerParams(vmem_limit_bytes=32 * 2**20),
        cost_estimate=pl.CostEstimate(
            flops=12 * 128 * 640 * 256, bytes_accessed=2 * 2**20, transcendentals=12 * 128 * 640
        ),
        name="window_late" if halo is None else "window_early",
    )(*operands)


def prepare_kernel(tokens, out):
    floats = tokens[...].astype(F32)
    scale = lax.rsqrt(jnp.mean(floats * floats, axis=-1, keepdims=True) + 1e-06)
    out[...] = (floats * scale).astype(BF16)


def prepare(tokens):
    return pl.pallas_call(
        prepare_kernel,
        out_shape=jax.ShapeDtypeStruct(tokens.shape, BF16),
        in_specs=[pl.BlockSpec(memory_space=pltpu.VMEM)],
        out_specs=pl.BlockSpec(memory_space=pltpu.VMEM),
        name="prepare",
    )(tokens)


def near_kernel(rows, weights, out):
    out[:, :384] = dot_t(rows[...], weights[192:, :]).astype(BF16)
    out[:, 384:] = dot_t(rows[...], weights[:192, :]).astype(BF16)


def far_kernel(info, near, opposite, diagonal, weights, out, edge):
    half = 4 * SENT
    out[:half, :] = near[...]
    cuts = ((slice(half, half + 2 * SENT), opposite), (slice(half + 2 * SENT, 2 * half), diagonal))
    for cut, rows in cuts:
        out[cut, :384] = dot_t(rows[...], weights[192:, :]).astype(BF16)
    for k in range(4):
        start = pl.multiple_of(info[4 + k] * SENT, 16)
        edge[k * 128 : (k + 1) * 128, :] = out[pl.ds(start, 128), :384]
    for cut, rows in cuts:
        out[cut, 384:] = dot_t(rows[...], weights[:192, :]).astype(BF16)


def project_one(weights, near, info=None, opposite=None, diagonal=None):
    vmem = pl.BlockSpec(memory_space=pltpu.VMEM)
    cost = pl.CostEstimate(flops=2 * 576 * 576 * D1, bytes_accessed=5 * 2**20, transcendentals=0)
    params = pltpu.CompilerParams(vmem_limit_bytes=24 * 2**20)
    if info is None:
        return pl.pallas_call(
            near_kernel,
            out_shape=jax.ShapeDtypeStruct((4 * SENT, 576), BF16),
            in_specs=[vmem] * 2,
            out_specs=vmem,
            compiler_params=params,
            cost_estimate=cost,
            name="project_near",
        )(near, weights)
    return pl.pallas_call(
        far_kernel,
        out_shape=(
            jax.ShapeDtypeStruct((8 * SENT, 576), BF16), jax.ShapeDtypeStruct((WIN, 384), BF16)
        ),
        in_specs=[pl.BlockSpec(memory_space=pltpu.SMEM)] + [vmem] * 4,
        out_specs=(vmem, vmem),
        compiler_params=params,
        cost_estimate=cost,
        name="project_far",
    )(info, near, opposite, diagonal, weights)


def pieces_kernel(near, opposite, diagonal, _, out, marks):
    blocks = [(part, k * 208) for part, n in ((near, 4), (opposite, 2), (diagonal, 2)) for k in range(n)]
    rows = []
    for k, (part, start) in enumerate(blocks):
        out[k * 192 : (k + 1) * 192, :] = part[start : start + 192, :]
        rows.append(part[start + 192 : start + 208, :128].astype(F32)[:1])
    marks[...] = jnp.concatenate(rows, axis=0)


def collect_pieces(near, opposite, diagonal, before):
    vmem = pl.BlockSpec(memory_space=pltpu.VMEM)
    return pl.pallas_call(
        pieces_kernel,
        out_shape=(
            jax.ShapeDtypeStruct((1536, 512), BF16), jax.ShapeDtypeStruct((8, 128), F32)
        ),
        in_specs=[vmem] * 3 + [pl.BlockSpec(memory_space=pl.ANY)],
        out_specs=(vmem, vmem),
        compiler_params=pltpu.CompilerParams(vmem_limit_bytes=16 * 2**20),
        name="collect_pieces",
    )(near, opposite, diagonal, before)


def mlp_kernel(gate, up, down, *refs):
    out, first = refs[-1], 0
    for rows in refs[:-1]:
        def some(step, _, rows=rows, first=first):
            start = pl.multiple_of(step * 256, 256)
            block = rows[pl.ds(start, 256), :]
            gated = dot(block, gate[...])
            hidden = gated / (1.0 + jnp.exp(-gated)) * dot(block, up[...])
            out[pl.ds(first + start, 256), :] = dot(hidden.astype(BF16), down[...]).astype(BF16)
            return 0

        lax.fori_loop(0, rows.shape[0] // 256, some, 0)
        first += rows.shape[0]


def mlp(gate, up, down, *rows):
    return pl.pallas_call(
        mlp_kernel,
        out_shape=jax.ShapeDtypeStruct((512, D1), BF16),
        in_specs=[pl.BlockSpec(memory_space=pltpu.VMEM)] * (3 + len(rows)),
        out_specs=pl.BlockSpec(memory_space=pltpu.VMEM),
        compiler_params=pltpu.CompilerParams(vmem_limit_bytes=32 * 2**20),
        cost_estimate=pl.CostEstimate(
            flops=2 * 512 * 1536 * 1536, bytes_accessed=8 * 2**20, transcendentals=512 * 512
        ),
        name="mlp",
    )(gate, up, down, *rows)


def project_kernel(
    info, near, opposite, diagonal, pieces, weights, valid, chunks, wide_own, pooled, total, squares
):
    step = pl.program_id(0)
    y = info[8]

    @pl.when(step == 0)
    def _():
        pooled[:256, :] = near[...]
        pooled[256:384, :] = opposite[...]
        pooled[384:, :] = diagonal[...]
        total[...] = jnp.zeros_like(total)
        squares[...] = jnp.zeros_like(squares)

    wide = dot(pooled[...], pieces[...].reshape(D1, 512)).astype(BF16)
    floats = wide.astype(F32)
    squares[...] += jnp.broadcast_to(
        jnp.sum(floats * floats, axis=-1, keepdims=True), squares.shape
    )
    for i in range(3):
        total[:, i * 512 : (i + 1) * 512] += dot(wide, weights[i])

    @pl.when(step == 0)
    def _():
        for p in range(8):
            start = pl.multiple_of(info[p] * 64, 64)
            wide_own[pl.ds(start, 64), :] = wide[p * 64 : (p + 1) * 64]

    @pl.when(step == 7)
    def _():
        scale = lax.rsqrt(squares[...] / D2 + 1e-06)
        for k in range(4):
            head = (y + k) & 3
            for i in range(3):
                cut = slice(i * 128, (i + 1) * 128)
                lanes = pl.ds(pl.multiple_of(i * 512 + head * 128, 128), 128)
                part = total[:, lanes] * (scale * SCORE_FACTOR if i == 0 else scale)
                part = part.astype(BF16)
                for p in range(8):
                    start = pl.multiple_of(info[p] * 64, 64)
                    chunks[k, pl.ds(start, 64), cut] = part[p * 64 : (p + 1) * 64]
                chunks[k, 512:, cut] = valid[...]


def project_two(info, pooled, pieces, weights, valid):
    return pl.pallas_call(
        project_kernel,
        out_shape=(
            jax.ShapeDtypeStruct((4, 512 + EXT, 384), BF16),
            jax.ShapeDtypeStruct((512, 512), BF16),
        ),
        grid_spec=pltpu.PrefetchScalarGridSpec(
            num_scalar_prefetch=1,
            grid=(8,),
            in_specs=[
                *[pl.BlockSpec((k, D1), lambda s, info: (0, 0)) for k in (256, 128, 128)],
                pl.BlockSpec((8, 1, 192, 512), lambda s, info: (0, s, 0, 0)),
                pl.BlockSpec((3, 512, 512), lambda s, info: (0, info[s], 0)),
                pl.BlockSpec((EXT, 128), lambda s, info: (0, 0)),
            ],
            out_specs=(
                pl.BlockSpec((4, 512 + EXT, 384), lambda s, info: (0, 0, 0)),
                pl.BlockSpec((512, 512), lambda s, info: (0, 0)),
            ),
            scratch_shapes=[
                pltpu.VMEM((512, D1), BF16),
                pltpu.VMEM((512, 1536), F32),
                pltpu.VMEM((512, 128), F32),
            ],
        ),
        compiler_params=pltpu.CompilerParams(vmem_limit_bytes=40 * 2**20),
        cost_estimate=pl.CostEstimate(
            flops=4 * 512 * 4096 * 1536, bytes_accessed=28 * 2**20, transcendentals=512
        ),
        name="project_two",
    )(info, *pooled, pieces, weights, valid)


def causal_kernel(own_part, info, queries, kv_pair, start, start_stats, out, out_stats, keys, values, even, odd):
    half, core, y = info[0], info[1], info[2]
    slot = pl.program_id(0)
    own_pair = (y + slot) & 3

    @pl.when(slot == 0)
    def _():
        def prepare(block, _):
            row = lax.broadcasted_iota(jnp.int32, (512, 128), 0).astype(F32)
            lane = lax.broadcasted_iota(jnp.int32, (512, 128), 1)
            for which, kv in enumerate(kv_pair):
                count = jnp.sum(kv[block, 512 : 512 + EXT, :128].astype(F32))
                invalid = (lane == 0) & (row >= count)
                keys[which * 4 + block, :, :128] = kv[block, :512, :128]
                keys[which * 4 + block, :, 128:] = jnp.where(invalid, MASKED, 0.0).astype(BF16)
                values[which * 4 + block] = kv[block, :512, 128:].T
            return 0

        lax.fori_loop(0, 4, prepare, 0)

    lane = lax.broadcasted_iota(jnp.int32, (512, 128), 1)
    query = jnp.concatenate([queries[0], jnp.where(lane == 0, 1.0, 0.0).astype(BF16)], axis=1)

    def block_of(pair, which):
        return (which ^ core) * 4 + ((pair - y) & 3)

    def scores_of(pair, which):
        return lax.dot_general(
            keys[block_of(pair, which)], query, (((1,), (1,)), ((), ())), preferred_element_type=F32
        )

    def absorb(scores, pair, which, carry, edge):
        largest, total, sums = carry
        if edge:
            key = lax.broadcasted_iota(jnp.int32, scores.shape, 0) + which * 512
            own = lax.broadcasted_iota(jnp.int32, scores.shape, 1) + core * 512
            scores = jnp.where(key <= own, scores, MASKED)
        new_largest = jnp.maximum(largest, jnp.max(scores, axis=0, keepdims=True))
        decay = jnp.exp2(largest - new_largest)
        weights = jnp.exp2(scores - new_largest)
        total = total * decay + jnp.sum(weights, axis=0, keepdims=True)
        sums = sums * decay + dot(values[block_of(pair, which)], weights.astype(BF16))
        return new_largest, total, sums

    even[...] = scores_of(0, 0)

    def both(pair, carry, edge=False):
        odd[...] = scores_of(pair, 1)
        carry = absorb(even[...], pair, 0, carry, edge)
        if not edge:
            even[...] = scores_of((pair + 1) & 3, 0)
        return absorb(odd[...], pair, 1, carry, edge)

    if own_part:
        carry = (
            jnp.full((1, 512), MASKED, F32), jnp.zeros((1, 512), F32), jnp.zeros((128, 512), F32)
        )
        carry = lax.fori_loop(0, own_pair, both, carry)
        largest, total, sums = both(own_pair, carry, True)
        out[0] = sums
        out_stats[0] = jnp.concatenate([largest, total, jnp.zeros((6, 512), F32)], axis=0)
    else:
        carry = (start_stats[0, 0:1], start_stats[0, 1:2], start[0])
        _, total, sums = lax.fori_loop(0, half * 4, both, carry)
        out[0] = (sums / total).T.astype(BF16)


def causal_attend(own_part, info, queries, kv_pair, start=None):
    def by_slot(*shape):
        return pl.BlockSpec((1, *shape), lambda s, info: (s, 0, 0))

    sums_shape = jax.ShapeDtypeStruct((4, 128, 512), F32)
    stats_shape = jax.ShapeDtypeStruct((4, 8, 512), F32)
    whole = pl.BlockSpec((4, 512 + EXT, 256), lambda s, info: (0, 0, 0))
    in_specs = [by_slot(512, 128), whole, whole]
    operands = [queries, *kv_pair]
    if own_part:
        def kernel(info, queries, kv, other, out, out_stats, *scratch):
            causal_kernel(True, info, queries, (kv, other), None, None, out, out_stats, *scratch)

        out_shape = (sums_shape, stats_shape)
        out_specs = (by_slot(128, 512), by_slot(8, 512))
        tiles = 18
    else:
        def kernel(info, queries, kv, other, start, start_stats, out, *scratch):
            causal_kernel(False, info, queries, (kv, other), start, start_stats, out, None, *scratch)

        out_shape = jax.ShapeDtypeStruct((4, 512, 128), BF16)
        out_specs = by_slot(512, 128)
        in_specs += [by_slot(128, 512), by_slot(8, 512)]
        operands += list(start)
        tiles = 32
    return pl.pallas_call(
        kernel,
        out_shape=out_shape,
        grid_spec=pltpu.PrefetchScalarGridSpec(
            num_scalar_prefetch=1,
            grid=(4,),
            in_specs=in_specs,
            out_specs=out_specs,
            scratch_shapes=[
                pltpu.VMEM((8, 512, 256), BF16),
                pltpu.VMEM((8, 128, 512), BF16),
                pltpu.VMEM((512, 512), F32),
                pltpu.VMEM((512, 512), F32),
            ],
        ),
        compiler_params=pltpu.CompilerParams(vmem_limit_bytes=40 * 2**20),
        cost_estimate=pl.CostEstimate(
            flops=tiles * 512 * 512 * 512, bytes_accessed=4 * 2**20, transcendentals=tiles * 2**18
        ),
        name="causal_own" if own_part else "causal_first_half",
    )(info, *operands)


def turn_y(value, steps, first=0):
    return lax.ppermute(
        value, "seq", [(i, (i & 9) | ((i + 2 * steps) & 6)) for i in range(first, 16)]
    )


def output_kernel(count, info, own, ahead, opposite, behind, weights, out, mixed):
    @pl.when(pl.program_id(0) == 0)
    def _():
        for k, part in enumerate((own, ahead, opposite, behind)):
            head = (info[count] + k) & 3
            mixed[:, pl.ds(pl.multiple_of(head * 128, 128), 128)] = part[...]

    out[...] = dot(mixed[...], weights[...]).astype(BF16)


def output_columns(blocks, y, parts, weights):
    count = blocks.shape[0]

    def kernel(*refs):
        output_kernel(count, *refs)

    return pl.pallas_call(
        kernel,
        out_shape=jax.ShapeDtypeStruct((count * 512, 512), BF16),
        grid_spec=pltpu.PrefetchScalarGridSpec(
            num_scalar_prefetch=1,
            grid=(count,),
            in_specs=[pl.BlockSpec((512, 128), lambda s, info: (0, 0))] * 4
            + [pl.BlockSpec((512, 512), lambda s, info: (0, info[s]))],
            out_specs=pl.BlockSpec((512, 512), lambda s, info: (s, 0)),
            scratch_shapes=[pltpu.VMEM((512, 512), BF16)],
        ),
        compiler_params=pltpu.CompilerParams(vmem_limit_bytes=24 * 2**20),
        cost_estimate=pl.CostEstimate(
            flops=2 * 512**3 * count, bytes_accessed=count * 2**20, transcendentals=0
        ),
        name="output_columns",
    )(jnp.concatenate([blocks, y[None]]).astype(jnp.int32), *parts, weights)


def flip_seq(value, bit):
    return lax.ppermute(value, "seq", [(i, i ^ bit) for i in range(16)])


def per_device(
    tokens, boundary, heads_in, heads_out, gate_up, down_weight, widen, heads_in_two, heads_out_two
):
    seq_position = lax.axis_index("seq")
    me = lax.axis_index("blk")
    rows = tokens.shape[0]
    capacity = 512
    width = D1 // 8
    block_of = jnp.stack([((me ^ (4 * x)) & 4) | ((me + z) & 3) for x, z in PLACES])
    numbers = jnp.arange(8, dtype=jnp.int32)
    place_of = jnp.sum(
        jnp.where(block_of[None, :] == numbers[:, None], numbers[None, :], 0), axis=1
    )

    heads_in_flat = heads_in.transpose(1, 2, 0).reshape(3 * width, D1)
    core, y, half = seq_position & 1, (seq_position >> 1) & 3, seq_position >> 3
    piece = lax.dynamic_slice(widen, ((seq_position & 7) * 192, 0), (192, 512))

    near, opposite, diagonal = gather_blk(prepare(tokens))
    arrived = near[2 * SENT :]
    gates = later(gate_up, arrived)
    gate_flat, up_flat = lax.optimization_barrier((gates[:, 0, :], gates[:, 1, :]))
    info = later(jnp.concatenate([place_of, seq_position[None]]).astype(jnp.int32), gate_flat)
    qkv_near = project_one(heads_in_flat, near)
    qkv, edge = project_one(heads_in_flat, qkv_near, info, opposite, diagonal)
    halo = lax.ppermute(edge, "seq", [(i, i + 1) for i in range(15)])
    attended = window_attend(info, qkv, halo, window_attend(info, qkv))
    attn_near = dot(attended[: 4 * rows], heads_out).astype(BF16)
    attn_far = dot(attended[4 * rows :], heads_out).astype(BF16)
    opposite, diagonal = reduce_first(attn_far)

    marks_rows = jnp.pad(boundary.astype(BF16)[None, :], ((0, EXT - 1), (0, 512 - rows)))
    pieces = gather_blk(jnp.concatenate([piece, marks_rows], axis=0), qkv)
    pieces, marks = collect_pieces(*pieces, attended)
    pieces = lax.all_gather(
        pieces, "seq", axis=0, axis_index_groups=[[h * 8 + k for k in range(8)] for h in range(2)]
    ).reshape(8, 8, 192, 512)
    mid_stream = (
        tokens.astype(F32) + reduce_second(attn_near, opposite, diagonal)
    ).astype(BF16)

    normed_mid = normalize(mid_stream).astype(BF16)

    parts = gather_blk(normed_mid)
    mlp_near = mlp(gate_flat, up_flat, down_weight, parts[0])
    mlp_far = mlp(gate_flat, up_flat, down_weight, *parts[1:])
    counts = jnp.sum(marks, axis=1)
    before = jnp.sum(
        jnp.where(block_of[None, :] < block_of[:, None], counts[None, :], 0.0), axis=1
    )
    steps = jnp.arange(rows)
    running = dot(marks.astype(BF16), (steps[:, None] <= steps[None, :]).astype(BF16))
    slots = jnp.where(marks > 0.5, before[:, None] + running - 1.0, -1.0).astype(jnp.int32)
    span_count = jnp.sum(counts).astype(jnp.int32)
    targets = (block_of[:, None] * 64 + jnp.arange(64)[None, :]).reshape(capacity, 1)
    selector = (slots.reshape(1, 8 * rows) == targets).astype(BF16)
    placed = (
        dot(selector[:, : 4 * rows], mlp_near)
        + dot(selector[:, 4 * rows :], mlp_far)
        + dot(selector[:, :rows], mid_stream)
    ).astype(BF16)
    pooled_own = reduce_blk(placed[:256], placed[256:]).astype(BF16)
    pooled = gather_blk(pooled_own)

    validity = (jnp.arange(capacity, dtype=jnp.int32) < span_count).astype(F32)
    valid_rows = jnp.pad(
        validity.reshape(4, 128).astype(BF16), ((0, EXT - 4), (0, 0))
    )
    info_one = jnp.concatenate([block_of, y[None]]).astype(jnp.int32)
    chunks, wide_cols = project_two(
        info_one, pooled, pieces, heads_in_two.transpose(1, 0, 2), valid_rows
    )
    opposite, diagonal = reduce_first(later(mlp_far, chunks[0]))
    from_behind = turn_y(chunks[1], 1)
    from_ahead = turn_y(chunks[3], 3)
    from_opposite = turn_y(chunks[2], 2)
    mine = jnp.stack([chunks[0], from_ahead, from_opposite, from_behind])
    queries, own_kv = mine[:, :capacity, :128], mine[:, :, 128:]
    first_kv = lax.ppermute(own_kv, "seq", [(i, i + 8) for i in range(8)])
    info_two = jnp.stack([half, core, y]).astype(jnp.int32)
    running = causal_attend(True, info_two, queries, (own_kv, flip_seq(own_kv, 1)))
    unread = jnp.broadcast_to(running[1][0:1, 2:3, :128], (1, EXT, 128)).astype(BF16)
    first_kv = lax.dynamic_update_slice(first_kv, unread, (0, capacity, 128))
    mixed = causal_attend(False, info_two, queries, (first_kv, flip_seq(first_kv, 1)), running)
    back = [mixed[0], turn_y(mixed[3], 3), turn_y(mixed[2], 2), turn_y(mixed[1], 1)]
    out_opposite = turn_z(output_columns(block_of[4:6], y, back, heads_out_two), 2)
    out_diagonal = output_columns(block_of[6:], y, back, heads_out_two)
    after_out = out_diagonal
    out_diagonal = flip_x(out_diagonal)
    level_one = (
        mid_stream.astype(F32)
        + reduce_second(later(mlp_near, after_out), opposite, diagonal)
    ).astype(BF16)
    out_near = output_columns(block_of[:4], y, back, heads_out_two)
    level_two = (
        (wide_cols.astype(F32) + reduce_second(out_near, out_opposite, out_diagonal)) * validity[:, None]
    ).astype(BF16)
    return (level_one, level_two)


def solution(mesh):
    placed = (
        P(("seq", "blk"), None),
        P(("seq", "blk")),
        P(None, None, "blk"),
        P("blk", None),
        P(None, None, "blk"),
        P("blk", None),
        P(None, "blk"),
        P(None, None, "blk"),
        P("blk", None),
    )
    return jax.shard_map(
        per_device,
        mesh=mesh,
        in_specs=placed,
        out_specs=(P(("seq", "blk"), None), P("seq", "blk")),
        check_vma=False,
    )
```

```python
import jax
import jax.numpy as jnp
from jax import lax
from jax.experimental import pallas as pl
from jax.experimental.pallas import tpu as pltpu
from jax.sharding import PartitionSpec as P

D1 = 1536
H1 = 24
D2 = 4096
H2 = 32
WIN = 512
EXT = 16
SENT = 128
BF16 = jnp.bfloat16
F32 = jnp.float32
MASKED = -1e30
SCORE_FACTOR = 128 ** (-0.5) * 1.4426950408889634

PLACES = ((0, 0), (1, 0), (0, 1), (0, 3), (0, 2), (1, 2), (1, 1), (1, 3))


def flip_x(value):
    return lax.ppermute(value, "blk", [(i, i ^ 4) for i in range(8)])


def turn_z(value, steps):
    return lax.ppermute(value, "blk", [(i, (i & 4) | ((i + steps) & 3)) for i in range(8)])


def later(array, value):
    return array + (value[0, 0].astype(F32) * 0.0).astype(array.dtype)


def gather_blk(own, between=None):
    across = flip_x(own)
    behind = turn_z(own, 1)
    ahead = turn_z(own, 3)
    first = jnp.concatenate([own, across], axis=0)
    second = jnp.concatenate([ahead, behind], axis=0)
    if between is not None:
        first, second = later(first, between), later(second, between)
    opposite = turn_z(first, 2)
    diagonal = flip_x(second)
    near = jnp.concatenate([first, second], axis=0)
    return near, opposite, diagonal


def reduce_first(far):
    count = far.shape[0] // 4
    return turn_z(far[: 2 * count], 2), flip_x(far[2 * count :])


def reduce_second(near, opposite, diagonal):
    count = near.shape[0] // 4

    def plus(block, other):
        return near[block * count : (block + 1) * count].astype(F32) + other.astype(F32)

    across = flip_x(plus(1, opposite[count:]).astype(BF16))
    behind = turn_z(plus(2, diagonal[:count]).astype(BF16), 1)
    ahead = turn_z(plus(3, diagonal[count:]).astype(BF16), 3)
    return (
        plus(0, opposite[:count])
        + across.astype(F32)
        + behind.astype(F32)
        + ahead.astype(F32)
    )


def reduce_blk(near, far):
    return reduce_second(near, *reduce_first(far))


def normalize(values):
    floats = values.astype(F32)
    return floats * lax.rsqrt(jnp.mean(floats * floats, axis=-1, keepdims=True) + 1e-06)


def dot(left, right):
    return jnp.dot(left, right, preferred_element_type=F32)


def dot_t(left, right):
    return lax.dot_general(left, right, (((1,), (1,)), ((), ())), preferred_element_type=F32)


def window_kernel(blocks, info, qkv, halo, before, out):
    rows, width, size, stride = 128, D1 // 8, D1 // H1, SENT
    key_count = WIN + rows
    i = lax.broadcasted_iota(jnp.int32, (key_count, rows), 1)
    j = lax.broadcasted_iota(jnp.int32, (key_count, rows), 0)
    band = (j > i) & (j <= i + WIN)
    seq_position = info[8]
    if before is not None:
        out[...] = before[...]
    for n in blocks:
        place = info[n]
        keys, values = [], []
        for k in range(n - 4, n + 1):
            if k >= 0:
                start = pl.multiple_of(info[k] * stride, 16)
                block = qkv[pl.ds(start, rows), :]
                keys.append(block[:, :width])
                values.append(block[:, width : 2 * width])
            else:
                block = halo[(k + 4) * rows : (k + 5) * rows, :]
                keys.append(block[:, :width])
                values.append(block[:, width:])
        keys = jnp.concatenate(keys, axis=0)
        values = jnp.concatenate(values, axis=0)
        queries = qkv[pl.ds(pl.multiple_of(place * stride, 16), rows), 2 * width :]
        allowed = band
        if n < 4:
            allowed = band & (j + ((n - 4) * rows + seq_position * 1024) >= 0)
        values = values.T
        parts = []
        for h in range(width // size):
            cut = slice(h * size, (h + 1) * size)
            scores = dot_t(keys[:, cut], queries[:, cut]) * size ** (-0.5)
            scores = jnp.where(allowed, scores, MASKED)
            largest = jnp.max(scores, axis=0, keepdims=True)
            weights = jnp.exp(scores - largest)
            total = jnp.sum(weights, axis=0, keepdims=True)
            parts.append(dot(values[cut, :], weights.astype(BF16)) / total)
        out[pl.ds(pl.multiple_of(place * rows, 16), rows), :] = jnp.concatenate(
            parts, axis=0
        ).T.astype(BF16)


def window_attend(info, qkv, halo=None, before=None):
    if halo is None:
        def kernel(info, qkv, out):
            window_kernel(range(4, 8), info, qkv, None, None, out)

        operands = (info, qkv)
    else:
        def kernel(info, qkv, halo, before, out):
            window_kernel(range(4), info, qkv, halo, before, out)

        operands = (info, qkv, halo, before)
    vmem = pl.BlockSpec(memory_space=pltpu.VMEM)
    return pl.pallas_call(
        kernel,
        out_shape=jax.ShapeDtypeStruct((1024, D1 // 8), BF16),
        in_specs=[pl.BlockSpec(memory_space=pltpu.SMEM)] + [vmem] * (len(operands) - 1),
        out_specs=vmem,
        compiler_params=pltpu.CompilerParams(vmem_limit_bytes=32 * 2**20),
        cost_estimate=pl.CostEstimate(
            flops=12 * 128 * 640 * 256, bytes_accessed=2 * 2**20, transcendentals=12 * 128 * 640
        ),
        name="window_late" if halo is None else "window_early",
    )(*operands)


def prepare_kernel(tokens, out):
    floats = tokens[...].astype(F32)
    scale = lax.rsqrt(jnp.mean(floats * floats, axis=-1, keepdims=True) + 1e-06)
    out[...] = (floats * scale).astype(BF16)


def prepare(tokens):
    return pl.pallas_call(
        prepare_kernel,
        out_shape=jax.ShapeDtypeStruct(tokens.shape, BF16),
        in_specs=[pl.BlockSpec(memory_space=pltpu.VMEM)],
        out_specs=pl.BlockSpec(memory_space=pltpu.VMEM),
        name="prepare",
    )(tokens)


def near_kernel(rows, weights, out):
    out[:, :384] = dot_t(rows[...], weights[192:, :]).astype(BF16)
    out[:, 384:] = dot_t(rows[...], weights[:192, :]).astype(BF16)


def far_kernel(info, near, opposite, diagonal, weights, out, edge):
    half = 4 * SENT
    out[:half, :] = near[...]
    cuts = ((slice(half, half + 2 * SENT), opposite), (slice(half + 2 * SENT, 2 * half), diagonal))
    for cut, rows in cuts:
        out[cut, :384] = dot_t(rows[...], weights[192:, :]).astype(BF16)
    for k in range(4):
        start = pl.multiple_of(info[4 + k] * SENT, 16)
        edge[k * 128 : (k + 1) * 128, :] = out[pl.ds(start, 128), :384]
    for cut, rows in cuts:
        out[cut, 384:] = dot_t(rows[...], weights[:192, :]).astype(BF16)


def project_one(weights, near, info=None, opposite=None, diagonal=None):
    vmem = pl.BlockSpec(memory_space=pltpu.VMEM)
    cost = pl.CostEstimate(flops=2 * 576 * 576 * D1, bytes_accessed=5 * 2**20, transcendentals=0)
    params = pltpu.CompilerParams(vmem_limit_bytes=24 * 2**20)
    if info is None:
        return pl.pallas_call(
            near_kernel,
            out_shape=jax.ShapeDtypeStruct((4 * SENT, 576), BF16),
            in_specs=[vmem] * 2,
            out_specs=vmem,
            compiler_params=params,
            cost_estimate=cost,
            name="project_near",
        )(near, weights)
    return pl.pallas_call(
        far_kernel,
        out_shape=(
            jax.ShapeDtypeStruct((8 * SENT, 576), BF16), jax.ShapeDtypeStruct((WIN, 384), BF16)
        ),
        in_specs=[pl.BlockSpec(memory_space=pltpu.SMEM)] + [vmem] * 4,
        out_specs=(vmem, vmem),
        compiler_params=params,
        cost_estimate=cost,
        name="project_far",
    )(info, near, opposite, diagonal, weights)


def pieces_kernel(near, opposite, diagonal, _, out, marks):
    blocks = [(part, k * 208) for part, n in ((near, 4), (opposite, 2), (diagonal, 2)) for k in range(n)]
    rows = []
    for k, (part, start) in enumerate(blocks):
        out[k * 192 : (k + 1) * 192, :] = part[start : start + 192, :]
        rows.append(part[start + 192 : start + 208, :128].astype(F32)[:1])
    marks[...] = jnp.concatenate(rows, axis=0)


def collect_pieces(near, opposite, diagonal, before):
    vmem = pl.BlockSpec(memory_space=pltpu.VMEM)
    return pl.pallas_call(
        pieces_kernel,
        out_shape=(
            jax.ShapeDtypeStruct((1536, 512), BF16), jax.ShapeDtypeStruct((8, 128), F32)
        ),
        in_specs=[vmem] * 3 + [pl.BlockSpec(memory_space=pl.ANY)],
        out_specs=(vmem, vmem),
        compiler_params=pltpu.CompilerParams(vmem_limit_bytes=16 * 2**20),
        name="collect_pieces",
    )(near, opposite, diagonal, before)


def mlp_kernel(gate, up, down, *refs):
    out, first = refs[-1], 0
    for rows in refs[:-1]:
        def some(step, _, rows=rows, first=first):
            start = pl.multiple_of(step * 256, 256)
            block = rows[pl.ds(start, 256), :]
            gated = dot(block, gate[...])
            hidden = gated / (1.0 + jnp.exp(-gated)) * dot(block, up[...])
            out[pl.ds(first + start, 256), :] = dot(hidden.astype(BF16), down[...]).astype(BF16)
            return 0

        lax.fori_loop(0, rows.shape[0] // 256, some, 0)
        first += rows.shape[0]


def mlp(gate, up, down, *rows):
    return pl.pallas_call(
        mlp_kernel,
        out_shape=jax.ShapeDtypeStruct((512, D1), BF16),
        in_specs=[pl.BlockSpec(memory_space=pltpu.VMEM)] * (3 + len(rows)),
        out_specs=pl.BlockSpec(memory_space=pltpu.VMEM),
        compiler_params=pltpu.CompilerParams(vmem_limit_bytes=32 * 2**20),
        cost_estimate=pl.CostEstimate(
            flops=2 * 512 * 1536 * 1536, bytes_accessed=8 * 2**20, transcendentals=512 * 512
        ),
        name="mlp",
    )(gate, up, down, *rows)


def project_kernel(
    info, near, opposite, diagonal, pieces, weights, valid, chunks, wide_own, pooled, total, squares
):
    step = pl.program_id(0)
    y = info[8]

    @pl.when(step == 0)
    def _():
        pooled[:256, :] = near[...]
        pooled[256:384, :] = opposite[...]
        pooled[384:, :] = diagonal[...]
        total[...] = jnp.zeros_like(total)
        squares[...] = jnp.zeros_like(squares)

    wide = dot(pooled[...], pieces[...].reshape(D1, 512)).astype(BF16)
    floats = wide.astype(F32)
    squares[...] += jnp.broadcast_to(
        jnp.sum(floats * floats, axis=-1, keepdims=True), squares.shape
    )
    for i in range(3):
        total[:, i * 512 : (i + 1) * 512] += dot(wide, weights[i])

    @pl.when(step == 0)
    def _():
        for p in range(8):
            start = pl.multiple_of(info[p] * 64, 64)
            wide_own[pl.ds(start, 64), :] = wide[p * 64 : (p + 1) * 64]

    @pl.when(step == 7)
    def _():
        scale = lax.rsqrt(squares[...] / D2 + 1e-06)
        for k in range(4):
            head = (y + k) & 3
            for i in range(3):
                cut = slice(i * 128, (i + 1) * 128)
                lanes = pl.ds(pl.multiple_of(i * 512 + head * 128, 128), 128)
                part = total[:, lanes] * (scale * SCORE_FACTOR if i == 0 else scale)
                part = part.astype(BF16)
                for p in range(8):
                    start = pl.multiple_of(info[p] * 64, 64)
                    chunks[k, pl.ds(start, 64), cut] = part[p * 64 : (p + 1) * 64]
                chunks[k, 512:, cut] = valid[...]


def project_two(info, pooled, pieces, weights, valid):
    return pl.pallas_call(
        project_kernel,
        out_shape=(
            jax.ShapeDtypeStruct((4, 512 + EXT, 384), BF16),
            jax.ShapeDtypeStruct((512, 512), BF16),
        ),
        grid_spec=pltpu.PrefetchScalarGridSpec(
            num_scalar_prefetch=1,
            grid=(8,),
            in_specs=[
                *[pl.BlockSpec((k, D1), lambda s, info: (0, 0)) for k in (256, 128, 128)],
                pl.BlockSpec((8, 1, 192, 512), lambda s, info: (0, s, 0, 0)),
                pl.BlockSpec((3, 512, 512), lambda s, info: (0, info[s], 0)),
                pl.BlockSpec((EXT, 128), lambda s, info: (0, 0)),
            ],
            out_specs=(
                pl.BlockSpec((4, 512 + EXT, 384), lambda s, info: (0, 0, 0)),
                pl.BlockSpec((512, 512), lambda s, info: (0, 0)),
            ),
            scratch_shapes=[
                pltpu.VMEM((512, D1), BF16),
                pltpu.VMEM((512, 1536), F32),
                pltpu.VMEM((512, 128), F32),
            ],
        ),
        compiler_params=pltpu.CompilerParams(vmem_limit_bytes=40 * 2**20),
        cost_estimate=pl.CostEstimate(
            flops=4 * 512 * 4096 * 1536, bytes_accessed=28 * 2**20, transcendentals=512
        ),
        name="project_two",
    )(info, *pooled, pieces, weights, valid)


def causal_kernel(own_part, info, queries, kv_pair, start, start_stats, out, out_stats, keys, values, even, odd):
    half, core, y = info[0], info[1], info[2]
    slot = pl.program_id(0)
    own_pair = (y + slot) & 3

    @pl.when(slot == 0)
    def _():
        def prepare(block, _):
            row = lax.broadcasted_iota(jnp.int32, (512, 128), 0).astype(F32)
            lane = lax.broadcasted_iota(jnp.int32, (512, 128), 1)
            for which, kv in enumerate(kv_pair):
                count = jnp.sum(kv[block, 512 : 512 + EXT, :128].astype(F32))
                invalid = (lane == 0) & (row >= count)
                keys[which * 4 + block, :, :128] = kv[block, :512, :128]
                keys[which * 4 + block, :, 128:] = jnp.where(invalid, MASKED, 0.0).astype(BF16)
                values[which * 4 + block] = kv[block, :512, 128:].T
            return 0

        lax.fori_loop(0, 4, prepare, 0)

    lane = lax.broadcasted_iota(jnp.int32, (512, 128), 1)
    query = jnp.concatenate([queries[0], jnp.where(lane == 0, 1.0, 0.0).astype(BF16)], axis=1)

    def block_of(pair, which):
        return (which ^ core) * 4 + ((pair - y) & 3)

    def scores_of(pair, which):
        return lax.dot_general(
            keys[block_of(pair, which)], query, (((1,), (1,)), ((), ())), preferred_element_type=F32
        )

    def absorb(scores, pair, which, carry, edge):
        largest, total, sums = carry
        if edge:
            key = lax.broadcasted_iota(jnp.int32, scores.shape, 0) + which * 512
            own = lax.broadcasted_iota(jnp.int32, scores.shape, 1) + core * 512
            scores = jnp.where(key <= own, scores, MASKED)
        new_largest = jnp.maximum(largest, jnp.max(scores, axis=0, keepdims=True))
        decay = jnp.exp2(largest - new_largest)
        weights = jnp.exp2(scores - new_largest)
        total = total * decay + jnp.sum(weights, axis=0, keepdims=True)
        sums = sums * decay + dot(values[block_of(pair, which)], weights.astype(BF16))
        return new_largest, total, sums

    even[...] = scores_of(0, 0)

    def both(pair, carry, edge=False):
        odd[...] = scores_of(pair, 1)
        carry = absorb(even[...], pair, 0, carry, edge)
        if not edge:
            even[...] = scores_of((pair + 1) & 3, 0)
        return absorb(odd[...], pair, 1, carry, edge)

    if own_part:
        carry = (
            jnp.full((1, 512), MASKED, F32), jnp.zeros((1, 512), F32), jnp.zeros((128, 512), F32)
        )
        carry = lax.fori_loop(0, own_pair, both, carry)
        largest, total, sums = both(own_pair, carry, True)
        out[0] = sums
        out_stats[0] = jnp.concatenate([largest, total, jnp.zeros((6, 512), F32)], axis=0)
    else:
        carry = (start_stats[0, 0:1], start_stats[0, 1:2], start[0])
        _, total, sums = lax.fori_loop(0, half * 4, both, carry)
        out[0] = (sums / total).T.astype(BF16)


def causal_attend(own_part, info, queries, kv_pair, start=None):
    def by_slot(*shape):
        return pl.BlockSpec((1, *shape), lambda s, info: (s, 0, 0))

    sums_shape = jax.ShapeDtypeStruct((4, 128, 512), F32)
    stats_shape = jax.ShapeDtypeStruct((4, 8, 512), F32)
    whole = pl.BlockSpec((4, 512 + EXT, 256), lambda s, info: (0, 0, 0))
    in_specs = [by_slot(512, 128), whole, whole]
    operands = [queries, *kv_pair]
    if own_part:
        def kernel(info, queries, kv, other, out, out_stats, *scratch):
            causal_kernel(True, info, queries, (kv, other), None, None, out, out_stats, *scratch)

        out_shape = (sums_shape, stats_shape)
        out_specs = (by_slot(128, 512), by_slot(8, 512))
        tiles = 18
    else:
        def kernel(info, queries, kv, other, start, start_stats, out, *scratch):
            causal_kernel(False, info, queries, (kv, other), start, start_stats, out, None, *scratch)

        out_shape = jax.ShapeDtypeStruct((4, 512, 128), BF16)
        out_specs = by_slot(512, 128)
        in_specs += [by_slot(128, 512), by_slot(8, 512)]
        operands += list(start)
        tiles = 32
    return pl.pallas_call(
        kernel,
        out_shape=out_shape,
        grid_spec=pltpu.PrefetchScalarGridSpec(
            num_scalar_prefetch=1,
            grid=(4,),
            in_specs=in_specs,
            out_specs=out_specs,
            scratch_shapes=[
                pltpu.VMEM((8, 512, 256), BF16),
                pltpu.VMEM((8, 128, 512), BF16),
                pltpu.VMEM((512, 512), F32),
                pltpu.VMEM((512, 512), F32),
            ],
        ),
        compiler_params=pltpu.CompilerParams(vmem_limit_bytes=40 * 2**20),
        cost_estimate=pl.CostEstimate(
            flops=tiles * 512 * 512 * 512, bytes_accessed=4 * 2**20, transcendentals=tiles * 2**18
        ),
        name="causal_own" if own_part else "causal_first_half",
    )(info, *operands)


def turn_y(value, steps, first=0):
    return lax.ppermute(
        value, "seq", [(i, (i & 9) | ((i + 2 * steps) & 6)) for i in range(first, 16)]
    )


def output_kernel(count, info, own, ahead, opposite, behind, weights, out, mixed):
    @pl.when(pl.program_id(0) == 0)
    def _():
        for k, part in enumerate((own, ahead, opposite, behind)):
            head = (info[count] + k) & 3
            mixed[:, pl.ds(pl.multiple_of(head * 128, 128), 128)] = part[...]

    out[...] = dot(mixed[...], weights[...]).astype(BF16)


def output_columns(blocks, y, parts, weights):
    count = blocks.shape[0]

    def kernel(*refs):
        output_kernel(count, *refs)

    return pl.pallas_call(
        kernel,
        out_shape=jax.ShapeDtypeStruct((count * 512, 512), BF16),
        grid_spec=pltpu.PrefetchScalarGridSpec(
            num_scalar_prefetch=1,
            grid=(count,),
            in_specs=[pl.BlockSpec((512, 128), lambda s, info: (0, 0))] * 4
            + [pl.BlockSpec((512, 512), lambda s, info: (0, info[s]))],
            out_specs=pl.BlockSpec((512, 512), lambda s, info: (s, 0)),
            scratch_shapes=[pltpu.VMEM((512, 512), BF16)],
        ),
        compiler_params=pltpu.CompilerParams(vmem_limit_bytes=24 * 2**20),
        cost_estimate=pl.CostEstimate(
            flops=2 * 512**3 * count, bytes_accessed=count * 2**20, transcendentals=0
        ),
        name="output_columns",
    )(jnp.concatenate([blocks, y[None]]).astype(jnp.int32), *parts, weights)


def flip_seq(value, bit):
    return lax.ppermute(value, "seq", [(i, i ^ bit) for i in range(16)])


def per_device(
    tokens, boundary, heads_in, heads_out, gate_up, down_weight, widen, heads_in_two, heads_out_two
):
    seq_position = lax.axis_index("seq")
    me = lax.axis_index("blk")
    rows = tokens.shape[0]
    capacity = 512
    width = D1 // 8
    block_of = jnp.stack([((me ^ (4 * x)) & 4) | ((me + z) & 3) for x, z in PLACES])
    numbers = jnp.arange(8, dtype=jnp.int32)
    place_of = jnp.sum(
        jnp.where(block_of[None, :] == numbers[:, None], numbers[None, :], 0), axis=1
    )

    heads_in_flat = heads_in.transpose(1, 2, 0).reshape(3 * width, D1)
    core, y, half = seq_position & 1, (seq_position >> 1) & 3, seq_position >> 3
    piece = lax.dynamic_slice(widen, ((seq_position & 7) * 192, 0), (192, 512))

    near, opposite, diagonal = gather_blk(prepare(tokens))
    arrived = near[2 * SENT :]
    gates = later(gate_up, arrived)
    gate_flat, up_flat = lax.optimization_barrier((gates[:, 0, :], gates[:, 1, :]))
    info = later(jnp.concatenate([place_of, seq_position[None]]).astype(jnp.int32), gate_flat)
    qkv_near = project_one(heads_in_flat, near)
    qkv, edge = project_one(heads_in_flat, qkv_near, info, opposite, diagonal)
    halo = lax.ppermute(edge, "seq", [(i, i + 1) for i in range(15)])
    attended = window_attend(info, qkv, halo, window_attend(info, qkv))
    attn_near = dot(attended[: 4 * rows], heads_out).astype(BF16)
    attn_far = dot(attended[4 * rows :], heads_out).astype(BF16)
    opposite, diagonal = reduce_first(attn_far)

    marks_rows = jnp.pad(boundary.astype(BF16)[None, :], ((0, EXT - 1), (0, 512 - rows)))
    pieces = gather_blk(jnp.concatenate([piece, marks_rows], axis=0), qkv)
    pieces, marks = collect_pieces(*pieces, attended)
    pieces = lax.all_gather(
        pieces, "seq", axis=0, axis_index_groups=[[h * 8 + k for k in range(8)] for h in range(2)]
    ).reshape(8, 8, 192, 512)
    mid_stream = (
        tokens.astype(F32) + reduce_second(attn_near, opposite, diagonal)
    ).astype(BF16)

    normed_mid = normalize(mid_stream).astype(BF16)

    parts = gather_blk(normed_mid)
    mlp_near = mlp(gate_flat, up_flat, down_weight, parts[0])
    mlp_far = mlp(gate_flat, up_flat, down_weight, *parts[1:])
    counts = jnp.sum(marks, axis=1)
    before = jnp.sum(
        jnp.where(block_of[None, :] < block_of[:, None], counts[None, :], 0.0), axis=1
    )
    steps = jnp.arange(rows)
    running = dot(marks.astype(BF16), (steps[:, None] <= steps[None, :]).astype(BF16))
    slots = jnp.where(marks > 0.5, before[:, None] + running - 1.0, -1.0).astype(jnp.int32)
    span_count = jnp.sum(counts).astype(jnp.int32)
    targets = (block_of[:, None] * 64 + jnp.arange(64)[None, :]).reshape(capacity, 1)
    selector = (slots.reshape(1, 8 * rows) == targets).astype(BF16)
    placed = (
        dot(selector[:, : 4 * rows], mlp_near)
        + dot(selector[:, 4 * rows :], mlp_far)
        + dot(selector[:, :rows], mid_stream)
    ).astype(BF16)
    pooled_own = reduce_blk(placed[:256], placed[256:]).astype(BF16)
    pooled = gather_blk(pooled_own)

    validity = (jnp.arange(capacity, dtype=jnp.int32) < span_count).astype(F32)
    valid_rows = jnp.pad(
        validity.reshape(4, 128).astype(BF16), ((0, EXT - 4), (0, 0))
    )
    info_one = jnp.concatenate([block_of, y[None]]).astype(jnp.int32)
    chunks, wide_cols = project_two(
        info_one, pooled, pieces, heads_in_two.transpose(1, 0, 2), valid_rows
    )
    opposite, diagonal = reduce_first(later(mlp_far, chunks[0]))
    from_behind = turn_y(chunks[1], 1)
    from_ahead = turn_y(chunks[3], 3)
    from_opposite = turn_y(chunks[2], 2)
    mine = jnp.stack([chunks[0], from_ahead, from_opposite, from_behind])
    queries, own_kv = mine[:, :capacity, :128], mine[:, :, 128:]
    first_kv = lax.ppermute(own_kv, "seq", [(i, i + 8) for i in range(8)])
    info_two = jnp.stack([half, core, y]).astype(jnp.int32)
    running = causal_attend(True, info_two, queries, (own_kv, flip_seq(own_kv, 1)))
    unread = jnp.broadcast_to(running[1][0:1, 2:3, :128], (1, EXT, 128)).astype(BF16)
    first_kv = lax.dynamic_update_slice(first_kv, unread, (0, capacity, 128))
    mixed = causal_attend(False, info_two, queries, (first_kv, flip_seq(first_kv, 1)), running)
    back = [mixed[0], turn_y(mixed[3], 3), turn_y(mixed[2], 2), turn_y(mixed[1], 1)]
    out_opposite = turn_z(output_columns(block_of[4:6], y, back, heads_out_two), 2)
    out_diagonal = flip_x(output_columns(block_of[6:], y, back, heads_out_two))
    level_one = (
        mid_stream.astype(F32)
        + reduce_second(later(mlp_near, mixed[0]), opposite, diagonal)
    ).astype(BF16)
    out_near = output_columns(later(block_of[:4], level_one), y, back, heads_out_two)
    level_two = (
        (wide_cols.astype(F32) + reduce_second(out_near, out_opposite, out_diagonal)) * validity[:, None]
    ).astype(BF16)
    return (level_one, level_two)


def solution(mesh):
    placed = (
        P(("seq", "blk"), None),
        P(("seq", "blk")),
        P(None, None, "blk"),
        P("blk", None),
        P(None, None, "blk"),
        P("blk", None),
        P(None, "blk"),
        P(None, None, "blk"),
        P("blk", None),
    )
    return jax.shard_map(
        per_device,
        mesh=mesh,
        in_specs=placed,
        out_specs=(P(("seq", "blk"), None), P("seq", "blk")),
        check_vma=False,
    )
```
